256 devices in a mesh: dp: 16 (over z, x_hi), shard: 16 (over x_lo, y, core).
Axes of the slice: x: 4 (x_hi: 2, x_lo: 2; x = x_hi * 2 + x_lo), y: 4, z: 8, core: 2. Of those that a mesh axis runs over, the one named last changes fastest.
Arguments:
- frames: bfloat16 [4096, 40, 1536], P(('dp', 'shard')), may hold values from -6 to 6
- slot_dest: int32 [4096], P(('dp', 'shard')), may hold values from 0 to 15, as said below
- recv_length: int32 [4096], P(('dp', 'shard')), may hold values from 8 to 40, as said below
- recv_offset: int32 [4096], P(('dp', 'shard')), may hold values from 0 to 383, as said below
- gain1: float32 [1536], replicated, may hold values from 0.5 to 1.5
- w_in: bfloat16 [1536, 3072], P('shard'), may hold values from -0.15625 to 0.15625
- w_depth: float32 [31, 1536], replicated, may hold values from -1 to 1
- gain2: float32 [1536], replicated, may hold values from 0.5 to 1.5
- cotangent: bfloat16 [98304, 1536], P(('dp', 'shard')), may hold values from -6 to 6
Outputs:
- output: bfloat16 [98304, 1536], P(('dp', 'shard'))
- grad_input: bfloat16 [98304, 1536], P(('dp', 'shard'))
- grad_w_in: float32 [1536, 3072], P('shard')
- grad_depth: float32 [31, 1536], replicated
- grad_gain1: float32 [1536], replicated
- grad_gain2: float32 [1536], replicated
The draws below stay inside these ranges and needn't reach their ends.
Inputs may be any that keep to these rules, and one draw needn't show every extreme that they name: Within each device's block, slot_dest is a permutation of the dp indices: every device holds one utterance for each device of its dp group. recv_length entry s of device (p, g) is the length of the utterance that device (s, g) holds for p; the lengths in each device's block sum to 384, and each block has one of exactly 40. In each device's block the intervals [recv_offset, recv_offset + recv_length) tile the rows 0 to 383 without gaps or intersections.
All inputs are finite; a program needn't handle non-finite values.
Results may differ from the reference program's by a relative error of at most 0.012.
Values may be sent and summed in bfloat16 or wider, within the bound.
A program may use at most 128 MiB of HBM per device.

```python
import jax
import jax.numpy as jnp
from jax import lax

D = 1536
K = 31
FR_DEV = 384
LMAX = 40
UTTS = 4096
TOKENS = 98304
N_DP = 16
N_SHARD = 16


def plan_tables(key):
    key = jax.random.fold_in(key, 11)
    base = FR_DEV // N_DP
    extra = LMAX - base
    half = N_DP // 2
    key_swing, key_order, key_route = jax.random.split(key, 3)
    swings = jax.random.randint(key_swing, (N_SHARD, N_DP, half), 0, extra + 1)
    swings = swings.at[:, :, 0].set(extra)
    lengths = jnp.concatenate([base + swings, base - swings], axis=2).astype(jnp.int32)
    lengths = jax.random.permutation(key_order, lengths, axis=2, independent=True)
    starts = (jnp.cumsum(lengths, axis=2) - lengths).astype(jnp.int32)
    ranks = jnp.broadcast_to(jnp.arange(N_DP, dtype=jnp.int32), (N_SHARD, N_DP, N_DP))
    routes = jax.random.permutation(key_route, ranks, axis=2, independent=True)
    dest_ids = jnp.arange(N_DP, dtype=jnp.int32)[:, None]
    source_ids = jnp.arange(N_DP, dtype=jnp.int32)[None, :]
    picks = jnp.broadcast_to(((dest_ids - source_ids) % N_DP)[None], (N_SHARD, N_DP, N_DP))
    recv_len = jnp.take_along_axis(lengths, picks, axis=2)
    recv_start = jnp.take_along_axis(starts, picks, axis=2)
    return (recv_len, recv_start, routes)


def draw_slot_dest(key, part):
    recv_len, recv_start, routes = plan_tables(key)
    return jnp.transpose(routes, (1, 0, 2)).reshape(-1).astype(jnp.int32)


def draw_recv_length(key, part):
    recv_len, recv_start, routes = plan_tables(key)
    return jnp.transpose(recv_len, (1, 0, 2)).reshape(-1).astype(jnp.int32)


def draw_recv_offset(key, part):
    recv_len, recv_start, routes = plan_tables(key)
    return jnp.transpose(recv_start, (1, 0, 2)).reshape(-1).astype(jnp.int32)


def block_scale(rng, shape, pieces, low, largest):
    def one(position, shards_of):
        heights = jax.random.uniform(jax.random.fold_in(jax.random.fold_in(rng, 6), position), (shards_of,), jnp.float32, low / len(pieces), largest / len(pieces))
        return jnp.repeat(jnp.exp(heights), shape[position] // shards_of).reshape((-1,) + (1,) * (len(shape) - position - 1))

    gain = one(*pieces[0])
    for cut in pieces[1:]:
        gain = gain * one(*cut)
    return gain


def normal_values(rng, dims, spread, most, shards=(), kind=jnp.bfloat16):
    array = jax.random.normal(rng, dims, jnp.float32) * spread
    if len(shards) > 0:
        array = block_scale(rng, dims, shards, -0.22, 0.18) * array
    return jnp.clip(array, min=-most, max=most).astype(kind)


def setup_inputs(seed: int = 0) -> dict:
    keys = jax.random.split(jax.random.key(seed), 10)
    return {
        "frames": normal_values(keys[0], (UTTS, LMAX, D), 1.0, 6.0, ((0, 256),)),
        "slot_dest": draw_slot_dest(jax.random.fold_in(keys[9], 71), 0),
        "recv_length": draw_recv_length(jax.random.fold_in(keys[9], 71), 0),
        "recv_offset": draw_recv_offset(jax.random.fold_in(keys[9], 71), 0),
        "gain1": jnp.clip(1.0 + 0.1 * jax.random.normal(keys[4], (D,), jnp.float32), 0.5, 1.5),
        "w_in": normal_values(keys[5], (D, 2 * D), D ** -0.5, 0.15625, ((0, 16),)),
        "w_depth": normal_values(keys[6], (K, D), K ** -0.5, 1.0, (), jnp.float32),
        "gain2": jnp.clip(1.0 + 0.1 * jax.random.normal(keys[7], (D,), jnp.float32), 0.5, 1.5),
        "cotangent": normal_values(keys[8], (TOKENS, D), 1.0, 6.0, ((0, 256),)),
    }


EPSILON = 1e-05

def gather_frames(pool, bases, lengths, offsets, frame_count, slot_len):
    rows_here = jnp.arange(frame_count, dtype=jnp.int32)[:, None]
    member = ((rows_here >= offsets[None, :]) & (rows_here < (offsets + lengths)[None, :])).astype(jnp.int32)
    sources = jnp.arange(lengths.shape[0], dtype=jnp.int32)[None, :]
    owner = lax.optimization_barrier(jnp.sum(member * sources, axis=1)).astype(jnp.int32)
    within = lax.optimization_barrier(jnp.sum(member * (rows_here - offsets[None, :]), axis=1)).astype(jnp.int32)
    base_row = lax.optimization_barrier(jnp.sum(member * bases[None, :], axis=1)).astype(jnp.int32)
    picked = jnp.take(pool, (base_row * slot_len + within).astype(jnp.int32), axis=0)
    return (picked, owner)

def normalize(values):
    center = values - lax.optimization_barrier(jnp.mean(values, axis=1, keepdims=True))
    inverse = lax.rsqrt(lax.optimization_barrier(jnp.mean(center * center, axis=1, keepdims=True)) + EPSILON)
    return (center * inverse, inverse)

def normalize_back(grad_unit, unit, inverse):
    first = lax.optimization_barrier(jnp.mean(grad_unit, axis=1, keepdims=True))
    second = lax.optimization_barrier(jnp.mean(grad_unit * unit, axis=1, keepdims=True))
    return inverse * (grad_unit - first - unit * second)

def depth_forward(values, segment, kernel):
    count = values.shape[0]
    reach = (kernel.shape[0] - 1) // 2
    padded = jnp.pad(values, ((reach, reach), (0, 0)))
    labels = jnp.pad(segment, (reach, reach), constant_values=-1)
    total = jnp.zeros_like(values)
    for tap_index in range(kernel.shape[0]):
        same = (labels[tap_index:tap_index + count] == segment)[:, None]
        total = total + jnp.where(same, padded[tap_index:tap_index + count], 0.0) * kernel[tap_index]
    return total

def depth_backward(grads, segment, kernel):
    count = grads.shape[0]
    reach = (kernel.shape[0] - 1) // 2
    padded = jnp.pad(grads, ((reach, reach), (0, 0)))
    labels = jnp.pad(segment, (reach, reach), constant_values=-1)
    total = jnp.zeros_like(grads)
    for tap_index in range(kernel.shape[0]):
        begin = 2 * reach - tap_index
        same = (labels[begin:begin + count] == segment)[:, None]
        total = total + jnp.where(same, padded[begin:begin + count], 0.0) * kernel[tap_index]
    return total

def depth_weight_grad(grads, values, segment, taps_count):
    count = values.shape[0]
    reach = (taps_count - 1) // 2
    padded = jnp.pad(values, ((reach, reach), (0, 0)))
    labels = jnp.pad(segment, (reach, reach), constant_values=-1)
    collected = []
    for tap_index in range(taps_count):
        same = (labels[tap_index:tap_index + count] == segment)[:, None]
        collected.append(lax.optimization_barrier(jnp.sum(jnp.where(same, padded[tap_index:tap_index + count], 0.0) * grads, axis=0)))
    return jnp.stack(collected, axis=0)

def block_math(inputs, segment, full_weight, gain1, w_depth, gain2, cot_block):
    model_width = inputs.shape[1]
    unit_in, inverse_in = normalize(inputs.astype(jnp.float32))
    normed = (unit_in * gain1).astype(jnp.bfloat16)
    projected = jnp.dot(normed, full_weight, preferred_element_type=jnp.float32)
    linear = projected[:, :model_width]
    gating = projected[:, model_width:]
    gate_sig = jax.nn.sigmoid(gating)
    gated = (linear * gate_sig).astype(jnp.bfloat16)
    gated_wide = gated.astype(jnp.float32)
    convolved = depth_forward(gated_wide, segment, w_depth)
    unit_out, inverse_out = normalize(convolved)
    scaled = unit_out * gain2
    sig_out = jax.nn.sigmoid(scaled)
    output = (scaled * sig_out).astype(jnp.bfloat16)
    grad_scaled = cot_block.astype(jnp.float32) * sig_out * (1.0 + scaled * (1.0 - sig_out))
    gain2_part = lax.optimization_barrier(jnp.sum(grad_scaled * unit_out, axis=0))
    grad_conv = normalize_back(grad_scaled * gain2, unit_out, inverse_out)
    depth_part = depth_weight_grad(grad_conv, gated_wide, segment, w_depth.shape[0])
    grad_gated = depth_backward(grad_conv, segment, w_depth)
    grad_pre = jnp.concatenate([grad_gated * gate_sig, grad_gated * linear * gate_sig * (1.0 - gate_sig)], axis=1).astype(jnp.bfloat16)
    grad_normed = lax.dot_general(grad_pre, full_weight, (((1,), (1,)), ((), ())), preferred_element_type=jnp.float32)
    gain1_part = lax.optimization_barrier(jnp.sum(grad_normed * unit_in, axis=0))
    grad_input = normalize_back(grad_normed * gain1, unit_in, inverse_in).astype(jnp.bfloat16)
    weight_part = lax.dot_general(normed, grad_pre, (((0,), (0,)), ((), ())), preferred_element_type=jnp.float32)
    return (output, grad_input, weight_part, gain1_part, gain2_part, depth_part)

def reference(frames, slot_dest, recv_length, recv_offset, gain1, w_in, w_depth, gain2, cotangent):
    devices = N_DP * N_SHARD
    slot_len = frames.shape[1]
    model_width = frames.shape[2]
    pool = frames.reshape(-1, model_width)
    routes = slot_dest.reshape(N_DP, N_SHARD, N_DP)
    length_table = recv_length.reshape(devices, N_DP)
    offset_table = recv_offset.reshape(devices, N_DP)
    cot_blocks = cotangent.reshape(devices, FR_DEV, model_width)
    sources = jnp.arange(N_DP, dtype=jnp.int32)

    def visit(carry, block):
        dest = block // N_SHARD
        group = block % N_SHARD
        table = lax.dynamic_index_in_dim(routes, group, axis=1, keepdims=False)
        chosen = (table == dest).astype(jnp.int32)
        slot_index = lax.optimization_barrier(jnp.sum(chosen * sources[None, :], axis=1)).astype(jnp.int32)
        bases = ((sources * N_SHARD + group) * N_DP + slot_index).astype(jnp.int32)
        lengths = lax.dynamic_index_in_dim(length_table, block, 0, False)
        offsets = lax.dynamic_index_in_dim(offset_table, block, 0, False)
        inputs, segment = gather_frames(pool, bases, lengths, offsets, FR_DEV, slot_len)
        cot_block = lax.dynamic_index_in_dim(cot_blocks, block, 0, False)
        output, grad_input, weight_part, gain1_part, gain2_part, depth_part = block_math(inputs, segment, w_in, gain1, w_depth, gain2, cot_block)
        acc_weight, acc_gain1, acc_gain2, acc_depth = carry
        updated = (acc_weight + weight_part, acc_gain1 + gain1_part, acc_gain2 + gain2_part, acc_depth + depth_part)
        return (updated, (output, grad_input))
    start_carry = (jnp.zeros((model_width, 2 * model_width), jnp.float32), jnp.zeros((model_width,), jnp.float32), jnp.zeros((model_width,), jnp.float32), jnp.zeros((w_depth.shape[0], model_width), jnp.float32))
    blocks = jnp.arange(devices, dtype=jnp.int32)
    totals, (outputs, grads) = lax.scan(visit, start_carry, blocks)
    return (outputs.reshape(-1, model_width), grads.reshape(-1, model_width), totals[0] / devices, totals[3] / devices, totals[1] / devices, totals[2] / devices)
```

```python
import jax
import jax.numpy as jnp
from jax import lax
from jax.experimental import pallas as pl
from jax.experimental.pallas import tpu as pltpu
from jax.sharding import PartitionSpec as P

EPSILON = 1e-05
MESH = pl.DeviceIdType.MESH
BF = jnp.bfloat16
F32 = jnp.float32

N_DP = 16
N_SHARD = 16
SMALL_ROWS = 40
SMALL_OWNERS = 12
CHUNKS = 3
CHUNK = 1024
HALF = CHUNK // 2


def shard_index(x_lo, y, core):
    return x_lo * 8 + y * 2 + core


def signal(sem, device):
    pl.semaphore_signal(sem, inc=1, device_id=device, device_id_type=MESH)


def remote(src, dst, send, recv, device):
    return pltpu.make_async_remote_copy(
        src_ref=src, dst_ref=dst, send_sem=send, recv_sem=recv, device_id=device, device_id_type=MESH
    )


def exchange_kernel(
    frames, slot_dest, w, pool, full, outgoing, own_sems, a2a_send, a2a_recv, w_send, w_recv
):
    p, g = lax.axis_index("dp"), lax.axis_index("shard")
    x_lo, y, core = g // 8, (g // 2) % 4, g % 2
    up, down, across = (y + 1) % 4, (y + 3) % 4, (y + 2) % 4
    g_x = shard_index(1 - x_lo, y, core)
    g_up = shard_index(x_lo, up, core)
    g_down = shard_index(x_lo, down, core)
    g_core = shard_index(x_lo, y, 1 - core)

    barrier = pltpu.get_barrier_semaphore()

    def greet(i, carry):
        signal(barrier, ((p + i) % N_DP, g))
        return carry

    lax.fori_loop(1, N_DP, greet, 0)
    for peer in (g_x, g_up, g_down, g_core):
        signal(barrier, (p, peer))

    own_w = pltpu.make_async_copy(w, full.at[g], own_sems.at[0])
    own_w.start()
    pl.semaphore_wait(barrier, N_DP - 1 + 4)

    def send(block, peer, slot, src=None):
        return remote(
            full.at[block] if src is None else src, full.at[block], w_send.at[slot], w_recv.at[slot], (p, peer)
        )

    sent = []

    def go(copy):
        copy.start()
        sent.append(copy)

    go(send(g, g_x, 0, w))
    go(send(g, g_up, 1, w))
    go(send(g, g_down, 2, w))
    go(send(g, g_core, 7, w))

    def source_of(d):
        index = jnp.int32(0)
        for j in range(N_DP):
            index = index + jnp.where(slot_dest[j] == d, j, 0)
        return jnp.minimum(index, N_DP - 1)

    def post(i, carry):
        d = (p + i) % N_DP
        outgoing[i] = frames[source_of(d)]
        remote(outgoing.at[i], pool.at[p], a2a_send.at[i - 1], a2a_recv.at[i - 1], (d, g)).start()
        return carry

    lax.fori_loop(1, N_DP, post, 0)
    outgoing[0] = frames[source_of(p)]
    own_frames = pltpu.make_async_copy(outgoing.at[0], pool.at[p], own_sems.at[1])
    own_frames.start()

    def arrived(block, slot):
        remote(full.at[block], full.at[block], w_send.at[slot], w_recv.at[slot], (p, g_x)).wait_recv()

    arrived(g_x, 0)
    go(send(g_x, g_up, 3))
    go(send(g_x, g_down, 4))
    go(send(g_x, g_core, 8))
    b = shard_index(x_lo, down, core)
    arrived(b, 1)
    go(send(b, g_up, 5))
    go(send(b, g_core, 9))
    b = shard_index(x_lo, up, core)
    arrived(b, 2)
    go(send(b, g_core, 10))
    b = shard_index(1 - x_lo, up, core)
    arrived(b, 4)
    go(send(b, g_down, 6))
    go(send(b, g_core, 11))
    b = shard_index(1 - x_lo, down, core)
    arrived(b, 3)
    go(send(b, g_core, 12))
    b = shard_index(x_lo, across, core)
    arrived(b, 5)
    go(send(b, g_core, 13))
    b = shard_index(1 - x_lo, across, core)
    arrived(b, 6)
    go(send(b, g_core, 14))
    other = 1 - core
    theirs = [
        (x_lo, y, 7), (1 - x_lo, y, 8), (x_lo, down, 9), (x_lo, up, 10),
        (1 - x_lo, up, 11), (1 - x_lo, down, 12), (x_lo, across, 13), (1 - x_lo, across, 14),
    ]
    for bx, by, slot in theirs:
        arrived(shard_index(bx, by, other), slot)

    def collect(i, carry):
        s = (p + N_DP - i) % N_DP
        copy = remote(outgoing.at[i], pool.at[s], a2a_send.at[i - 1], a2a_recv.at[i - 1], (s, g))
        copy.wait_recv()
        copy.wait_send()
        return carry

    lax.fori_loop(1, N_DP, collect, 0)
    for copy in sent:
        copy.wait_send()
    own_frames.wait()
    own_w.wait()


def exchange(frames, slot_dest, w):
    slots, slot_len, width = frames.shape
    rows, cols = w.shape
    return pl.pallas_call(
        exchange_kernel,
        out_shape=(
            jax.ShapeDtypeStruct((slots, slot_len, width), BF),
            jax.ShapeDtypeStruct((N_SHARD, rows, cols), BF),
        ),
        in_specs=[
            pl.BlockSpec(memory_space=pltpu.VMEM),
            pl.BlockSpec(memory_space=pltpu.SMEM),
            pl.BlockSpec(memory_space=pl.ANY),
        ],
        out_specs=(pl.BlockSpec(memory_space=pl.ANY), pl.BlockSpec(memory_space=pl.ANY)),
        scratch_shapes=[
            pltpu.VMEM((slots, slot_len, width), BF),
            pltpu.SemaphoreType.DMA((2,)),
            pltpu.SemaphoreType.DMA((N_DP - 1,)),
            pltpu.SemaphoreType.DMA((N_DP - 1,)),
            pltpu.SemaphoreType.DMA((15,)),
            pltpu.SemaphoreType.DMA((15,)),
        ],
        compiler_params=pltpu.CompilerParams(
            collective_id=0, has_side_effects=True, vmem_limit_bytes=32 * 1024 * 1024
        ),
        name="exchange",
    )(frames, slot_dest, w)


def add_blocks(dst, src, count, cols):
    def step(i, carry):
        block, row = i // 2, pl.multiple_of((i % 2) * 48, 48)
        d, s = dst(block), src(block)
        value = d[pl.ds(row, 48), cols].astype(F32) + s[pl.ds(row, 48), :].astype(F32)
        d[pl.ds(row, 48), cols] = value.astype(BF)
        return carry

    lax.fori_loop(0, count * 2, step, 0)


def reduce_kernel(
    part, small, out, small_out,
    own, rx0, rx1, rx2, rx3, rx4, red, fin, rxs, rxd, small_fin,
    load_sems, s0, r0, s1, r1, s2, r2, s3, r3, s4, r4, s5, r5, st1, rt1, st2, rt2, st3, rt3,
):
    p, g = lax.axis_index("dp"), lax.axis_index("shard")
    z, x_hi = p // 2, p % 2
    x_lo, y, core = g // 8, (g // 2) % 4, g % 2
    y_a, y_b = y + 1 - 2 * (y % 2), 3 - y
    mates = (y_a, y_b)
    scale = 1.0 / (N_DP * N_SHARD)

    def load(k):
        return pltpu.make_async_copy(
            part.at[:, :, core, :, pl.ds(CHUNK * k, CHUNK)], own.at[k], load_sems.at[k]
        )

    for k in range(CHUNKS):
        load(k).start()

    barrier = pltpu.get_barrier_semaphore()

    def greet(i, carry):
        signal(barrier, ((p + i) % N_DP, g))
        signal(barrier, (p, (g + i) % N_SHARD))
        return carry

    lax.fori_loop(1, 16, greet, 0)
    pl.semaphore_wait(barrier, 30)

    def copy0(k):
        return remote(
            part.at[:, :, 1 - core, :, pl.ds(CHUNK * k, CHUNK)], rx0.at[k], s0.at[k], r0.at[k],
            (p, shard_index(x_lo, y, 1 - core)),
        )

    for k in range(CHUNKS):
        copy0(k).start()

    def piece(j):
        return pl.ds(pl.multiple_of(j * 128, 128), 128)

    def send_piece(j, carry):
        @pl.when(j != g)
        def _():
            remote(small.at[:, piece(j)], rxs.at[g], st1.at[j], rt1.at[g], (p, j)).start()

        return carry

    lax.fori_loop(0, SMALL_OWNERS, send_piece, 0)

    def cols(h):
        return pl.ds(HALF * h, HALF)

    def copy1(k, h, j):
        q = mates[h]
        after = 3 - q if h == 0 else q + 1 - 2 * (q % 2)
        block = q if j == 0 else after
        return remote(
            own.at[k, :, block, :, cols(h)], rx1.at[k, h, j], s1.at[k, h, j], r1.at[k, h, j],
            (p, shard_index(x_lo, q, core)),
        )

    for k in range(CHUNKS):
        load(k).wait()
        copy0(k).wait_recv()
        add_blocks(
            lambda i: own.at[k, i // 4, i % 4], lambda i: rx0.at[k, i // 4, i % 4], 8, slice(None)
        )
        for h in range(2):
            for j in (1, 0):
                copy1(k, h, j).start()

    def send_sum(i, carry):
        remote(rxd.at[p], rxd.at[p], st2.at[i - 1], rt2.at[p], ((p + i) % N_DP, g)).start()
        return carry

    @pl.when(g < SMALL_OWNERS)
    def _():
        def take(i, carry):
            s = (g + i) % N_SHARD
            remote(small.at[:, piece(0)], rxs.at[s], st1.at[0], rt1.at[s], (p, s)).wait_recv()
            return carry

        lax.fori_loop(1, N_SHARD, take, 0)
        rxs[g] = small[:, piece(g)]
        total = rxs[0]
        for s in range(1, N_SHARD):
            total = total + rxs[s]
        rxd[p] = total
        lax.fori_loop(1, N_DP, send_sum, 0)

    def copy2(k, h):
        q = mates[1 - h]
        return remote(
            own.at[k, :, q, :, cols(h)], rx2.at[k, h], s2.at[k, h], r2.at[k, h],
            (p, shard_index(x_lo, q, core)),
        )

    for k in range(CHUNKS):
        for h in range(2):
            copy1(k, h, 1).wait_recv()
            add_blocks(lambda i: own.at[k, i, mates[1 - h]], lambda i: rx1.at[k, h, 1, i], 2, cols(h))
            copy2(k, h).start()
            copy1(k, h, 0).wait_recv()
            add_blocks(lambda i: own.at[k, i, y], lambda i: rx1.at[k, h, 0, i], 2, cols(h))

    def send_final(i, carry):
        remote(
            small_fin.at[:, piece(g)], small_fin.at[:, piece(g)], st3.at[i - 1], rt3.at[g],
            (p, (g + i) % N_SHARD),
        ).start()
        return carry

    @pl.when(g < SMALL_OWNERS)
    def _():
        def take(i, carry):
            s = (p + i) % N_DP
            remote(rxd.at[s], rxd.at[s], st2.at[0], rt2.at[s], (s, g)).wait_recv()
            return carry

        lax.fori_loop(1, N_DP, take, 0)
        total = rxd[0]
        for s in range(1, N_DP):
            total = total + rxd[s]
        small_fin[:, piece(g)] = total
        lax.fori_loop(1, N_SHARD, send_final, 0)

    def copy3(k):
        return remote(
            own.at[k, 1 - x_lo, y], rx3.at[k], s3.at[k], r3.at[k], (p, shard_index(1 - x_lo, y, core))
        )

    for k in range(CHUNKS):
        for h in range(2):
            copy2(k, h).wait_recv()
            add_blocks(lambda i: own.at[k, i, y], lambda i: rx2.at[k, h, i], 2, cols(h))
        copy3(k).start()

    def at_piece(ref, d, base):
        return ref.at[
            pl.ds(pl.multiple_of((d % 2) * 48, 48), 48), pl.ds(pl.multiple_of(base + (d // 2) * 128, 128), 128)
        ]

    def copy4(k, i):
        d = (p + i) % N_DP
        return remote(
            at_piece(own.at[k, x_lo, y], d, 0), rx4.at[k, i - 1], s4.at[k, i - 1], r4.at[k, i - 1], (d, g)
        )

    def copy5(k, i):
        d = (p + i) % N_DP
        return remote(
            red.at[k], at_piece(fin, p, CHUNK * k), s5.at[k, i - 1], r5.at[k, i - 1], (d, g)
        )

    for k in range(CHUNKS):
        copy3(k).wait_recv()
        add_blocks(lambda i: own.at[k, x_lo, y], lambda i: rx3.at[k], 1, slice(None))

        def post(i, carry):
            copy4(k, i).start()
            return carry

        lax.fori_loop(1, N_DP, post, 0)

    for k in range(CHUNKS):
        def take(i, carry):
            copy4(k, i).wait_recv()
            return carry

        lax.fori_loop(1, N_DP, take, 0)
        total = at_piece(own.at[k, x_lo, y], p, 0)[...].astype(F32)
        for i in range(N_DP - 1):
            total = total + rx4[k, i].astype(F32)
        total = total.astype(BF)
        red[k] = total
        at_piece(fin, p, CHUNK * k)[...] = total

        def post(i, carry):
            copy5(k, i).start()
            return carry

        lax.fori_loop(1, N_DP, post, 0)

    def take_final(j, carry):
        @pl.when(j != g)
        def _():
            remote(
                small_fin.at[:, piece(j)], small_fin.at[:, piece(j)], st3.at[0], rt3.at[j], (p, j)
            ).wait_recv()

        return carry

    lax.fori_loop(0, SMALL_OWNERS, take_final, 0)
    small_out[...] = small_fin[...] * scale

    for k in range(CHUNKS):
        def take(i, carry):
            s = (p + N_DP - i) % N_DP
            remote(
                red.at[k], at_piece(fin, s, CHUNK * k), s5.at[k, i - 1], r5.at[k, i - 1], (s, g)
            ).wait_recv()
            return carry

        lax.fori_loop(1, N_DP, take, 0)

        def widen(i, carry):
            rows = pl.ds(pl.multiple_of(i * 48, 48), 48)
            out[rows, pl.ds(CHUNK * k, CHUNK)] = fin[rows, pl.ds(CHUNK * k, CHUNK)].astype(F32) * scale
            return carry

        lax.fori_loop(0, 2, widen, 0)

    for k in range(CHUNKS):
        copy0(k).wait_send()
        copy3(k).wait_send()
        for h in range(2):
            copy1(k, h, 0).wait_send()
            copy1(k, h, 1).wait_send()
            copy2(k, h).wait_send()

        def sent(i, carry):
            copy4(k, i).wait_send()
            copy5(k, i).wait_send()
            return carry

        lax.fori_loop(1, N_DP, sent, 0)

    def piece_sent(j, carry):
        @pl.when(j != g)
        def _():
            remote(small.at[:, piece(j)], rxs.at[g], st1.at[j], rt1.at[g], (p, j)).wait_send()

        return carry

    lax.fori_loop(0, SMALL_OWNERS, piece_sent, 0)

    @pl.when(g < SMALL_OWNERS)
    def _():
        def sums_sent(i, carry):
            remote(rxd.at[p], rxd.at[p], st2.at[i - 1], rt2.at[p], (p, g)).wait_send()
            remote(
                small_fin.at[:, piece(g)], small_fin.at[:, piece(g)], st3.at[i - 1], rt3.at[g], (p, g)
            ).wait_send()
            return carry

        lax.fori_loop(1, 16, sums_sent, 0)


def reduce_gradients(part, small):
    rows, cols = part.shape
    block = rows // N_SHARD
    width = small.shape[1]
    dma = pltpu.SemaphoreType.DMA
    return pl.pallas_call(
        reduce_kernel,
        out_shape=(
            jax.ShapeDtypeStruct((block, cols), F32),
            jax.ShapeDtypeStruct((SMALL_ROWS, width), F32),
        ),
        in_specs=[pl.BlockSpec(memory_space=pl.ANY), pl.BlockSpec(memory_space=pltpu.VMEM)],
        out_specs=(pl.BlockSpec(memory_space=pltpu.VMEM), pl.BlockSpec(memory_space=pltpu.VMEM)),
        scratch_shapes=[
            pltpu.VMEM((CHUNKS, 2, 4, block, CHUNK), BF),
            pltpu.VMEM((CHUNKS, 2, 4, block, CHUNK), BF),
            pltpu.VMEM((CHUNKS, 2, 2, 2, block, HALF), BF),
            pltpu.VMEM((CHUNKS, 2, 2, block, HALF), BF),
            pltpu.VMEM((CHUNKS, block, CHUNK), BF),
            pltpu.VMEM((CHUNKS, N_DP - 1, block // 2, 128), BF),
            pltpu.VMEM((CHUNKS, block // 2, 128), BF),
            pltpu.VMEM((block, cols), BF),
            pltpu.VMEM((N_SHARD, SMALL_ROWS, 128), F32),
            pltpu.VMEM((N_DP, SMALL_ROWS, 128), F32),
            pltpu.VMEM((SMALL_ROWS, width), F32),
            dma((CHUNKS,)),
            dma((CHUNKS,)), dma((CHUNKS,)),
            dma((CHUNKS, 2, 2)), dma((CHUNKS, 2, 2)),
            dma((CHUNKS, 2)), dma((CHUNKS, 2)),
            dma((CHUNKS,)), dma((CHUNKS,)),
            dma((CHUNKS, N_DP - 1)), dma((CHUNKS, N_DP - 1)),
            dma((CHUNKS, N_DP - 1)), dma((CHUNKS, N_DP - 1)),
            dma((SMALL_OWNERS,)), dma((N_SHARD,)),
            dma((N_DP - 1,)), dma((N_DP,)),
            dma((N_SHARD - 1,)), dma((SMALL_OWNERS,)),
        ],
        compiler_params=pltpu.CompilerParams(
            collective_id=1, has_side_effects=True, vmem_limit_bytes=40 * 1024 * 1024
        ),
        name="reduce_gradients",
    )(part.reshape(2, 4, 2, block, cols), small)


def gather_frames(pool, lengths, offsets, frame_count, slot_len):
    rows_here = jnp.arange(frame_count, dtype=jnp.int32)[:, None]
    member = ((rows_here >= offsets[None, :]) & (rows_here < (offsets + lengths)[None, :])).astype(
        jnp.int32
    )
    sources = jnp.arange(lengths.shape[0], dtype=jnp.int32)[None, :]
    owner = jnp.sum(member * sources, axis=1)
    within = jnp.sum(member * (rows_here - offsets[None, :]), axis=1)
    picked = jnp.take(pool, owner * slot_len + within, axis=0, mode="clip")
    return (picked, owner)


def normalize(values):
    center = values - jnp.mean(values, axis=1, keepdims=True)
    inverse = lax.rsqrt(jnp.mean(center * center, axis=1, keepdims=True) + EPSILON)
    return (center * inverse, inverse)


def normalize_back(grad_unit, unit, inverse):
    first = jnp.mean(grad_unit, axis=1, keepdims=True)
    second = jnp.mean(grad_unit * unit, axis=1, keepdims=True)
    return inverse * (grad_unit - first - unit * second)


def depth_forward(values, segment, kernel):
    count = values.shape[0]
    reach = (kernel.shape[0] - 1) // 2
    padded = jnp.pad(values, ((reach, reach), (0, 0)))
    labels = jnp.pad(segment, (reach, reach), constant_values=-1)
    total = jnp.zeros_like(values)
    for tap_index in range(kernel.shape[0]):
        same = (labels[tap_index : tap_index + count] == segment)[:, None]
        total = (
            total + jnp.where(same, padded[tap_index : tap_index + count], 0.0) * kernel[tap_index]
        )
    return total


def depth_backward(grads, segment, kernel):
    count = grads.shape[0]
    reach = (kernel.shape[0] - 1) // 2
    padded = jnp.pad(grads, ((reach, reach), (0, 0)))
    labels = jnp.pad(segment, (reach, reach), constant_values=-1)
    total = jnp.zeros_like(grads)
    for tap_index in range(kernel.shape[0]):
        begin = 2 * reach - tap_index
        same = (labels[begin : begin + count] == segment)[:, None]
        total = total + jnp.where(same, padded[begin : begin + count], 0.0) * kernel[tap_index]
    return total


def depth_weight_grad(grads, values, segment, taps_count):
    count = values.shape[0]
    reach = (taps_count - 1) // 2
    padded = jnp.pad(values, ((reach, reach), (0, 0)))
    labels = jnp.pad(segment, (reach, reach), constant_values=-1)
    collected = []
    for tap_index in range(taps_count):
        same = (labels[tap_index : tap_index + count] == segment)[:, None]
        collected.append(
            jnp.sum(jnp.where(same, padded[tap_index : tap_index + count], 0.0) * grads, axis=0)
        )
    return jnp.stack(collected, axis=0)


def body(frames, slot_dest, recv_length, recv_offset, gain1, w_in, w_depth, gain2, cotangent):
    frame_count = cotangent.shape[0]
    slot_len = frames.shape[1]
    model_width = frames.shape[2]
    taps = w_depth.shape[0]
    pool, full = exchange(frames, slot_dest, w_in)
    full_weight = full.reshape(model_width, 2 * model_width)
    inputs, segment = gather_frames(
        pool.reshape(-1, model_width), recv_length, recv_offset, frame_count, slot_len
    )
    unit_in, inverse_in = normalize(inputs.astype(F32))
    normed = (unit_in * gain1).astype(BF)
    projected = jnp.dot(normed, full_weight, preferred_element_type=F32)
    linear = projected[:, :model_width]
    gating = projected[:, model_width:]
    gate_sig = jax.nn.sigmoid(gating)
    gated = (linear * gate_sig).astype(BF)
    gated_wide = gated.astype(F32)
    convolved = depth_forward(gated_wide, segment, w_depth)
    unit_out, inverse_out = normalize(convolved)
    scaled = unit_out * gain2
    sig_out = jax.nn.sigmoid(scaled)
    output = (scaled * sig_out).astype(BF)
    grad_scaled = cotangent.astype(F32) * sig_out * (1.0 + scaled * (1.0 - sig_out))
    gain2_part = jnp.sum(grad_scaled * unit_out, axis=0)
    grad_conv = normalize_back(grad_scaled * gain2, unit_out, inverse_out)
    depth_part = depth_weight_grad(grad_conv, gated_wide, segment, taps)
    grad_gated = depth_backward(grad_conv, segment, w_depth)
    grad_pre = jnp.concatenate(
        [grad_gated * gate_sig, grad_gated * linear * gate_sig * (1.0 - gate_sig)], axis=1
    ).astype(BF)
    grad_normed = lax.dot_general(
        grad_pre, full_weight, (((1,), (1,)), ((), ())), preferred_element_type=F32
    )
    gain1_part = jnp.sum(grad_normed * unit_in, axis=0)
    grad_input = normalize_back(grad_normed * gain1, unit_in, inverse_in).astype(BF)
    weight_part = lax.dot_general(
        normed, grad_pre, (((0,), (0,)), ((), ())), preferred_element_type=F32
    ).astype(BF)
    small = jnp.concatenate(
        [depth_part, gain1_part[None], gain2_part[None], jnp.zeros((SMALL_ROWS - taps - 2, model_width), F32)], axis=0
    )
    grad_w, small_sum = reduce_gradients(weight_part, small)
    return (output, grad_input, grad_w, small_sum[:taps], small_sum[taps], small_sum[taps + 1])


def solution(mesh):
    in_specs = (
        P(("dp", "shard"), None, None),
        P(("dp", "shard")),
        P(("dp", "shard")),
        P(("dp", "shard")),
        P(),
        P("shard", None),
        P(),
        P(),
        P(("dp", "shard"), None),
    )
    out_specs = (
        P(("dp", "shard"), None),
        P(("dp", "shard"), None),
        P("shard", None),
        P(),
        P(),
        P(),
    )
    return jax.shard_map(body, mesh=mesh, in_specs=in_specs, out_specs=out_specs, check_vma=False)
```

```python
import jax
import jax.numpy as jnp
from jax import lax
from jax.experimental import pallas as pl
from jax.experimental.pallas import tpu as pltpu
from jax.sharding import PartitionSpec as P

EPSILON = 1e-05
MESH = pl.DeviceIdType.MESH
BF = jnp.bfloat16
F32 = jnp.float32

N_DP = 16
N_SHARD = 16
SMALL_ROWS = 40
SMALL_OWNERS = 12
CHUNKS = 3
CHUNK = 1024
HALF = CHUNK // 2


def shard_index(x_lo, y, core):
    return x_lo * 8 + y * 2 + core


def signal(sem, device):
    pl.semaphore_signal(sem, inc=1, device_id=device, device_id_type=MESH)


def remote(src, dst, send, recv, device):
    return pltpu.make_async_remote_copy(
        src_ref=src, dst_ref=dst, send_sem=send, recv_sem=recv, device_id=device, device_id_type=MESH
    )


def exchange_kernel(
    frames, slot_dest, w, pool, full, outgoing, own_sems, a2a_send, a2a_recv, w_send, w_recv
):
    p, g = lax.axis_index("dp"), lax.axis_index("shard")
    x_lo, y, core = g // 8, (g // 2) % 4, g % 2
    up, down, across = (y + 1) % 4, (y + 3) % 4, (y + 2) % 4
    g_x = shard_index(1 - x_lo, y, core)
    g_up = shard_index(x_lo, up, core)
    g_down = shard_index(x_lo, down, core)
    g_core = shard_index(x_lo, y, 1 - core)

    barrier = pltpu.get_barrier_semaphore()

    def greet(i, carry):
        signal(barrier, ((p + i) % N_DP, g))
        return carry

    lax.fori_loop(1, N_DP, greet, 0)
    for peer in (g_x, g_up, g_down, g_core):
        signal(barrier, (p, peer))

    own_w = pltpu.make_async_copy(w, full.at[g], own_sems.at[0])
    own_w.start()
    pl.semaphore_wait(barrier, N_DP - 1 + 4)

    def send(block, peer, slot, src=None):
        return remote(
            full.at[block] if src is None else src, full.at[block], w_send.at[slot], w_recv.at[slot], (p, peer)
        )

    sent = []

    def go(copy):
        copy.start()
        sent.append(copy)

    go(send(g, g_x, 0, w))
    go(send(g, g_up, 1, w))
    go(send(g, g_down, 2, w))
    go(send(g, g_core, 7, w))

    def source_of(d):
        index = jnp.int32(0)
        for j in range(N_DP):
            index = index + jnp.where(slot_dest[j] == d, j, 0)
        return jnp.minimum(index, N_DP - 1)

    def post(i, carry):
        d = (p + i) % N_DP
        outgoing[i] = frames[source_of(d)]
        remote(outgoing.at[i], pool.at[p], a2a_send.at[i - 1], a2a_recv.at[i - 1], (d, g)).start()
        return carry

    lax.fori_loop(1, N_DP, post, 0)
    outgoing[0] = frames[source_of(p)]
    own_frames = pltpu.make_async_copy(outgoing.at[0], pool.at[p], own_sems.at[1])
    own_frames.start()

    def arrived(block, slot):
        remote(full.at[block], full.at[block], w_send.at[slot], w_recv.at[slot], (p, g_x)).wait_recv()

    arrived(g_x, 0)
    go(send(g_x, g_up, 3))
    go(send(g_x, g_down, 4))
    go(send(g_x, g_core, 8))
    b = shard_index(x_lo, down, core)
    arrived(b, 1)
    go(send(b, g_up, 5))
    go(send(b, g_core, 9))
    b = shard_index(x_lo, up, core)
    arrived(b, 2)
    go(send(b, g_core, 10))
    b = shard_index(1 - x_lo, up, core)
    arrived(b, 4)
    go(send(b, g_down, 6))
    go(send(b, g_core, 11))
    b = shard_index(1 - x_lo, down, core)
    arrived(b, 3)
    go(send(b, g_core, 12))
    b = shard_index(x_lo, across, core)
    arrived(b, 5)
    go(send(b, g_core, 13))
    b = shard_index(1 - x_lo, across, core)
    arrived(b, 6)
    go(send(b, g_core, 14))
    other = 1 - core
    theirs = [
        (x_lo, y, 7), (1 - x_lo, y, 8), (x_lo, down, 9), (x_lo, up, 10),
        (1 - x_lo, up, 11), (1 - x_lo, down, 12), (x_lo, across, 13), (1 - x_lo, across, 14),
    ]
    for bx, by, slot in theirs:
        arrived(shard_index(bx, by, other), slot)

    def collect(i, carry):
        s = (p + N_DP - i) % N_DP
        copy = remote(outgoing.at[i], pool.at[s], a2a_send.at[i - 1], a2a_recv.at[i - 1], (s, g))
        copy.wait_recv()
        copy.wait_send()
        return carry

    lax.fori_loop(1, N_DP, collect, 0)
    for copy in sent:
        copy.wait_send()
    own_frames.wait()
    own_w.wait()


def exchange(frames, slot_dest, w):
    slots, slot_len, width = frames.shape
    rows, cols = w.shape
    return pl.pallas_call(
        exchange_kernel,
        out_shape=(
            jax.ShapeDtypeStruct((slots, slot_len, width), BF),
            jax.ShapeDtypeStruct((N_SHARD, rows, cols), BF),
        ),
        in_specs=[
            pl.BlockSpec(memory_space=pltpu.VMEM),
            pl.BlockSpec(memory_space=pltpu.SMEM),
            pl.BlockSpec(memory_space=pl.ANY),
        ],
        out_specs=(pl.BlockSpec(memory_space=pl.ANY), pl.BlockSpec(memory_space=pl.ANY)),
        scratch_shapes=[
            pltpu.VMEM((slots, slot_len, width), BF),
            pltpu.SemaphoreType.DMA((2,)),
            pltpu.SemaphoreType.DMA((N_DP - 1,)),
            pltpu.SemaphoreType.DMA((N_DP - 1,)),
            pltpu.SemaphoreType.DMA((15,)),
            pltpu.SemaphoreType.DMA((15,)),
        ],
        compiler_params=pltpu.CompilerParams(
            collective_id=0, has_side_effects=True, vmem_limit_bytes=32 * 1024 * 1024
        ),
        name="exchange",
    )(frames, slot_dest, w)


def add_blocks(dst, src, count, cols):
    def step(i, carry):
        block, row = i // 2, pl.multiple_of((i % 2) * 48, 48)
        d, s = dst(block), src(block)
        value = d[pl.ds(row, 48), cols].astype(F32) + s[pl.ds(row, 48), :].astype(F32)
        d[pl.ds(row, 48), cols] = value.astype(BF)
        return carry

    lax.fori_loop(0, count * 2, step, 0)


def reduce_kernel(
    part, small, out, small_out,
    own, rx0, rx1, rx2, rx3, rx4, red, fin, rxs, rxd, small_fin,
    load_sems, s0, r0, s1, r1, s2, r2, s3, r3, s4, r4, s5, r5, st1, rt1, st2, rt2, st3, rt3,
):
    p, g = lax.axis_index("dp"), lax.axis_index("shard")
    z, x_hi = p // 2, p % 2
    x_lo, y, core = g // 8, (g // 2) % 4, g % 2
    y_a, y_b = y + 1 - 2 * (y % 2), 3 - y
    mates = (y_a, y_b)
    scale = 1.0 / (N_DP * N_SHARD)

    def load(k):
        return pltpu.make_async_copy(
            part.at[k, :, :, core], own.at[k], load_sems.at[k]
        )

    for k in range(CHUNKS):
        load(k).start()

    barrier = pltpu.get_barrier_semaphore()

    def greet(i, carry):
        signal(barrier, ((p + i) % N_DP, g))
        signal(barrier, (p, (g + i) % N_SHARD))
        return carry

    lax.fori_loop(1, 16, greet, 0)
    pl.semaphore_wait(barrier, 30)

    def copy0(k):
        return remote(
            part.at[k, :, :, 1 - core], rx0.at[k], s0.at[k], r0.at[k],
            (p, shard_index(x_lo, y, 1 - core)),
        )

    for k in range(CHUNKS):
        copy0(k).start()

    def piece(j):
        return pl.ds(pl.multiple_of(j * 128, 128), 128)

    def send_piece(j, carry):
        @pl.when(j != g)
        def _():
            remote(small.at[:, piece(j)], rxs.at[g], st1.at[j], rt1.at[g], (p, j)).start()

        return carry

    lax.fori_loop(0, SMALL_OWNERS, send_piece, 0)

    def cols(h):
        return pl.ds(HALF * h, HALF)

    def copy1(k, h, j):
        q = mates[h]
        after = 3 - q if h == 0 else q + 1 - 2 * (q % 2)
        block = q if j == 0 else after
        return remote(
            own.at[k, :, block, :, cols(h)], rx1.at[k, h, j], s1.at[k, h, j], r1.at[k, h, j],
            (p, shard_index(x_lo, q, core)),
        )

    for k in range(CHUNKS):
        load(k).wait()
        copy0(k).wait_recv()
        add_blocks(
            lambda i: own.at[k, i // 4, i % 4], lambda i: rx0.at[k, i // 4, i % 4], 8, slice(None)
        )
        for h in range(2):
            for j in (1, 0):
                copy1(k, h, j).start()

    def send_sum(i, carry):
        remote(rxd.at[p], rxd.at[p], st2.at[i - 1], rt2.at[p], ((p + i) % N_DP, g)).start()
        return carry

    @pl.when(g < SMALL_OWNERS)
    def _():
        def take(i, carry):
            s = (g + i) % N_SHARD
            remote(small.at[:, piece(0)], rxs.at[s], st1.at[0], rt1.at[s], (p, s)).wait_recv()
            return carry

        lax.fori_loop(1, N_SHARD, take, 0)
        rxs[g] = small[:, piece(g)]
        total = rxs[0]
        for s in range(1, N_SHARD):
            total = total + rxs[s]
        rxd[p] = total
        lax.fori_loop(1, N_DP, send_sum, 0)

    def copy2(k, h):
        q = mates[1 - h]
        return remote(
            own.at[k, :, q, :, cols(h)], rx2.at[k, h], s2.at[k, h], r2.at[k, h],
            (p, shard_index(x_lo, q, core)),
        )

    for k in range(CHUNKS):
        for h in range(2):
            copy1(k, h, 1).wait_recv()
            add_blocks(lambda i: own.at[k, i, mates[1 - h]], lambda i: rx1.at[k, h, 1, i], 2, cols(h))
            copy2(k, h).start()
            copy1(k, h, 0).wait_recv()
            add_blocks(lambda i: own.at[k, i, y], lambda i: rx1.at[k, h, 0, i], 2, cols(h))

    def send_final(i, carry):
        remote(
            small_fin.at[:, piece(g)], small_fin.at[:, piece(g)], st3.at[i - 1], rt3.at[g],
            (p, (g + i) % N_SHARD),
        ).start()
        return carry

    @pl.when(g < SMALL_OWNERS)
    def _():
        def take(i, carry):
            s = (p + i) % N_DP
            remote(rxd.at[s], rxd.at[s], st2.at[0], rt2.at[s], (s, g)).wait_recv()
            return carry

        lax.fori_loop(1, N_DP, take, 0)
        total = rxd[0]
        for s in range(1, N_DP):
            total = total + rxd[s]
        small_fin[:, piece(g)] = total
        lax.fori_loop(1, N_SHARD, send_final, 0)

    def copy3(k):
        return remote(
            own.at[k, 1 - x_lo, y], rx3.at[k], s3.at[k], r3.at[k], (p, shard_index(1 - x_lo, y, core))
        )

    for k in range(CHUNKS):
        for h in range(2):
            copy2(k, h).wait_recv()
            add_blocks(lambda i: own.at[k, i, y], lambda i: rx2.at[k, h, i], 2, cols(h))
        copy3(k).start()

    def at_piece(ref, d, base):
        return ref.at[
            pl.ds(pl.multiple_of((d % 2) * 48, 48), 48), pl.ds(pl.multiple_of(base + (d // 2) * 128, 128), 128)
        ]

    def copy4(k, i):
        d = (p + i) % N_DP
        return remote(
            at_piece(own.at[k, x_lo, y], d, 0), rx4.at[k, i - 1], s4.at[k, i - 1], r4.at[k, i - 1], (d, g)
        )

    def copy5(k, i):
        d = (p + i) % N_DP
        return remote(
            red.at[k], at_piece(fin, p, CHUNK * k), s5.at[k, i - 1], r5.at[k, i - 1], (d, g)
        )

    for k in range(CHUNKS):
        copy3(k).wait_recv()
        add_blocks(lambda i: own.at[k, x_lo, y], lambda i: rx3.at[k], 1, slice(None))

        def post(i, carry):
            copy4(k, i).start()
            return carry

        lax.fori_loop(1, N_DP, post, 0)

    for k in range(CHUNKS):
        def take(i, carry):
            copy4(k, i).wait_recv()
            return carry

        lax.fori_loop(1, N_DP, take, 0)
        total = at_piece(own.at[k, x_lo, y], p, 0)[...].astype(F32)
        for i in range(N_DP - 1):
            total = total + rx4[k, i].astype(F32)
        total = total.astype(BF)
        red[k] = total
        at_piece(fin, p, CHUNK * k)[...] = total

        def post(i, carry):
            copy5(k, i).start()
            return carry

        lax.fori_loop(1, N_DP, post, 0)

    def take_final(j, carry):
        @pl.when(j != g)
        def _():
            remote(
                small_fin.at[:, piece(j)], small_fin.at[:, piece(j)], st3.at[0], rt3.at[j], (p, j)
            ).wait_recv()

        return carry

    lax.fori_loop(0, SMALL_OWNERS, take_final, 0)
    small_out[...] = small_fin[...] * scale

    for k in range(CHUNKS):
        def take(i, carry):
            s = (p + N_DP - i) % N_DP
            remote(
                red.at[k], at_piece(fin, s, CHUNK * k), s5.at[k, i - 1], r5.at[k, i - 1], (s, g)
            ).wait_recv()
            return carry

        lax.fori_loop(1, N_DP, take, 0)

        def widen(i, carry):
            rows = pl.ds(pl.multiple_of(i * 48, 48), 48)
            for h in range(2):
                out[rows, pl.ds(h * WIDTH + HALF * k, HALF)] = (
                    fin[rows, pl.ds(CHUNK * k + HALF * h, HALF)].astype(F32) * scale
                )
            return carry

        lax.fori_loop(0, 2, widen, 0)

    for k in range(CHUNKS):
        copy0(k).wait_send()
        copy3(k).wait_send()
        for h in range(2):
            copy1(k, h, 0).wait_send()
            copy1(k, h, 1).wait_send()
            copy2(k, h).wait_send()

        def sent(i, carry):
            copy4(k, i).wait_send()
            copy5(k, i).wait_send()
            return carry

        lax.fori_loop(1, N_DP, sent, 0)

    def piece_sent(j, carry):
        @pl.when(j != g)
        def _():
            remote(small.at[:, piece(j)], rxs.at[g], st1.at[j], rt1.at[g], (p, j)).wait_send()

        return carry

    lax.fori_loop(0, SMALL_OWNERS, piece_sent, 0)

    @pl.when(g < SMALL_OWNERS)
    def _():
        def sums_sent(i, carry):
            remote(rxd.at[p], rxd.at[p], st2.at[i - 1], rt2.at[p], (p, g)).wait_send()
            remote(
                small_fin.at[:, piece(g)], small_fin.at[:, piece(g)], st3.at[i - 1], rt3.at[g], (p, g)
            ).wait_send()
            return carry

        lax.fori_loop(1, 16, sums_sent, 0)


def reduce_gradients(part, small):
    block, cols = part.shape[4], CHUNKS * part.shape[5]
    width = small.shape[1]
    dma = pltpu.SemaphoreType.DMA
    return pl.pallas_call(
        reduce_kernel,
        out_shape=(
            jax.ShapeDtypeStruct((block, cols), F32),
            jax.ShapeDtypeStruct((SMALL_ROWS, width), F32),
        ),
        in_specs=[pl.BlockSpec(memory_space=pl.ANY), pl.BlockSpec(memory_space=pltpu.VMEM)],
        out_specs=(pl.BlockSpec(memory_space=pltpu.VMEM), pl.BlockSpec(memory_space=pltpu.VMEM)),
        scratch_shapes=[
            pltpu.VMEM((CHUNKS, 2, 4, block, CHUNK), BF),
            pltpu.VMEM((CHUNKS, 2, 4, block, CHUNK), BF),
            pltpu.VMEM((CHUNKS, 2, 2, 2, block, HALF), BF),
            pltpu.VMEM((CHUNKS, 2, 2, block, HALF), BF),
            pltpu.VMEM((CHUNKS, block, CHUNK), BF),
            pltpu.VMEM((CHUNKS, N_DP - 1, block // 2, 128), BF),
            pltpu.VMEM((CHUNKS, block // 2, 128), BF),
            pltpu.VMEM((block, cols), BF),
            pltpu.VMEM((N_SHARD, SMALL_ROWS, 128), F32),
            pltpu.VMEM((N_DP, SMALL_ROWS, 128), F32),
            pltpu.VMEM((SMALL_ROWS, width), F32),
            dma((CHUNKS,)),
            dma((CHUNKS,)), dma((CHUNKS,)),
            dma((CHUNKS, 2, 2)), dma((CHUNKS, 2, 2)),
            dma((CHUNKS, 2)), dma((CHUNKS, 2)),
            dma((CHUNKS,)), dma((CHUNKS,)),
            dma((CHUNKS, N_DP - 1)), dma((CHUNKS, N_DP - 1)),
            dma((CHUNKS, N_DP - 1)), dma((CHUNKS, N_DP - 1)),
            dma((SMALL_OWNERS,)), dma((N_SHARD,)),
            dma((N_DP - 1,)), dma((N_DP,)),
            dma((N_SHARD - 1,)), dma((SMALL_OWNERS,)),
        ],
        compiler_params=pltpu.CompilerParams(
            collective_id=1, has_side_effects=True, vmem_limit_bytes=40 * 1024 * 1024
        ),
        name="reduce_gradients",
    )(part, small)


ROWS = 384
WIDTH = 1536
TAPS = 31
REACH = 15
PAD = 16
LANES = 128
BLOCKS = WIDTH // LANES
TILE = 256
GROUP = 48


def sigmoid(v):
    return 1.0 / (1.0 + jnp.exp(-v))


def dot(a, b):
    return lax.dot_general(a, b, (((1,), (0,)), ((), ())), preferred_element_type=F32)


def dot_t(a, b):
    return lax.dot_general(a, b, (((1,), (1,)), ((), ())), preferred_element_type=F32)


def row_mean(blocks):
    total = blocks[0]
    for b in blocks[1:]:
        total = total + b
    return jnp.sum(total, axis=1, keepdims=True) * (1.0 / WIDTH)


def lanes(b):
    return pl.ds(b * LANES, LANES)


def load_inputs(lengths, offsets, pool, gain1, r):
    slot_len = pool.shape[0] // N_DP
    rows = lax.broadcasted_iota(jnp.int32, (ROWS, LANES), 0)
    pick = jnp.zeros((ROWS, LANES), jnp.int32)
    behind = jnp.zeros((ROWS, LANES), jnp.int32)
    ahead = jnp.zeros((ROWS, LANES), jnp.int32)
    for s in range(N_DP):
        begin = offsets[s]
        end = begin + lengths[s]
        inside = (rows >= begin) & (rows < end)
        pick = jnp.where(inside, rows - begin + s * slot_len, pick)
        behind = jnp.where(inside, rows - begin, behind)
        ahead = jnp.where(inside, end - 1 - rows, ahead)
    r["behind"][...] = behind
    r["ahead"][...] = ahead
    lane = lax.broadcasted_iota(jnp.int32, (ROWS, LANES), 1)
    for t in range(pool.shape[0] // LANES):
        r["chosen"][:, lanes(t)] = (pick == lane + t * LANES).astype(F32).astype(BF)

    def gather(t, carry):
        cols = pl.ds(pl.multiple_of(t * TILE, TILE), TILE)
        r["unit_in"][:, cols] = dot(r["chosen"][...], pool[:, cols])
        return carry

    lax.fori_loop(0, WIDTH // TILE, gather, 0)

    def norm(i, carry):
        rows = pl.ds(pl.multiple_of(i * 16, 16), 16)
        x = [r["unit_in"][rows, lanes(b)] for b in range(BLOCKS)]
        mean = row_mean(x)
        x = [v - mean for v in x]
        inverse = lax.rsqrt(row_mean([v * v for v in x]) + EPSILON)
        r["inv_in"][rows, :] = jnp.broadcast_to(inverse, (16, LANES))
        for b in range(BLOCKS):
            unit = x[b] * inverse
            r["unit_in"][rows, lanes(b)] = unit
            r["normed"][rows, lanes(b)] = (unit * gain1[:, lanes(b)]).astype(BF)
        return carry

    lax.fori_loop(0, ROWS // 16, norm, 0)


def transpose_normed(r):
    for b in range(BLOCKS):
        r["normed_t"][lanes(b), :] = r["normed"][:, lanes(b)].T


def project(w, wait_tile, r):
    def tile(t, carry):
        wait_tile(t)
        cols = pl.ds(pl.multiple_of(t * TILE, TILE), TILE)
        gates = pl.ds(pl.multiple_of(t * TILE + WIDTH, TILE), TILE)
        linear = dot(r["normed"][...], w[:, cols])
        sig = sigmoid(dot(r["normed"][...], w[:, gates]))
        r["linear"][:, cols] = linear
        r["sig"][:, cols] = sig
        gated = (linear * sig).astype(BF).astype(F32)
        for j in range(TILE // LANES):
            r["gated"][t * (TILE // LANES) + j, PAD : PAD + ROWS, :] = gated[:, j * LANES : (j + 1) * LANES]
        return carry

    lax.fori_loop(0, WIDTH // TILE, tile, 0)


def tap_mask(behind, ahead, shift):
    return ahead >= shift if shift > 0 else behind >= -shift


def convolve(w_depth, r):
    def pair(c, carry):
        for g in range(ROWS // GROUP):
            begin = g * GROUP
            behind = r["behind"][begin : begin + GROUP, :]
            ahead = r["ahead"][begin : begin + GROUP, :]
            total = [jnp.zeros((GROUP, LANES), F32)] * 2
            for k in range(TAPS):
                shift = k - REACH
                same = tap_mask(behind, ahead, shift)
                for j in range(2):
                    b = c * 2 + j
                    x = r["gated"][b, PAD + begin + shift : PAD + begin + shift + GROUP, :]
                    if shift != 0:
                        x = jnp.where(same, x, 0.0)
                    total[j] = total[j] + x * w_depth[b, k : k + 1, :]
            for j in range(2):
                r["conv"][c * 2 + j, PAD + begin : PAD + begin + GROUP, :] = total[j]
        return carry

    lax.fori_loop(0, BLOCKS // 2, pair, 0)


def finish_forward(gain2, cotangent, output, r):
    r["gain2_sum"][...] = jnp.zeros_like(r["gain2_sum"])

    def rows16(i, carry):
        rows = pl.ds(pl.multiple_of(i * 16, 16), 16)
        held = pl.ds(pl.multiple_of(i * 16 + PAD, 16), 16)
        x = [r["conv"][b, held, :] for b in range(BLOCKS)]
        mean = row_mean(x)
        x = [v - mean for v in x]
        inverse = lax.rsqrt(row_mean([v * v for v in x]) + EPSILON)
        units, grads = [], []
        for b in range(BLOCKS):
            unit = x[b] * inverse
            gain = gain2[:, lanes(b)]
            scaled = unit * gain
            sig = sigmoid(scaled)
            output[rows, lanes(b)] = (scaled * sig).astype(BF)
            grad = cotangent[rows, lanes(b)].astype(F32) * sig * (1.0 + scaled * (1.0 - sig))
            both = grad * unit
            r["gain2_sum"][b] = r["gain2_sum"][b] + (both[:8] + both[8:])
            units.append(unit)
            grads.append(grad * gain)
        first = row_mean(grads)
        second = row_mean([q * u for q, u in zip(grads, units)])
        for b in range(BLOCKS):
            r["conv"][b, held, :] = inverse * (grads[b] - first - units[b] * second)
        return carry

    lax.fori_loop(0, ROWS // 16, rows16, 0)


def back_convolve(chunk, w_depth, small, r):
    def pair(c, carry):
        first = chunk * (HALF // LANES) + c * 2
        r["tap_sum"][...] = jnp.zeros_like(r["tap_sum"])
        for g in range(ROWS // GROUP):
            begin = g * GROUP
            rows = slice(begin, begin + GROUP)
            behind = r["behind"][rows, :]
            ahead = r["ahead"][rows, :]
            total = [jnp.zeros((GROUP, LANES), F32)] * 2
            gated = [r["gated"][first + j, PAD + begin : PAD + begin + GROUP, :] for j in range(2)]
            for k in range(TAPS):
                shift = REACH - k
                same = tap_mask(behind, ahead, shift)
                for j in range(2):
                    x = r["conv"][first + j, PAD + begin + shift : PAD + begin + shift + GROUP, :]
                    if shift != 0:
                        x = jnp.where(same, x, 0.0)
                    total[j] = total[j] + x * w_depth[first + j, k : k + 1, :]
                    product = x * gated[j]
                    part = product[0:8]
                    for q in range(1, GROUP // 8):
                        part = part + product[q * 8 : (q + 1) * 8]
                    r["tap_sum"][j, k] = r["tap_sum"][j, k] + part
            for j in range(2):
                at = pl.multiple_of((first + j) * LANES, LANES)
                linear = r["linear"][rows, pl.ds(at, LANES)]
                sig = r["sig"][rows, pl.ds(at, LANES)]
                grad = total[j] * sig
                r["grad_pre"][rows, pl.ds(at, LANES)] = grad.astype(BF)
                r["grad_pre"][rows, pl.ds(at + WIDTH, LANES)] = (grad * linear * (1.0 - sig)).astype(BF)
        for j in range(2):
            at = pl.multiple_of((first + j) * LANES, LANES)
            small[0:TAPS, pl.ds(at, LANES)] = jnp.sum(r["tap_sum"][j], axis=1)
        return carry

    lax.fori_loop(0, HALF // LANES // 2, pair, 0)


def weight_term(chunk, part, r):
    def tile(i, carry):
        rows = pl.ds(pl.multiple_of(i * 384, 384), 384)
        for h in range(2):
            cols = pl.ds(h * WIDTH + chunk * HALF, HALF)
            value = dot(r["normed_t"][rows, :], r["grad_pre"][:, cols]).astype(BF)
            for q in range(4):
                part[i // 2, (i % 2) * 2 + q // 2, q % 2, :, h * HALF : (h + 1) * HALF] = value[q * 96 : (q + 1) * 96]
        return carry

    lax.fori_loop(0, 4, tile, 0)


def finish_back(w, gain1, grad_input, small, r):
    def tile(t, carry):
        cols = pl.ds(pl.multiple_of(t * TILE, TILE), TILE)
        r["linear"][:, cols] = dot_t(r["grad_pre"][...], w[cols, :])
        return carry

    lax.fori_loop(0, WIDTH // TILE, tile, 0)
    r["gain1_sum"][...] = jnp.zeros_like(r["gain1_sum"])

    def rows16(i, carry):
        rows = pl.ds(pl.multiple_of(i * 16, 16), 16)
        inverse = r["inv_in"][rows, :]
        units = [r["unit_in"][rows, lanes(b)] for b in range(BLOCKS)]
        grads = [r["linear"][rows, lanes(b)] for b in range(BLOCKS)]
        for b in range(BLOCKS):
            both = grads[b] * units[b]
            r["gain1_sum"][b] = r["gain1_sum"][b] + (both[:8] + both[8:])
        grads = [grads[b] * gain1[:, lanes(b)] for b in range(BLOCKS)]
        first = row_mean(grads)
        second = row_mean([q * u for q, u in zip(grads, units)])
        for b in range(BLOCKS):
            grad_input[rows, lanes(b)] = (inverse * (grads[b] - first - units[b] * second)).astype(BF)
        return carry

    lax.fori_loop(0, ROWS // 16, rows16, 0)
    for b in range(BLOCKS):
        small[TAPS : TAPS + 1, lanes(b)] = jnp.sum(r["gain1_sum"][b], axis=0, keepdims=True)
        small[TAPS + 1 : TAPS + 2, lanes(b)] = jnp.sum(r["gain2_sum"][b], axis=0, keepdims=True)
    small[TAPS + 2 : SMALL_ROWS, :] = jnp.zeros((SMALL_ROWS - TAPS - 2, WIDTH), F32)


WORK = (
    ("behind", (ROWS, LANES), jnp.int32),
    ("ahead", (ROWS, LANES), jnp.int32),
    ("chosen", (ROWS, 640), BF),
    ("unit_in", (ROWS, WIDTH), F32),
    ("inv_in", (ROWS, LANES), F32),
    ("normed", (ROWS, WIDTH), BF),
    ("normed_t", (WIDTH, ROWS), BF),
    ("linear", (ROWS, WIDTH), F32),
    ("sig", (ROWS, WIDTH), F32),
    ("gated", (BLOCKS, PAD + ROWS + PAD, LANES), F32),
    ("conv", (BLOCKS, PAD + ROWS + PAD, LANES), F32),
    ("gain1_sum", (BLOCKS, 8, LANES), F32),
    ("gain2_sum", (BLOCKS, 8, LANES), F32),
    ("tap_sum", (2, TAPS, 8, LANES), F32),
    ("grad_pre", (ROWS, 2 * WIDTH), BF),
)


def forward(lengths, offsets, pool, w_hbm, gain1, w_depth, gain2, cotangent, output, w, w_sems, r):
    def copy_w(t, h):
        cols = pl.ds(pl.multiple_of(t * TILE + h * WIDTH, TILE), TILE)
        return pltpu.make_async_copy(w_hbm.at[:, cols], w.at[:, cols], w_sems.at[h, t])

    for t in range(WIDTH // TILE):
        for h in range(2):
            copy_w(t, h).start()

    def wait_tile(t):
        for h in range(2):
            copy_w(t, h).wait()

    for name in ("gated", "conv"):
        r[name][:, 0:PAD, :] = jnp.zeros((BLOCKS, PAD, LANES), F32)
        r[name][:, PAD + ROWS :, :] = jnp.zeros((BLOCKS, PAD, LANES), F32)
    load_inputs(lengths, offsets, pool, gain1, r)
    project(w, wait_tile, r)
    convolve(w_depth, r)
    finish_forward(gain2, cotangent, output, r)
    transpose_normed(r)


def module_kernel(
    lengths, offsets, pool, w_hbm, gain1, w_depth, gain2, cotangent,
    output, grad_input, part, small, w, w_sems, *work
):
    r = {name: ref for (name, _, _), ref in zip(WORK, work)}
    forward(lengths, offsets, pool, w_hbm, gain1, w_depth, gain2, cotangent, output, w, w_sems, r)
    for chunk in range(CHUNKS):
        back_convolve(chunk, w_depth, small, r)
        weight_term(chunk, part.at[chunk], r)
    finish_back(w, gain1, grad_input, small, r)


def module(lengths, offsets, pool, full, gain1, w_depth, gain2, cotangent):
    vmem = pl.BlockSpec(memory_space=pltpu.VMEM)
    smem = pl.BlockSpec(memory_space=pltpu.SMEM)
    block = WIDTH // N_SHARD
    return pl.pallas_call(
        module_kernel,
        out_shape=(
            jax.ShapeDtypeStruct((ROWS, WIDTH), BF),
            jax.ShapeDtypeStruct((ROWS, WIDTH), BF),
            jax.ShapeDtypeStruct((CHUNKS, 2, 4, 2, block, CHUNK), BF),
            jax.ShapeDtypeStruct((SMALL_ROWS, WIDTH), F32),
        ),
        in_specs=[smem, smem, vmem, pl.BlockSpec(memory_space=pl.ANY), vmem, vmem, vmem, vmem],
        out_specs=(vmem,) * 4,
        scratch_shapes=[
            pltpu.VMEM((WIDTH, 2 * WIDTH), BF),
            pltpu.SemaphoreType.DMA((2, WIDTH // TILE)),
            *[pltpu.VMEM(shape, dtype) for _, shape, dtype in WORK],
        ],
        compiler_params=pltpu.CompilerParams(vmem_limit_bytes=58 * 1024 * 1024),
        name="module",
    )(lengths, offsets, pool, full, gain1, w_depth, gain2, cotangent)


def body(frames, slot_dest, recv_length, recv_offset, gain1, w_in, w_depth, gain2, cotangent):
    model_width = frames.shape[2]
    taps = w_depth.shape[0]
    pool, full = exchange(frames, slot_dest, w_in)
    blocked = w_depth.reshape(taps, BLOCKS, LANES).transpose(1, 0, 2)
    output, grad_input, part, small = module(
        recv_length, recv_offset, pool.reshape(-1, model_width), full.reshape(model_width, 2 * model_width),
        gain1[None], blocked, gain2[None], cotangent,
    )
    grad_w, small_sum = reduce_gradients(part, small)
    return (output, grad_input, grad_w, small_sum[:taps], small_sum[taps], small_sum[taps + 1])


def solution(mesh):
    in_specs = (
        P(("dp", "shard"), None, None),
        P(("dp", "shard")),
        P(("dp", "shard")),
        P(("dp", "shard")),
        P(),
        P("shard", None),
        P(),
        P(),
        P(("dp", "shard"), None),
    )
    out_specs = (
        P(("dp", "shard"), None),
        P(("dp", "shard"), None),
        P("shard", None),
        P(),
        P(),
        P(),
    )
    return jax.shard_map(body, mesh=mesh, in_specs=in_specs, out_specs=out_specs, check_vma=False)
```

```python
import jax
import jax.numpy as jnp
from jax import lax
from jax.experimental import pallas as pl
from jax.experimental.pallas import tpu as pltpu
from jax.sharding import PartitionSpec as P

EPSILON = 1e-05
MESH = pl.DeviceIdType.MESH
BF = jnp.bfloat16
F32 = jnp.float32

N_DP = 16
N_SHARD = 16
SMALL_ROWS = 40
SMALL_OWNERS = 12
CHUNKS = 3
CHUNK = 1024
HALF = CHUNK // 2


def shard_index(x_lo, y, core):
    return x_lo * 8 + y * 2 + core


def signal(sem, device):
    pl.semaphore_signal(sem, inc=1, device_id=device, device_id_type=MESH)


def remote(src, dst, send, recv, device):
    return pltpu.make_async_remote_copy(
        src_ref=src, dst_ref=dst, send_sem=send, recv_sem=recv, device_id=device, device_id_type=MESH
    )


def exchange_kernel(
    frames, slot_dest, w, pool, full, outgoing, own_sems, a2a_send, a2a_recv, w_send, w_recv
):
    p, g = lax.axis_index("dp"), lax.axis_index("shard")
    x_lo, y, core = g // 8, (g // 2) % 4, g % 2
    up, down, across = (y + 1) % 4, (y + 3) % 4, (y + 2) % 4
    g_x = shard_index(1 - x_lo, y, core)
    g_up = shard_index(x_lo, up, core)
    g_down = shard_index(x_lo, down, core)
    g_core = shard_index(x_lo, y, 1 - core)

    barrier = pltpu.get_barrier_semaphore()

    def greet(i, carry):
        signal(barrier, ((p + i) % N_DP, g))
        return carry

    lax.fori_loop(1, N_DP, greet, 0)
    for peer in (g_x, g_up, g_down, g_core):
        signal(barrier, (p, peer))

    own_w = pltpu.make_async_copy(w, full.at[g], own_sems.at[0])
    own_w.start()
    pl.semaphore_wait(barrier, N_DP - 1 + 4)

    def send(block, peer, slot, src=None):
        return remote(
            full.at[block] if src is None else src, full.at[block], w_send.at[slot], w_recv.at[slot], (p, peer)
        )

    sent = []

    def go(copy):
        copy.start()
        sent.append(copy)

    go(send(g, g_x, 0, w))
    go(send(g, g_up, 1, w))
    go(send(g, g_down, 2, w))
    go(send(g, g_core, 7, w))

    def source_of(d):
        index = jnp.int32(0)
        for j in range(N_DP):
            index = index + jnp.where(slot_dest[j] == d, j, 0)
        return jnp.minimum(index, N_DP - 1)

    def post(i, carry):
        d = (p + i) % N_DP
        outgoing[i] = frames[source_of(d)]
        remote(outgoing.at[i], pool.at[p], a2a_send.at[i - 1], a2a_recv.at[i - 1], (d, g)).start()
        return carry

    lax.fori_loop(1, N_DP, post, 0)
    outgoing[0] = frames[source_of(p)]
    own_frames = pltpu.make_async_copy(outgoing.at[0], pool.at[p], own_sems.at[1])
    own_frames.start()

    def arrived(block, slot):
        remote(full.at[block], full.at[block], w_send.at[slot], w_recv.at[slot], (p, g_x)).wait_recv()

    arrived(g_x, 0)
    go(send(g_x, g_up, 3))
    go(send(g_x, g_down, 4))
    go(send(g_x, g_core, 8))
    b = shard_index(x_lo, down, core)
    arrived(b, 1)
    go(send(b, g_up, 5))
    go(send(b, g_core, 9))
    b = shard_index(x_lo, up, core)
    arrived(b, 2)
    go(send(b, g_core, 10))
    b = shard_index(1 - x_lo, up, core)
    arrived(b, 4)
    go(send(b, g_down, 6))
    go(send(b, g_core, 11))
    b = shard_index(1 - x_lo, down, core)
    arrived(b, 3)
    go(send(b, g_core, 12))
    b = shard_index(x_lo, across, core)
    arrived(b, 5)
    go(send(b, g_core, 13))
    b = shard_index(1 - x_lo, across, core)
    arrived(b, 6)
    go(send(b, g_core, 14))
    other = 1 - core
    theirs = [
        (x_lo, y, 7), (1 - x_lo, y, 8), (x_lo, down, 9), (x_lo, up, 10),
        (1 - x_lo, up, 11), (1 - x_lo, down, 12), (x_lo, across, 13), (1 - x_lo, across, 14),
    ]
    for bx, by, slot in theirs:
        arrived(shard_index(bx, by, other), slot)

    def collect(i, carry):
        s = (p + N_DP - i) % N_DP
        copy = remote(outgoing.at[i], pool.at[s], a2a_send.at[i - 1], a2a_recv.at[i - 1], (s, g))
        copy.wait_recv()
        copy.wait_send()
        return carry

    lax.fori_loop(1, N_DP, collect, 0)
    for copy in sent:
        copy.wait_send()
    own_frames.wait()
    own_w.wait()


def exchange(frames, slot_dest, w):
    slots, slot_len, width = frames.shape
    rows, cols = w.shape
    return pl.pallas_call(
        exchange_kernel,
        out_shape=(
            jax.ShapeDtypeStruct((slots, slot_len, width), BF),
            jax.ShapeDtypeStruct((N_SHARD, rows, cols), BF),
        ),
        in_specs=[
            pl.BlockSpec(memory_space=pltpu.VMEM),
            pl.BlockSpec(memory_space=pltpu.SMEM),
            pl.BlockSpec(memory_space=pl.ANY),
        ],
        out_specs=(pl.BlockSpec(memory_space=pl.ANY), pl.BlockSpec(memory_space=pl.ANY)),
        scratch_shapes=[
            pltpu.VMEM((slots, slot_len, width), BF),
            pltpu.SemaphoreType.DMA((2,)),
            pltpu.SemaphoreType.DMA((N_DP - 1,)),
            pltpu.SemaphoreType.DMA((N_DP - 1,)),
            pltpu.SemaphoreType.DMA((15,)),
            pltpu.SemaphoreType.DMA((15,)),
        ],
        compiler_params=pltpu.CompilerParams(
            collective_id=0, has_side_effects=True, vmem_limit_bytes=32 * 1024 * 1024
        ),
        name="exchange",
    )(frames, slot_dest, w)


ROWS = 384
WIDTH = 1536
TAPS = 31
REACH = 15
PAD = 16
LANES = 128
BLOCKS = WIDTH // LANES
TILE = 256
GROUP = 48
STEP = 32


def sigmoid(v):
    return 1.0 / (1.0 + jnp.exp(-v))


def dot(a, b):
    return lax.dot_general(a, b, (((1,), (0,)), ((), ())), preferred_element_type=F32)


def dot_t(a, b):
    return lax.dot_general(a, b, (((1,), (1,)), ((), ())), preferred_element_type=F32)


def fold(v):
    total = v[0:8]
    for q in range(1, v.shape[0] // 8):
        total = total + v[q * 8 : (q + 1) * 8]
    return total


def row_mean(blocks):
    total = blocks[0]
    for b in blocks[1:]:
        total = total + b
    return jnp.sum(total, axis=1, keepdims=True) * (1.0 / WIDTH)


def lanes(b):
    return pl.ds(b * LANES if isinstance(b, int) else pl.multiple_of(b * LANES, LANES), LANES)


def load_inputs(lengths, offsets, pool, gain1, r):
    slot_len = pool.shape[0] // N_DP
    rows = lax.broadcasted_iota(jnp.int32, (ROWS, LANES), 0)
    pick = jnp.zeros((ROWS, LANES), jnp.int32)
    behind = jnp.zeros((ROWS, LANES), jnp.int32)
    ahead = jnp.zeros((ROWS, LANES), jnp.int32)
    for s in range(N_DP):
        begin = offsets[s]
        end = begin + lengths[s]
        inside = (rows >= begin) & (rows < end)
        pick = jnp.where(inside, rows - begin + s * slot_len, pick)
        behind = jnp.where(inside, rows - begin, behind)
        ahead = jnp.where(inside, end - 1 - rows, ahead)
    r["behind"][...] = behind
    r["ahead"][...] = ahead
    lane = lax.broadcasted_iota(jnp.int32, (ROWS, LANES), 1)
    for t in range(pool.shape[0] // LANES):
        r["chosen"][:, lanes(t)] = (pick == lane + t * LANES).astype(F32).astype(BF)

    def gather(t, carry):
        cols = pl.ds(pl.multiple_of(t * TILE, TILE), TILE)
        r["unit_in"][:, cols] = dot(r["chosen"][...], pool[:, cols])
        return carry

    lax.fori_loop(0, WIDTH // TILE, gather, 0)

    def norm(i, carry):
        rows = pl.ds(pl.multiple_of(i * STEP, STEP), STEP)
        x = [r["unit_in"][rows, lanes(b)] for b in range(BLOCKS)]
        mean = row_mean(x)
        x = [v - mean for v in x]
        inverse = lax.rsqrt(row_mean([v * v for v in x]) + EPSILON)
        r["inv_in"][rows, :] = jnp.broadcast_to(inverse, (STEP, LANES))
        for b in range(BLOCKS):
            unit = x[b] * inverse
            r["unit_in"][rows, lanes(b)] = unit
            r["normed"][rows, lanes(b)] = (unit * gain1[lanes(b)].reshape(1, LANES)).astype(BF)
        return carry

    lax.fori_loop(0, ROWS // STEP, norm, 0)


def transpose_normed(r):
    for b in range(BLOCKS):
        r["normed_t"][lanes(b), :] = r["normed"][:, lanes(b)].T


def project(w, wait_tile, r):
    def tile(t, carry):
        wait_tile(t)
        cols = pl.ds(pl.multiple_of(t * TILE, TILE), TILE)
        gates = pl.ds(pl.multiple_of(t * TILE + WIDTH, TILE), TILE)
        linear = dot(r["normed"][...], w[:, cols])
        sig = sigmoid(dot(r["normed"][...], w[:, gates]))
        r["linear"][:, cols] = linear
        r["sig"][:, cols] = sig
        gated = (linear * sig).astype(BF).astype(F32)
        for j in range(TILE // LANES):
            r["gated"][t * (TILE // LANES) + j, PAD : PAD + ROWS, :] = gated[:, j * LANES : (j + 1) * LANES]
        return carry

    lax.fori_loop(0, WIDTH // TILE, tile, 0)


def tap_mask(behind, ahead, shift):
    return ahead >= shift if shift > 0 else behind >= -shift


def convolve(w_depth, r):
    def pair(c, carry):
        for g in range(ROWS // GROUP):
            begin = g * GROUP
            behind = r["behind"][begin : begin + GROUP, :]
            ahead = r["ahead"][begin : begin + GROUP, :]
            total = [jnp.zeros((GROUP, LANES), F32)] * 2
            for k in range(TAPS):
                shift = k - REACH
                same = tap_mask(behind, ahead, shift)
                for j in range(2):
                    b = c * 2 + j
                    x = r["gated"][b, PAD + begin + shift : PAD + begin + shift + GROUP, :]
                    if shift != 0:
                        x = jnp.where(same, x, 0.0)
                    total[j] = total[j] + x * w_depth[k : k + 1, lanes(b)]
            for j in range(2):
                r["conv"][c * 2 + j, PAD + begin : PAD + begin + GROUP, :] = total[j]
        return carry

    lax.fori_loop(0, BLOCKS // 2, pair, 0)


def finish_forward(gain2, cotangent, output, r):
    r["gain2_sum"][...] = jnp.zeros_like(r["gain2_sum"])

    def row_step(i, carry):
        rows = pl.ds(pl.multiple_of(i * STEP, STEP), STEP)
        held = pl.ds(pl.multiple_of(i * STEP + PAD, 16), STEP)
        x = [r["conv"][b, held, :] for b in range(BLOCKS)]
        mean = row_mean(x)
        x = [v - mean for v in x]
        inverse = lax.rsqrt(row_mean([v * v for v in x]) + EPSILON)
        units, grads = [], []
        for b in range(BLOCKS):
            unit = x[b] * inverse
            gain = gain2[lanes(b)].reshape(1, LANES)
            scaled = unit * gain
            sig = sigmoid(scaled)
            output[rows, lanes(b)] = (scaled * sig).astype(BF)
            grad = cotangent[rows, lanes(b)].astype(F32) * sig * (1.0 + scaled * (1.0 - sig))
            both = grad * unit
            r["gain2_sum"][b] = r["gain2_sum"][b] + fold(both)
            units.append(unit)
            grads.append(grad * gain)
        first = row_mean(grads)
        second = row_mean([q * u for q, u in zip(grads, units)])
        for b in range(BLOCKS):
            r["conv"][b, held, :] = inverse * (grads[b] - first - units[b] * second)
        return carry

    lax.fori_loop(0, ROWS // STEP, row_step, 0)


def back_convolve(chunk, w_depth, small, r):
    def pair(c, carry):
        first = chunk * (HALF // LANES) + c * 2
        r["tap_sum"][...] = jnp.zeros_like(r["tap_sum"])
        for g in range(ROWS // GROUP):
            begin = g * GROUP
            rows = slice(begin, begin + GROUP)
            behind = r["behind"][rows, :]
            ahead = r["ahead"][rows, :]
            total = [jnp.zeros((GROUP, LANES), F32)] * 2
            gated = [r["gated"][first + j, PAD + begin : PAD + begin + GROUP, :] for j in range(2)]
            for k in range(TAPS):
                shift = REACH - k
                same = tap_mask(behind, ahead, shift)
                for j in range(2):
                    x = r["conv"][first + j, PAD + begin + shift : PAD + begin + shift + GROUP, :]
                    if shift != 0:
                        x = jnp.where(same, x, 0.0)
                    total[j] = total[j] + x * w_depth[k : k + 1, lanes(first + j)]
                    product = x * gated[j]
                    r["tap_sum"][j, k] = r["tap_sum"][j, k] + fold(product)
            for j in range(2):
                at = pl.multiple_of((first + j) * LANES, LANES)
                linear = r["linear"][rows, pl.ds(at, LANES)]
                sig = r["sig"][rows, pl.ds(at, LANES)]
                grad = total[j] * sig
                r["grad_pre"][rows, pl.ds(at, LANES)] = grad.astype(BF)
                r["grad_pre"][rows, pl.ds(at + WIDTH, LANES)] = (grad * linear * (1.0 - sig)).astype(BF)
        for j in range(2):
            at = pl.multiple_of((first + j) * LANES, LANES)
            small[0:TAPS, pl.ds(at, LANES)] = jnp.sum(r["tap_sum"][j], axis=1)
        return carry

    lax.fori_loop(0, HALF // LANES // 2, pair, 0)


def weight_term(chunk, part, r):
    def tile(i, carry):
        rows = pl.ds(pl.multiple_of(i * 384, 384), 384)
        for h in range(2):
            cols = pl.ds(h * WIDTH + chunk * HALF, HALF)
            value = dot(r["normed_t"][rows, :], r["grad_pre"][:, cols]).astype(BF)
            for q in range(4):
                part[i // 2, (i % 2) * 2 + q // 2, q % 2, :, h * HALF : (h + 1) * HALF] = value[q * 96 : (q + 1) * 96]
        return carry

    lax.fori_loop(0, 4, tile, 0)


def back_project(w, r):
    def tile(t, carry):
        cols = pl.ds(pl.multiple_of(t * TILE, TILE), TILE)
        r["linear"][:, cols] = dot_t(r["grad_pre"][...], w[cols, :])
        return carry

    lax.fori_loop(0, WIDTH // TILE, tile, 0)


def finish_back(gain1, grad_input, small, r):
    r["gain1_sum"][...] = jnp.zeros_like(r["gain1_sum"])

    def row_step(i, carry):
        rows = pl.ds(pl.multiple_of(i * STEP, STEP), STEP)
        inverse = r["inv_in"][rows, :]
        units = [r["unit_in"][rows, lanes(b)] for b in range(BLOCKS)]
        grads = [r["linear"][rows, lanes(b)] for b in range(BLOCKS)]
        for b in range(BLOCKS):
            both = grads[b] * units[b]
            r["gain1_sum"][b] = r["gain1_sum"][b] + fold(both)
        grads = [grads[b] * gain1[lanes(b)].reshape(1, LANES) for b in range(BLOCKS)]
        first = row_mean(grads)
        second = row_mean([q * u for q, u in zip(grads, units)])
        for b in range(BLOCKS):
            grad_input[rows, lanes(b)] = (inverse * (grads[b] - first - units[b] * second)).astype(BF)
        return carry

    lax.fori_loop(0, ROWS // STEP, row_step, 0)
    for b in range(BLOCKS):
        small[TAPS : TAPS + 1, lanes(b)] = jnp.sum(r["gain1_sum"][b], axis=0, keepdims=True)
        small[TAPS + 1 : TAPS + 2, lanes(b)] = jnp.sum(r["gain2_sum"][b], axis=0, keepdims=True)
    small[TAPS + 2 : SMALL_ROWS, :] = jnp.zeros((SMALL_ROWS - TAPS - 2, WIDTH), F32)


WORK = (
    ("behind", (ROWS, LANES), jnp.int32),
    ("ahead", (ROWS, LANES), jnp.int32),
    ("chosen", (ROWS, 640), BF),
    ("unit_in", (ROWS, WIDTH), F32),
    ("inv_in", (ROWS, LANES), F32),
    ("normed", (ROWS, WIDTH), BF),
    ("normed_t", (WIDTH, ROWS), BF),
    ("linear", (ROWS, WIDTH), F32),
    ("sig", (ROWS, WIDTH), F32),
    ("gated", (BLOCKS, PAD + ROWS + PAD, LANES), F32),
    ("conv", (BLOCKS, PAD + ROWS + PAD, LANES), F32),
    ("gain1_sum", (BLOCKS, 8, LANES), F32),
    ("gain2_sum", (BLOCKS, 8, LANES), F32),
    ("tap_sum", (2, TAPS, 8, LANES), F32),
    ("grad_pre", (ROWS, 2 * WIDTH), BF),
)


def forward(lengths, offsets, pool, w_hbm, gain1, w_depth, gain2, cotangent, output, w, w_sems, r):
    def copy_w(t, h):
        cols = pl.ds(pl.multiple_of(t * TILE + h * WIDTH, TILE), TILE)
        return pltpu.make_async_copy(w_hbm.at[:, cols], w.at[:, cols], w_sems.at[h, t])

    for t in range(WIDTH // TILE):
        for h in range(2):
            copy_w(t, h).start()

    def wait_tile(t):
        for h in range(2):
            copy_w(t, h).wait()

    for name in ("gated", "conv"):
        r[name][:, 0:PAD, :] = jnp.zeros((BLOCKS, PAD, LANES), F32)
        r[name][:, PAD + ROWS :, :] = jnp.zeros((BLOCKS, PAD, LANES), F32)
    load_inputs(lengths, offsets, pool, gain1, r)
    project(w, wait_tile, r)
    convolve(w_depth, r)
    finish_forward(gain2, cotangent, output, r)
    transpose_normed(r)


def add_blocks(dst, src, count, cols):
    def step(i, carry):
        block, row = i // 2, pl.multiple_of((i % 2) * 48, 48)
        d, s = dst(block), src(block)
        value = d[pl.ds(row, 48), cols].astype(F32) + s[pl.ds(row, 48), :].astype(F32)
        d[pl.ds(row, 48), cols] = value.astype(BF)
        return carry

    lax.fori_loop(0, count * 2, step, 0)


X_FIRST = (False, True, False)


def module_kernel(
    lengths, offsets, pool, w_hbm, gain1, w_depth, gain2, cotangent,
    output, grad_input, out, small_out,
    w, w_sems, small, part, rx0, rx1, rx2, rx3, rx3_all, rx4, red, fin, rxs, rxd, small_fin,
    s0, r0, s1, r1, s2, r2, s3, r3, s4, r4, s5, r5, st1, rt1, st2, rt2, st3, rt3,
    *work
):
    r = {name: ref for (name, _, _), ref in zip(WORK, work)}
    p, g = lax.axis_index("dp"), lax.axis_index("shard")
    x_lo, y, core = g // 8, (g // 2) % 4, g % 2
    mates = (y + 1 - 2 * (y % 2), 3 - y)
    scale = 1.0 / (N_DP * N_SHARD)

    barrier = pltpu.get_barrier_semaphore()

    def greet(i, carry):
        signal(barrier, ((p + i) % N_DP, g))
        signal(barrier, (p, (g + i) % N_SHARD))
        return carry

    lax.fori_loop(1, 16, greet, 0)

    def core_copy(k):
        return remote(
            part.at[k, :, :, 1 - core], rx0.at[k], s0.at[k], r0.at[k], (p, shard_index(x_lo, y, 1 - core))
        )

    def finish_core(k):
        core_copy(k).wait_recv()
        add_blocks(
            lambda i: part.at[k, i // 4, i % 4, core], lambda i: rx0.at[k, i // 4, i % 4], 8, slice(None)
        )

    def cols(h):
        return pl.ds(HALF * h, HALF)

    def wide(k):
        return 1 if X_FIRST[k] else 2

    def first_x(k, i):
        return x_lo if X_FIRST[k] else i

    def y_block(k, block, h):
        if X_FIRST[k]:
            return part.at[k, pl.ds(x_lo, 1), block, core, :, cols(h)]
        return part.at[k, :, block, core, :, cols(h)]

    def y1_copy(k, h, j):
        q = mates[h]
        after = 3 - q if h == 0 else q + 1 - 2 * (q % 2)
        return remote(
            y_block(k, q if j == 0 else after, h), rx1.at[k, h, j, pl.ds(0, wide(k))],
            s1.at[k, h, j], r1.at[k, h, j], (p, shard_index(x_lo, q, core)),
        )

    def start_y1(k):
        for j in (1, 0):
            for h in range(2):
                y1_copy(k, h, j).start()

    def y2_copy(k, h):
        q = mates[1 - h]
        return remote(
            y_block(k, q, h), rx2.at[k, h, pl.ds(0, wide(k))], s2.at[k, h], r2.at[k, h],
            (p, shard_index(x_lo, q, core)),
        )

    def turn_y(k):
        for h in range(2):
            y1_copy(k, h, 1).wait_recv()
            add_blocks(
                lambda i: part.at[k, first_x(k, i), mates[1 - h], core],
                lambda i: rx1.at[k, h, 1, i], wide(k), cols(h),
            )
            y2_copy(k, h).start()
        for h in range(2):
            y1_copy(k, h, 0).wait_recv()
            add_blocks(
                lambda i: part.at[k, first_x(k, i), y, core], lambda i: rx1.at[k, h, 0, i], wide(k), cols(h)
            )

    def finish_y(k):
        for h in range(2):
            y2_copy(k, h).wait_recv()
            add_blocks(
                lambda i: part.at[k, first_x(k, i), y, core], lambda i: rx2.at[k, h, i], wide(k), cols(h)
            )

    def x_copy(k):
        peer = (p, shard_index(1 - x_lo, y, core))
        if X_FIRST[k]:
            return remote(part.at[k, 1 - x_lo, :, core], rx3_all, s3.at[k], r3.at[k], peer)
        return remote(part.at[k, 1 - x_lo, y, core], rx3.at[k], s3.at[k], r3.at[k], peer)

    def finish_x(k):
        x_copy(k).wait_recv()
        if X_FIRST[k]:
            add_blocks(lambda i: part.at[k, x_lo, i, core], lambda i: rx3_all.at[i], 4, slice(None))
        else:
            add_blocks(lambda i: part.at[k, x_lo, y, core], lambda i: rx3.at[k], 1, slice(None))

    def at_piece(ref, d, base):
        return ref.at[
            pl.ds(pl.multiple_of((d % 2) * 48, 48), 48), pl.ds(pl.multiple_of(base + (d // 2) * 128, 128), 128)
        ]

    def piece_copy(k, i):
        d = (p + i) % N_DP
        return remote(
            at_piece(part.at[k, x_lo, y, core], d, 0), rx4.at[k, i - 1], s4.at[k, i - 1], r4.at[k, i - 1], (d, g)
        )

    def sum_copy(k, i, sender):
        d = (p + i) % N_DP
        return remote(red.at[k], at_piece(fin, sender, CHUNK * k), s5.at[k, i - 1], r5.at[k, i - 1], (d, g))

    def each(count, do):
        def step(i, carry):
            do(i)
            return carry

        lax.fori_loop(1, count, step, 0)

    def start_pieces(k):
        each(N_DP, lambda i: piece_copy(k, i).start())

    def turn_pieces(k):
        each(N_DP, lambda i: piece_copy(k, i).wait_recv())
        total = at_piece(part.at[k, x_lo, y, core], p, 0)[...].astype(F32)
        for i in range(N_DP - 1):
            total = total + rx4[k, i].astype(F32)
        total = total.astype(BF)
        red[k] = total
        at_piece(fin, p, CHUNK * k)[...] = total
        each(N_DP, lambda i: sum_copy(k, i, p).start())

    def finish_pieces(k):
        each(N_DP, lambda i: sum_copy(k, i, (p + N_DP - i) % N_DP).wait_recv())

        def widen(i, carry):
            rows = pl.ds(pl.multiple_of(i * 48, 48), 48)
            for h in range(2):
                out[rows, pl.ds(h * WIDTH + HALF * k, HALF)] = (
                    fin[rows, pl.ds(CHUNK * k + HALF * h, HALF)].astype(F32) * scale
                )
            return carry

        lax.fori_loop(0, 2, widen, 0)

    def column(j):
        return pl.ds(pl.multiple_of(j * LANES, LANES), LANES)

    def small_copy(j):
        return remote(small.at[:, column(j)], rxs.at[g], st1.at[j], rt1.at[g], (p, j))

    def each_owner(do):
        def step(j, carry):
            @pl.when(j != g)
            def _():
                do(j)

            return carry

        lax.fori_loop(0, SMALL_OWNERS, step, 0)

    def small_sum_copy(i):
        return remote(rxd.at[p], rxd.at[p], st2.at[i - 1], rt2.at[p], ((p + i) % N_DP, g))

    def small_final_copy(i):
        return remote(
            small_fin.at[:, column(g)], small_fin.at[:, column(g)], st3.at[i - 1], rt3.at[g],
            (p, (g + i) % N_SHARD),
        )

    def add_small_shard():
        @pl.when(g < SMALL_OWNERS)
        def _():
            def take(i):
                s = (g + i) % N_SHARD
                remote(small.at[:, column(0)], rxs.at[s], st1.at[0], rt1.at[s], (p, s)).wait_recv()

            each(N_SHARD, take)
            rxs[g] = small[:, column(g)]
            total = rxs[0]
            for s in range(1, N_SHARD):
                total = total + rxs[s]
            rxd[p] = total
            each(N_DP, lambda i: small_sum_copy(i).start())

    def add_small_dp():
        @pl.when(g < SMALL_OWNERS)
        def _():
            def take(i):
                s = (p + i) % N_DP
                remote(rxd.at[s], rxd.at[s], st2.at[0], rt2.at[s], (s, g)).wait_recv()

            each(N_DP, take)
            total = rxd[0]
            for s in range(1, N_DP):
                total = total + rxd[s]
            small_fin[:, column(g)] = total
            each(N_SHARD, lambda i: small_final_copy(i).start())

    forward(lengths, offsets, pool, w_hbm, gain1, w_depth, gain2, cotangent, output, w, w_sems, r)
    pl.semaphore_wait(barrier, 30)
    for k in range(CHUNKS):
        back_convolve(k, w_depth, small, r)
        weight_term(k, part.at[k], r)
        core_copy(k).start()
        if k == 1:
            finish_core(0)
            start_y1(0)
    finish_core(1)
    x_copy(1).start()
    back_project(w, r)
    finish_core(2)
    start_y1(2)
    turn_y(0)
    finish_back(gain1, grad_input, small, r)
    each_owner(lambda j: small_copy(j).start())
    finish_y(0)
    x_copy(0).start()
    turn_y(2)
    finish_x(1)
    start_y1(1)
    finish_x(0)
    start_pieces(0)
    add_small_shard()
    finish_y(2)
    x_copy(2).start()
    turn_y(1)
    turn_pieces(0)
    finish_x(2)
    start_pieces(2)
    finish_y(1)
    start_pieces(1)
    add_small_dp()
    turn_pieces(2)
    turn_pieces(1)

    def take_final(j):
        remote(
            small_fin.at[:, column(j)], small_fin.at[:, column(j)], st3.at[0], rt3.at[j], (p, j)
        ).wait_recv()

    each_owner(take_final)
    small_out[...] = small_fin[...] * scale
    for k in (0, 2, 1):
        finish_pieces(k)

    for k in range(CHUNKS):
        core_copy(k).wait_send()
        x_copy(k).wait_send()
        for h in range(2):
            y1_copy(k, h, 0).wait_send()
            y1_copy(k, h, 1).wait_send()
            y2_copy(k, h).wait_send()

        def sent(i):
            piece_copy(k, i).wait_send()
            sum_copy(k, i, p).wait_send()

        each(N_DP, sent)
    each_owner(lambda j: small_copy(j).wait_send())

    @pl.when(g < SMALL_OWNERS)
    def _():
        def sent(i):
            small_sum_copy(i).wait_send()
            small_final_copy(i).wait_send()

        each(16, sent)


def module(lengths, offsets, pool, full, gain1, w_depth, gain2, cotangent):
    vmem = pl.BlockSpec(memory_space=pltpu.VMEM)
    smem = pl.BlockSpec(memory_space=pltpu.SMEM)
    block = WIDTH // N_SHARD
    dma = pltpu.SemaphoreType.DMA
    return pl.pallas_call(
        module_kernel,
        out_shape=(
            jax.ShapeDtypeStruct((ROWS, WIDTH), BF),
            jax.ShapeDtypeStruct((ROWS, WIDTH), BF),
            jax.ShapeDtypeStruct((block, 2 * WIDTH), F32),
            jax.ShapeDtypeStruct((SMALL_ROWS, WIDTH), F32),
        ),
        in_specs=[smem, smem, vmem, pl.BlockSpec(memory_space=pl.ANY), vmem, vmem, vmem, vmem],
        out_specs=(vmem,) * 4,
        scratch_shapes=[
            pltpu.VMEM((WIDTH, 2 * WIDTH), BF),
            dma((2, WIDTH // TILE)),
            pltpu.VMEM((SMALL_ROWS, WIDTH), F32),
            pltpu.VMEM((CHUNKS, 2, 4, 2, block, CHUNK), BF),
            pltpu.VMEM((CHUNKS, 2, 4, block, CHUNK), BF),
            pltpu.VMEM((CHUNKS, 2, 2, 2, block, HALF), BF),
            pltpu.VMEM((CHUNKS, 2, 2, block, HALF), BF),
            pltpu.VMEM((CHUNKS, block, CHUNK), BF),
            pltpu.VMEM((4, block, CHUNK), BF),
            pltpu.VMEM((CHUNKS, N_DP - 1, block // 2, 128), BF),
            pltpu.VMEM((CHUNKS, block // 2, 128), BF),
            pltpu.VMEM((block, 2 * WIDTH), BF),
            pltpu.VMEM((N_SHARD, SMALL_ROWS, 128), F32),
            pltpu.VMEM((N_DP, SMALL_ROWS, 128), F32),
            pltpu.VMEM((SMALL_ROWS, WIDTH), F32),
            dma((CHUNKS,)), dma((CHUNKS,)),
            dma((CHUNKS, 2, 2)), dma((CHUNKS, 2, 2)),
            dma((CHUNKS, 2)), dma((CHUNKS, 2)),
            dma((CHUNKS,)), dma((CHUNKS,)),
            dma((CHUNKS, N_DP - 1)), dma((CHUNKS, N_DP - 1)),
            dma((CHUNKS, N_DP - 1)), dma((CHUNKS, N_DP - 1)),
            dma((SMALL_OWNERS,)), dma((N_SHARD,)),
            dma((N_DP - 1,)), dma((N_DP,)),
            dma((N_SHARD - 1,)), dma((SMALL_OWNERS,)),
            *[pltpu.VMEM(shape, dtype) for _, shape, dtype in WORK],
        ],
        compiler_params=pltpu.CompilerParams(
            collective_id=1, has_side_effects=True, vmem_limit_bytes=60 * 1024 * 1024
        ),
        name="module",
    )(lengths, offsets, pool, full, gain1, w_depth, gain2, cotangent)


def body(frames, slot_dest, recv_length, recv_offset, gain1, w_in, w_depth, gain2, cotangent):
    model_width = frames.shape[2]
    taps = w_depth.shape[0]
    pool, full = exchange(frames, slot_dest, w_in)
    output, grad_input, grad_w, small_sum = module(
        recv_length, recv_offset, pool.reshape(-1, model_width), full.reshape(model_width, 2 * model_width),
        gain1, w_depth, gain2, cotangent,
    )
    return (output, grad_input, grad_w, small_sum[:taps], small_sum[taps], small_sum[taps + 1])


def solution(mesh):
    in_specs = (
        P(("dp", "shard"), None, None),
        P(("dp", "shard")),
        P(("dp", "shard")),
        P(("dp", "shard")),
        P(),
        P("shard", None),
        P(),
        P(),
        P(("dp", "shard"), None),
    )
    out_specs = (
        P(("dp", "shard"), None),
        P(("dp", "shard"), None),
        P("shard", None),
        P(),
        P(),
        P(),
    )
    return jax.shard_map(body, mesh=mesh, in_specs=in_specs, out_specs=out_specs, check_vma=False)
```

```python
import jax
import jax.numpy as jnp
from jax import lax
from jax.experimental import pallas as pl
from jax.experimental.pallas import tpu as pltpu
from jax.sharding import PartitionSpec as P

EPSILON = 1e-05
MESH = pl.DeviceIdType.MESH
BF = jnp.bfloat16
F32 = jnp.float32

N_DP = 16
N_SHARD = 16
SMALL_ROWS = 40
SMALL_OWNERS = 12
CHUNKS = 3
CHUNK = 1024
HALF = CHUNK // 2


def shard_index(x_lo, y, core):
    return x_lo * 8 + y * 2 + core


def signal(sem, device):
    pl.semaphore_signal(sem, inc=1, device_id=device, device_id_type=MESH)


def remote(src, dst, send, recv, device):
    return pltpu.make_async_remote_copy(
        src_ref=src, dst_ref=dst, send_sem=send, recv_sem=recv, device_id=device, device_id_type=MESH
    )


def source_of(slot_dest, d):
    index = jnp.int32(0)
    for j in range(N_DP):
        index = index + jnp.where(slot_dest[j] == d, j, 0)
    return jnp.minimum(index, N_DP - 1)


def exchange(frames, slot_dest, w_own, pool, w, outgoing, own_sem, a2a_send, a2a_recv, w_send, w_recv, between):
    p, g = lax.axis_index("dp"), lax.axis_index("shard")
    x_lo, y, core = g // 8, (g // 2) % 4, g % 2
    up, down, across = (y + 1) % 4, (y + 3) % 4, (y + 2) % 4
    g_x = shard_index(1 - x_lo, y, core)
    g_up = shard_index(x_lo, up, core)
    g_down = shard_index(x_lo, down, core)
    g_core = shard_index(x_lo, y, 1 - core)
    depth = w_own.shape[0]

    def rows(block):
        return w.at[pl.ds(pl.multiple_of(block * depth, depth), depth), :]

    def send(block, peer, slot, src=None):
        return remote(
            rows(block) if src is None else src, rows(block), w_send.at[slot], w_recv.at[slot], (p, peer)
        )

    sent = []

    def go(copy):
        copy.start()
        sent.append(copy)

    go(send(g, g_up, 1, w_own))
    go(send(g, g_down, 2, w_own))
    go(send(g, g_x, 0, w_own))

    def post(i, carry):
        d = (p + i + 6) % N_DP
        j = jnp.where(i + 6 < N_DP, i + 6, i + 6 - N_DP)
        outgoing[j] = frames[source_of(slot_dest, d)]
        remote(outgoing.at[j], pool.at[p], a2a_send.at[j], a2a_recv.at[j], (d, g)).start()
        return carry

    lax.fori_loop(0, N_DP - 6, post, 0)
    lax.fori_loop(N_DP - 5, N_DP, post, 0)
    go(send(g, g_core, 7, w_own))
    own_w = pltpu.make_async_copy(w_own, rows(g), own_sem)
    own_w.start()
    pool[p] = frames[source_of(slot_dest, p)]
    between()

    def arrived(block, slot):
        remote(rows(block), rows(block), w_send.at[slot], w_recv.at[slot], (p, g_x)).wait_recv()

    arrived(g_x, 0)
    go(send(g_x, g_up, 3))
    go(send(g_x, g_down, 4))
    go(send(g_x, g_core, 8))
    b = shard_index(x_lo, down, core)
    arrived(b, 1)
    go(send(b, g_up, 5))
    go(send(b, g_core, 9))
    b = shard_index(x_lo, up, core)
    arrived(b, 2)
    go(send(b, g_core, 10))
    b = shard_index(1 - x_lo, up, core)
    arrived(b, 4)
    go(send(b, g_down, 6))
    go(send(b, g_core, 11))
    b = shard_index(1 - x_lo, down, core)
    arrived(b, 3)
    go(send(b, g_core, 12))
    b = shard_index(x_lo, across, core)
    arrived(b, 5)
    go(send(b, g_core, 13))
    b = shard_index(1 - x_lo, across, core)
    arrived(b, 6)
    go(send(b, g_core, 14))

    def collect(i, carry):
        s = (p + N_DP - i) % N_DP
        copy = remote(outgoing.at[i], pool.at[s], a2a_send.at[i], a2a_recv.at[i], (s, g))
        copy.wait_recv()
        return carry

    lax.fori_loop(1, N_DP, collect, 0)

    def finish_weight():
        other = 1 - core
        theirs = [
            (x_lo, y, 7), (1 - x_lo, y, 8), (x_lo, down, 9), (x_lo, up, 10),
            (1 - x_lo, up, 11), (1 - x_lo, down, 12), (x_lo, across, 13), (1 - x_lo, across, 14),
        ]
        for bx, by, slot in theirs:
            arrived(shard_index(bx, by, other), slot)
        own_w.wait()

    def finish_sends():
        def collect_sent(i, carry):
            remote(outgoing.at[i], pool.at[p], a2a_send.at[i], a2a_recv.at[i], (p, g_x)).wait_send()
            return carry

        lax.fori_loop(1, N_DP, collect_sent, 0)
        for copy in sent:
            copy.wait_send()

    return finish_weight, finish_sends


ROWS = 384
WIDTH = 1536
TAPS = 31
REACH = 15
PAD = 16
LANES = 128
BLOCKS = WIDTH // LANES
TILE = 256
GROUP = 48
STEP = 32
SLOT = 40


def sigmoid(v):
    return 1.0 / (1.0 + jnp.exp(-v))


def dot(a, b):
    return lax.dot_general(a, b, (((1,), (0,)), ((), ())), preferred_element_type=F32)


def dot_t(a, b):
    return lax.dot_general(a, b, (((1,), (1,)), ((), ())), preferred_element_type=F32)


def fold(v):
    total = v[0:8]
    for q in range(1, v.shape[0] // 8):
        total = total + v[q * 8 : (q + 1) * 8]
    return total


def row_mean(blocks):
    total = blocks[0]
    for b in blocks[1:]:
        total = total + b
    return jnp.sum(total, axis=1, keepdims=True) * (1.0 / WIDTH)


def lanes(b):
    return pl.ds(b * LANES if isinstance(b, int) else pl.multiple_of(b * LANES, LANES), LANES)


def find_rows(lengths, offsets, r):
    slot_len = SLOT
    rows = lax.broadcasted_iota(jnp.int32, (ROWS, LANES), 0)
    pick = jnp.zeros((ROWS, LANES), jnp.int32)
    behind = jnp.zeros((ROWS, LANES), jnp.int32)
    ahead = jnp.zeros((ROWS, LANES), jnp.int32)
    for s in range(N_DP):
        begin = offsets[s]
        end = begin + lengths[s]
        inside = (rows >= begin) & (rows < end)
        pick = jnp.where(inside, rows - begin + s * slot_len, pick)
        behind = jnp.where(inside, rows - begin, behind)
        ahead = jnp.where(inside, end - 1 - rows, ahead)
    r["behind"][...] = behind
    r["ahead"][...] = ahead
    lane = lax.broadcasted_iota(jnp.int32, (ROWS, LANES), 1)
    for t in range(N_DP * SLOT // LANES):
        r["chosen"][:, lanes(t)] = (pick == lane + t * LANES).astype(F32).astype(BF)


def load_inputs(pool, gain1, r):
    def gather(t, carry):
        cols = pl.ds(pl.multiple_of(t * TILE, TILE), TILE)
        r["unit_in"][:, cols] = dot(r["chosen"][...], pool[:, cols])
        return carry

    lax.fori_loop(0, WIDTH // TILE, gather, 0)

    def norm(i, carry):
        rows = pl.ds(pl.multiple_of(i * STEP, STEP), STEP)
        x = [r["unit_in"][rows, lanes(b)] for b in range(BLOCKS)]
        mean = row_mean(x)
        x = [v - mean for v in x]
        inverse = lax.rsqrt(row_mean([v * v for v in x]) + EPSILON)
        r["inv_in"][rows, :] = jnp.broadcast_to(inverse, (STEP, LANES))
        for b in range(BLOCKS):
            unit = x[b] * inverse
            r["unit_in"][rows, lanes(b)] = unit
            r["normed"][rows, lanes(b)] = (unit * gain1[lanes(b)].reshape(1, LANES)).astype(BF)
        return carry

    lax.fori_loop(0, ROWS // STEP, norm, 0)


def transpose_normed(r):
    for b in range(BLOCKS):
        r["normed_t"][lanes(b), :] = r["normed"][:, lanes(b)].T


def project(w, r):
    def tile(t, carry):
        cols = pl.ds(pl.multiple_of(t * TILE, TILE), TILE)
        gates = pl.ds(pl.multiple_of(t * TILE + WIDTH, TILE), TILE)
        linear = dot(r["normed"][...], w[:, cols])
        sig = sigmoid(dot(r["normed"][...], w[:, gates]))
        r["linear"][:, cols] = linear
        r["sig"][:, cols] = sig
        gated = (linear * sig).astype(BF).astype(F32)
        for j in range(TILE // LANES):
            r["gated"][t * (TILE // LANES) + j, PAD : PAD + ROWS, :] = gated[:, j * LANES : (j + 1) * LANES]
        return carry

    lax.fori_loop(0, WIDTH // TILE, tile, 0)


def tap_mask(behind, ahead, shift):
    return ahead >= shift if shift > 0 else behind >= -shift


def convolve(w_depth, r):
    def pair(c, carry):
        for g in range(ROWS // GROUP):
            begin = g * GROUP
            behind = r["behind"][begin : begin + GROUP, :]
            ahead = r["ahead"][begin : begin + GROUP, :]
            total = [jnp.zeros((GROUP, LANES), F32)] * 2
            for k in range(TAPS):
                shift = k - REACH
                same = tap_mask(behind, ahead, shift)
                for j in range(2):
                    b = c * 2 + j
                    x = r["gated"][b, PAD + begin + shift : PAD + begin + shift + GROUP, :]
                    if shift != 0:
                        x = jnp.where(same, x, 0.0)
                    total[j] = total[j] + x * w_depth[k : k + 1, lanes(b)]
            for j in range(2):
                r["conv"][c * 2 + j, PAD + begin : PAD + begin + GROUP, :] = total[j]
        return carry

    lax.fori_loop(0, BLOCKS // 2, pair, 0)


def finish_forward(gain2, cotangent, output, r):
    r["gain2_sum"][...] = jnp.zeros_like(r["gain2_sum"])

    def row_step(i, carry):
        rows = pl.ds(pl.multiple_of(i * STEP, STEP), STEP)
        held = pl.ds(pl.multiple_of(i * STEP + PAD, 16), STEP)
        x = [r["conv"][b, held, :] for b in range(BLOCKS)]
        mean = row_mean(x)
        x = [v - mean for v in x]
        inverse = lax.rsqrt(row_mean([v * v for v in x]) + EPSILON)
        units, grads = [], []
        for b in range(BLOCKS):
            unit = x[b] * inverse
            gain = gain2[lanes(b)].reshape(1, LANES)
            scaled = unit * gain
            sig = sigmoid(scaled)
            output[rows, lanes(b)] = (scaled * sig).astype(BF)
            grad = cotangent[rows, lanes(b)].astype(F32) * sig * (1.0 + scaled * (1.0 - sig))
            both = grad * unit
            r["gain2_sum"][b] = r["gain2_sum"][b] + fold(both)
            units.append(unit)
            grads.append(grad * gain)
        first = row_mean(grads)
        second = row_mean([q * u for q, u in zip(grads, units)])
        for b in range(BLOCKS):
            r["conv"][b, held, :] = inverse * (grads[b] - first - units[b] * second)
        return carry

    lax.fori_loop(0, ROWS // STEP, row_step, 0)


def back_convolve(chunk, w_depth, small, r):
    def pair(c, carry):
        first = chunk * (HALF // LANES) + c * 2
        r["tap_sum"][...] = jnp.zeros_like(r["tap_sum"])
        for g in range(ROWS // GROUP):
            begin = g * GROUP
            rows = slice(begin, begin + GROUP)
            behind = r["behind"][rows, :]
            ahead = r["ahead"][rows, :]
            total = [jnp.zeros((GROUP, LANES), F32)] * 2
            gated = [r["gated"][first + j, PAD + begin : PAD + begin + GROUP, :] for j in range(2)]
            for k in range(TAPS):
                shift = REACH - k
                same = tap_mask(behind, ahead, shift)
                for j in range(2):
                    x = r["conv"][first + j, PAD + begin + shift : PAD + begin + shift + GROUP, :]
                    if shift != 0:
                        x = jnp.where(same, x, 0.0)
                    total[j] = total[j] + x * w_depth[k : k + 1, lanes(first + j)]
                    product = x * gated[j]
                    r["tap_sum"][j, k] = r["tap_sum"][j, k] + fold(product)
            for j in range(2):
                at = pl.multiple_of((first + j) * LANES, LANES)
                linear = r["linear"][rows, pl.ds(at, LANES)]
                sig = r["sig"][rows, pl.ds(at, LANES)]
                grad = total[j] * sig
                r["grad_pre"][rows, pl.ds(at, LANES)] = grad.astype(BF)
                r["grad_pre"][rows, pl.ds(at + WIDTH, LANES)] = (grad * linear * (1.0 - sig)).astype(BF)
        for j in range(2):
            at = pl.multiple_of((first + j) * LANES, LANES)
            small[0:TAPS, pl.ds(at, LANES)] = jnp.sum(r["tap_sum"][j], axis=1)
        return carry

    lax.fori_loop(0, HALF // LANES // 2, pair, 0)


def weight_term(chunk, part, r):
    def tile(i, carry):
        rows = pl.ds(pl.multiple_of(i * 384, 384), 384)
        for h in range(2):
            cols = pl.ds(h * WIDTH + chunk * HALF, HALF)
            value = dot(r["normed_t"][rows, :], r["grad_pre"][:, cols]).astype(BF)
            for q in range(4):
                part[i // 2, (i % 2) * 2 + q // 2, q % 2, :, h * HALF : (h + 1) * HALF] = value[q * 96 : (q + 1) * 96]
        return carry

    lax.fori_loop(0, 4, tile, 0)


def back_project(w, r):
    def tile(t, carry):
        cols = pl.ds(pl.multiple_of(t * TILE, TILE), TILE)
        r["linear"][:, cols] = dot_t(r["grad_pre"][...], w[cols, :])
        return carry

    lax.fori_loop(0, WIDTH // TILE, tile, 0)


def finish_back(gain1, grad_input, small, r):
    r["gain1_sum"][...] = jnp.zeros_like(r["gain1_sum"])

    def row_step(i, carry):
        rows = pl.ds(pl.multiple_of(i * STEP, STEP), STEP)
        inverse = r["inv_in"][rows, :]
        units = [r["unit_in"][rows, lanes(b)] for b in range(BLOCKS)]
        grads = [r["linear"][rows, lanes(b)] for b in range(BLOCKS)]
        for b in range(BLOCKS):
            both = grads[b] * units[b]
            r["gain1_sum"][b] = r["gain1_sum"][b] + fold(both)
        grads = [grads[b] * gain1[lanes(b)].reshape(1, LANES) for b in range(BLOCKS)]
        first = row_mean(grads)
        second = row_mean([q * u for q, u in zip(grads, units)])
        for b in range(BLOCKS):
            grad_input[rows, lanes(b)] = (inverse * (grads[b] - first - units[b] * second)).astype(BF)
        return carry

    lax.fori_loop(0, ROWS // STEP, row_step, 0)
    for b in range(BLOCKS):
        small[TAPS : TAPS + 1, lanes(b)] = jnp.sum(r["gain1_sum"][b], axis=0, keepdims=True)
        small[TAPS + 1 : TAPS + 2, lanes(b)] = jnp.sum(r["gain2_sum"][b], axis=0, keepdims=True)
    small[TAPS + 2 : SMALL_ROWS, :] = jnp.zeros((SMALL_ROWS - TAPS - 2, WIDTH), F32)


WORK = (
    ("behind", (ROWS, LANES), jnp.int32),
    ("ahead", (ROWS, LANES), jnp.int32),
    ("chosen", (ROWS, N_DP * SLOT), BF),
    ("unit_in", (ROWS, WIDTH), F32),
    ("inv_in", (ROWS, LANES), F32),
    ("normed", (ROWS, WIDTH), BF),
    ("normed_t", (WIDTH, ROWS), BF),
    ("linear", (ROWS, WIDTH), F32),
    ("sig", (ROWS, WIDTH), F32),
    ("gated", (BLOCKS, PAD + ROWS + PAD, LANES), F32),
    ("conv", (BLOCKS, PAD + ROWS + PAD, LANES), F32),
    ("gain1_sum", (BLOCKS, 8, LANES), F32),
    ("gain2_sum", (BLOCKS, 8, LANES), F32),
    ("tap_sum", (2, TAPS, 8, LANES), F32),
    ("grad_pre", (ROWS, 2 * WIDTH), BF),
)


def add_blocks(dst, src, count, cols):
    def step(i, carry):
        block, row = i // 2, pl.multiple_of((i % 2) * 48, 48)
        d, s = dst(block), src(block)
        value = d[pl.ds(row, 48), cols].astype(F32) + s[pl.ds(row, 48), :].astype(F32)
        d[pl.ds(row, 48), cols] = value.astype(BF)
        return carry

    lax.fori_loop(0, count * 2, step, 0)


X_FIRST = (False, True, False)


def module_kernel(
    frames, slot_dest, lengths, offsets, gain1, w_own, w_depth, gain2, cotangent,
    output, grad_input, out, depth_out, gain1_out, gain2_out,
    arriving, pool, w, outgoing, own_sem, a2a_send, a2a_recv, w_send, w_recv, small, part, rx0, rx1, rx2, rx3, rx3_all, rx4, red, fin, rxs, rxd, small_fin,
    s0, r0, s1, r1, s2, r2, s3, r3, s4, r4, s5, r5, st1, rt1, st2, rt2, st3, rt3,
    *work
):
    r = {name: ref for (name, _, _), ref in zip(WORK, work)}
    p, g = lax.axis_index("dp"), lax.axis_index("shard")
    x_lo, y, core = g // 8, (g // 2) % 4, g % 2
    mates = (y + 1 - 2 * (y % 2), 3 - y)
    scale = 1.0 / (N_DP * N_SHARD)

    barrier = pltpu.get_barrier_semaphore()

    def greet(i, carry):
        signal(barrier, ((p + i) % N_DP, g))
        signal(barrier, (p, (g + i) % N_SHARD))
        return carry

    lax.fori_loop(1, 16, greet, 0)

    def core_copy(k):
        return remote(
            part.at[k, :, :, 1 - core], rx0.at[k], s0.at[k], r0.at[k], (p, shard_index(x_lo, y, 1 - core))
        )

    def finish_core(k):
        core_copy(k).wait_recv()
        add_blocks(
            lambda i: part.at[k, i // 4, i % 4, core], lambda i: rx0.at[k, i // 4, i % 4], 8, slice(None)
        )

    def cols(h):
        return pl.ds(HALF * h, HALF)

    def wide(k):
        return 1 if X_FIRST[k] else 2

    def first_x(k, i):
        return x_lo if X_FIRST[k] else i

    def y_block(k, block, h):
        if X_FIRST[k]:
            return part.at[k, pl.ds(x_lo, 1), block, core, :, cols(h)]
        return part.at[k, :, block, core, :, cols(h)]

    def y1_copy(k, h, j):
        q = mates[h]
        after = 3 - q if h == 0 else q + 1 - 2 * (q % 2)
        return remote(
            y_block(k, q if j == 0 else after, h), rx1.at[k, h, j, pl.ds(0, wide(k))],
            s1.at[k, h, j], r1.at[k, h, j], (p, shard_index(x_lo, q, core)),
        )

    def start_y1(k):
        for j in (1, 0):
            for h in range(2):
                y1_copy(k, h, j).start()

    def y2_copy(k, h):
        q = mates[1 - h]
        return remote(
            y_block(k, q, h), rx2.at[k, h, pl.ds(0, wide(k))], s2.at[k, h], r2.at[k, h],
            (p, shard_index(x_lo, q, core)),
        )

    def turn_y(k):
        for h in range(2):
            y1_copy(k, h, 1).wait_recv()
            add_blocks(
                lambda i: part.at[k, first_x(k, i), mates[1 - h], core],
                lambda i: rx1.at[k, h, 1, i], wide(k), cols(h),
            )
            y2_copy(k, h).start()
        for h in range(2):
            y1_copy(k, h, 0).wait_recv()
            add_blocks(
                lambda i: part.at[k, first_x(k, i), y, core], lambda i: rx1.at[k, h, 0, i], wide(k), cols(h)
            )

    def finish_y(k):
        for h in range(2):
            y2_copy(k, h).wait_recv()
            add_blocks(
                lambda i: part.at[k, first_x(k, i), y, core], lambda i: rx2.at[k, h, i], wide(k), cols(h)
            )

    def x_copy(k):
        peer = (p, shard_index(1 - x_lo, y, core))
        if X_FIRST[k]:
            return remote(part.at[k, 1 - x_lo, :, core], rx3_all, s3.at[k], r3.at[k], peer)
        return remote(part.at[k, 1 - x_lo, y, core], rx3.at[k], s3.at[k], r3.at[k], peer)

    def finish_x(k):
        x_copy(k).wait_recv()
        if X_FIRST[k]:
            add_blocks(lambda i: part.at[k, x_lo, i, core], lambda i: rx3_all.at[i], 4, slice(None))
        else:
            add_blocks(lambda i: part.at[k, x_lo, y, core], lambda i: rx3.at[k], 1, slice(None))

    def at_piece(ref, d, base):
        return ref.at[
            pl.ds(pl.multiple_of((d % 2) * 48, 48), 48), pl.ds(pl.multiple_of(base + (d // 2) * 128, 128), 128)
        ]

    def piece_copy(k, i):
        d = (p + i) % N_DP
        return remote(
            at_piece(part.at[k, x_lo, y, core], d, 0), rx4.at[k, i - 1], s4.at[k, i - 1], r4.at[k, i - 1], (d, g)
        )

    def sum_copy(k, i, sender):
        d = (p + i) % N_DP
        return remote(red.at[k], at_piece(fin, sender, CHUNK * k), s5.at[k, i - 1], r5.at[k, i - 1], (d, g))

    def each(count, do):
        def step(i, carry):
            do(i)
            return carry

        lax.fori_loop(1, count, step, 0)

    def start_pieces(k):
        each(N_DP, lambda i: piece_copy(k, i).start())

    def turn_pieces(k):
        each(N_DP, lambda i: piece_copy(k, i).wait_recv())
        total = at_piece(part.at[k, x_lo, y, core], p, 0)[...].astype(F32)
        for i in range(N_DP - 1):
            total = total + rx4[k, i].astype(F32)
        total = total.astype(BF)
        red[k] = total
        at_piece(fin, p, CHUNK * k)[...] = total
        each(N_DP, lambda i: sum_copy(k, i, p).start())

    def finish_pieces(k):
        each(N_DP, lambda i: sum_copy(k, i, (p + N_DP - i) % N_DP).wait_recv())

        def widen(i, carry):
            rows = pl.ds(pl.multiple_of(i * 48, 48), 48)
            for h in range(2):
                out[rows, pl.ds(h * WIDTH + HALF * k, HALF)] = (
                    fin[rows, pl.ds(CHUNK * k + HALF * h, HALF)].astype(F32) * scale
                )
            return carry

        lax.fori_loop(0, 2, widen, 0)

    def column(j):
        return pl.ds(pl.multiple_of(j * LANES, LANES), LANES)

    def small_copy(j):
        return remote(small.at[:, column(j)], rxs.at[g], st1.at[j], rt1.at[g], (p, j))

    def each_owner(do):
        def step(j, carry):
            @pl.when(j != g)
            def _():
                do(j)

            return carry

        lax.fori_loop(0, SMALL_OWNERS, step, 0)

    def small_sum_copy(i):
        return remote(rxd.at[p], rxd.at[p], st2.at[i - 1], rt2.at[p], ((p + i) % N_DP, g))

    def small_final_copy(i):
        return remote(
            small_fin.at[:, column(g)], small_fin.at[:, column(g)], st3.at[i - 1], rt3.at[g],
            (p, (g + i) % N_SHARD),
        )

    def add_small_shard():
        @pl.when(g < SMALL_OWNERS)
        def _():
            def take(i):
                s = (g + i) % N_SHARD
                remote(small.at[:, column(0)], rxs.at[s], st1.at[0], rt1.at[s], (p, s)).wait_recv()

            each(N_SHARD, take)
            rxs[g] = small[:, column(g)]
            total = rxs[0]
            for s in range(1, N_SHARD):
                total = total + rxs[s]
            rxd[p] = total
            each(N_DP, lambda i: small_sum_copy(i).start())

    def add_small_dp():
        @pl.when(g < SMALL_OWNERS)
        def _():
            def take(i):
                s = (p + i) % N_DP
                remote(rxd.at[s], rxd.at[s], st2.at[0], rt2.at[s], (s, g)).wait_recv()

            each(N_DP, take)
            total = rxd[0]
            for s in range(1, N_DP):
                total = total + rxd[s]
            small_fin[:, column(g)] = total
            each(N_SHARD, lambda i: small_final_copy(i).start())

    pl.semaphore_wait(barrier, 30)

    def between():
        for name in ("gated", "conv"):
            r[name][:, 0:PAD, :] = jnp.zeros((BLOCKS, PAD, LANES), F32)
            r[name][:, PAD + ROWS :, :] = jnp.zeros((BLOCKS, PAD, LANES), F32)
        find_rows(lengths, offsets, r)

    finish_weight, finish_sends = exchange(
        frames, slot_dest, w_own, arriving, w, outgoing, own_sem, a2a_send, a2a_recv, w_send, w_recv, between
    )
    for s in range(N_DP):
        pool[s * SLOT : (s + 1) * SLOT, :] = arriving[s]
    load_inputs(pool, gain1, r)
    finish_weight()
    project(w, r)
    convolve(w_depth, r)
    finish_forward(gain2, cotangent, output, r)
    transpose_normed(r)
    for k in range(CHUNKS):
        back_convolve(k, w_depth, small, r)
        weight_term(k, part.at[k], r)
        core_copy(k).start()
        if k == 1:
            finish_core(0)
            start_y1(0)
    finish_core(1)
    x_copy(1).start()
    back_project(w, r)
    finish_core(2)
    start_y1(2)
    turn_y(0)
    finish_back(gain1, grad_input, small, r)
    each_owner(lambda j: small_copy(j).start())
    finish_y(0)
    x_copy(0).start()
    turn_y(2)
    finish_x(1)
    start_y1(1)
    finish_x(0)
    start_pieces(0)
    finish_y(2)
    x_copy(2).start()
    add_small_shard()
    turn_y(1)
    turn_pieces(0)
    finish_x(2)
    start_pieces(2)
    finish_y(1)
    start_pieces(1)
    add_small_dp()
    turn_pieces(2)
    turn_pieces(1)
    finish_pieces(0)

    def take_final(j):
        remote(
            small_fin.at[:, column(j)], small_fin.at[:, column(j)], st3.at[0], rt3.at[j], (p, j)
        ).wait_recv()

    each_owner(take_final)
    depth_out[...] = small_fin[0:TAPS, :] * scale
    for b in range(BLOCKS):
        gain1_out[lanes(b)] = small_fin[TAPS, lanes(b)] * scale
        gain2_out[lanes(b)] = small_fin[TAPS + 1, lanes(b)] * scale
    finish_sends()
    finish_pieces(2)
    finish_pieces(1)

    for k in range(CHUNKS):
        core_copy(k).wait_send()
        x_copy(k).wait_send()
        for h in range(2):
            y1_copy(k, h, 0).wait_send()
            y1_copy(k, h, 1).wait_send()
            y2_copy(k, h).wait_send()

        def sent(i):
            piece_copy(k, i).wait_send()
            sum_copy(k, i, p).wait_send()

        each(N_DP, sent)
    each_owner(lambda j: small_copy(j).wait_send())

    @pl.when(g < SMALL_OWNERS)
    def _():
        def sent(i):
            small_sum_copy(i).wait_send()
            small_final_copy(i).wait_send()

        each(16, sent)


def module(frames, slot_dest, lengths, offsets, gain1, w_in, w_depth, gain2, cotangent):
    vmem = pl.BlockSpec(memory_space=pltpu.VMEM)
    smem = pl.BlockSpec(memory_space=pltpu.SMEM)
    block = WIDTH // N_SHARD
    dma = pltpu.SemaphoreType.DMA
    return pl.pallas_call(
        module_kernel,
        out_shape=(
            jax.ShapeDtypeStruct((ROWS, WIDTH), BF),
            jax.ShapeDtypeStruct((ROWS, WIDTH), BF),
            jax.ShapeDtypeStruct((block, 2 * WIDTH), F32),
            jax.ShapeDtypeStruct((TAPS, WIDTH), F32),
            jax.ShapeDtypeStruct((WIDTH,), F32),
            jax.ShapeDtypeStruct((WIDTH,), F32),
        ),
        in_specs=[vmem, smem, smem, smem, vmem, pl.BlockSpec(memory_space=pl.ANY), vmem, vmem, vmem],
        out_specs=(vmem,) * 6,
        scratch_shapes=[
            pltpu.VMEM((N_DP, SLOT, WIDTH), BF),
            pltpu.VMEM((N_DP * SLOT, WIDTH), BF),
            pltpu.VMEM((WIDTH, 2 * WIDTH), BF),
            pltpu.VMEM((N_DP, SLOT, WIDTH), BF),
            dma,
            dma((N_DP,)), dma((N_DP,)),
            dma((15,)), dma((15,)),
            pltpu.VMEM((SMALL_ROWS, WIDTH), F32),
            pltpu.VMEM((CHUNKS, 2, 4, 2, block, CHUNK), BF),
            pltpu.VMEM((CHUNKS, 2, 4, block, CHUNK), BF),
            pltpu.VMEM((CHUNKS, 2, 2, 2, block, HALF), BF),
            pltpu.VMEM((CHUNKS, 2, 2, block, HALF), BF),
            pltpu.VMEM((CHUNKS, block, CHUNK), BF),
            pltpu.VMEM((4, block, CHUNK), BF),
            pltpu.VMEM((CHUNKS, N_DP - 1, block // 2, 128), BF),
            pltpu.VMEM((CHUNKS, block // 2, 128), BF),
            pltpu.VMEM((block, 2 * WIDTH), BF),
            pltpu.VMEM((N_SHARD, SMALL_ROWS, 128), F32),
            pltpu.VMEM((N_DP, SMALL_ROWS, 128), F32),
            pltpu.VMEM((SMALL_ROWS, WIDTH), F32),
            dma((CHUNKS,)), dma((CHUNKS,)),
            dma((CHUNKS, 2, 2)), dma((CHUNKS, 2, 2)),
            dma((CHUNKS, 2)), dma((CHUNKS, 2)),
            dma((CHUNKS,)), dma((CHUNKS,)),
            dma((CHUNKS, N_DP - 1)), dma((CHUNKS, N_DP - 1)),
            dma((CHUNKS, N_DP - 1)), dma((CHUNKS, N_DP - 1)),
            dma((SMALL_OWNERS,)), dma((N_SHARD,)),
            dma((N_DP - 1,)), dma((N_DP,)),
            dma((N_SHARD - 1,)), dma((SMALL_OWNERS,)),
            *[pltpu.VMEM(shape, dtype) for _, shape, dtype in WORK],
        ],
        compiler_params=pltpu.CompilerParams(
            collective_id=0, has_side_effects=True, vmem_limit_bytes=64 * 1024 * 1024 - 65536
        ),
        name="module",
    )(frames, slot_dest, lengths, offsets, gain1, w_in, w_depth, gain2, cotangent)


def body(frames, slot_dest, recv_length, recv_offset, gain1, w_in, w_depth, gain2, cotangent):
    return module(frames, slot_dest, recv_length, recv_offset, gain1, w_in, w_depth, gain2, cotangent)


def solution(mesh):
    in_specs = (
        P(("dp", "shard"), None, None),
        P(("dp", "shard")),
        P(("dp", "shard")),
        P(("dp", "shard")),
        P(),
        P("shard", None),
        P(),
        P(),
        P(("dp", "shard"), None),
    )
    out_specs = (
        P(("dp", "shard"), None),
        P(("dp", "shard"), None),
        P("shard", None),
        P(),
        P(),
        P(),
    )
    return jax.shard_map(body, mesh=mesh, in_specs=in_specs, out_specs=out_specs, check_vma=False)
```

```python
import jax
import jax.numpy as jnp
from jax import lax
from jax.experimental import pallas as pl
from jax.experimental.pallas import tpu as pltpu
from jax.sharding import PartitionSpec as P

EPSILON = 1e-05
MESH = pl.DeviceIdType.MESH
BF = jnp.bfloat16
F32 = jnp.float32

N_DP = 16
N_SHARD = 16
SMALL_ROWS = 40
SMALL_OWNERS = 12
CHUNKS = 3
CHUNK = 1024
HALF = CHUNK // 2


def shard_index(x_lo, y, core):
    return x_lo * 8 + y * 2 + core


def signal(sem, device):
    pl.semaphore_signal(sem, inc=1, device_id=device, device_id_type=MESH)


def remote(src, dst, send, recv, device):
    return pltpu.make_async_remote_copy(
        src_ref=src, dst_ref=dst, send_sem=send, recv_sem=recv, device_id=device, device_id_type=MESH
    )


def source_of(slot_dest, d):
    index = jnp.int32(0)
    for j in range(N_DP):
        index = index + jnp.where(slot_dest[j] == d, j, 0)
    return jnp.minimum(index, N_DP - 1)


def exchange(frames, slot_dest, w_own, pool, w, outgoing, own_sem, a2a_send, a2a_recv, w_send, w_recv, ready, between):
    p, g = lax.axis_index("dp"), lax.axis_index("shard")
    x_lo, y, core = g // 8, (g // 2) % 4, g % 2
    up, down, across = (y + 1) % 4, (y + 3) % 4, (y + 2) % 4
    g_x = shard_index(1 - x_lo, y, core)
    g_up = shard_index(x_lo, up, core)
    g_down = shard_index(x_lo, down, core)
    g_core = shard_index(x_lo, y, 1 - core)
    depth = w_own.shape[0]

    def order(j, carry):
        outgoing[j] = frames[source_of(slot_dest, (p + j) % N_DP)]
        return carry

    lax.fori_loop(1, N_DP, order, 0)
    pool[p] = frames[source_of(slot_dest, p)]
    ready()

    def rows(block):
        return w.at[pl.ds(pl.multiple_of(block * depth, depth), depth), :]

    def send(block, peer, slot, src=None):
        return remote(
            rows(block) if src is None else src, rows(block), w_send.at[slot], w_recv.at[slot], (p, peer)
        )

    sent = []

    def go(copy):
        copy.start()
        sent.append(copy)

    go(send(g, g_up, 1, w_own))
    go(send(g, g_down, 2, w_own))
    go(send(g, g_x, 0, w_own))

    def post(j):
        d = (p + j) % N_DP
        remote(outgoing.at[j], pool.at[p], a2a_send.at[j], a2a_recv.at[j], (d, g)).start()

    def post_even(i, carry):
        post(2 * i)
        return carry

    def post_odd(i, carry):
        post(2 * i + 1)
        return carry

    lax.fori_loop(1, N_DP // 2, post_even, 0)
    lax.fori_loop(0, N_DP // 2, post_odd, 0)
    go(send(g, g_core, 7, w_own))
    own_w = pltpu.make_async_copy(w_own, rows(g), own_sem)
    own_w.start()
    between()

    def arrived(block, slot):
        remote(rows(block), rows(block), w_send.at[slot], w_recv.at[slot], (p, g_x)).wait_recv()

    arrived(g_x, 0)
    go(send(g_x, g_down, 4))
    go(send(g_x, g_up, 3))
    go(send(g_x, g_core, 8))
    b = shard_index(x_lo, down, core)
    arrived(b, 1)
    go(send(b, g_up, 5))
    go(send(b, g_core, 9))
    b = shard_index(x_lo, up, core)
    arrived(b, 2)
    go(send(b, g_core, 10))
    b = shard_index(1 - x_lo, up, core)
    arrived(b, 4)
    go(send(b, g_down, 6))
    go(send(b, g_core, 11))
    b = shard_index(1 - x_lo, down, core)
    arrived(b, 3)
    go(send(b, g_core, 12))
    b = shard_index(x_lo, across, core)
    arrived(b, 5)
    go(send(b, g_core, 13))
    b = shard_index(1 - x_lo, across, core)
    arrived(b, 6)
    go(send(b, g_core, 14))

    def collect(i, carry):
        s = (p + N_DP - i) % N_DP
        copy = remote(outgoing.at[i], pool.at[s], a2a_send.at[i], a2a_recv.at[i], (s, g))
        copy.wait_recv()
        return carry

    lax.fori_loop(1, N_DP, collect, 0)

    def finish_weight():
        other = 1 - core
        theirs = [
            (x_lo, y, 7), (1 - x_lo, y, 8), (x_lo, down, 9), (x_lo, up, 10),
            (1 - x_lo, up, 11), (1 - x_lo, down, 12), (x_lo, across, 13), (1 - x_lo, across, 14),
        ]
        for bx, by, slot in theirs:
            arrived(shard_index(bx, by, other), slot)
        own_w.wait()

    def finish_sends():
        def collect_sent(i, carry):
            remote(outgoing.at[i], pool.at[p], a2a_send.at[i], a2a_recv.at[i], (p, g_x)).wait_send()
            return carry

        lax.fori_loop(1, N_DP, collect_sent, 0)
        for copy in sent:
            copy.wait_send()

    return finish_weight, finish_sends


ROWS = 384
WIDTH = 1536
TAPS = 31
REACH = 15
PAD = 16
LANES = 128
BLOCKS = WIDTH // LANES
TILE = 256
GROUP = 48
STEP = 32
SLOT = 40


def sigmoid(v):
    return 1.0 / (1.0 + jnp.exp(-v))


def dot(a, b):
    return lax.dot_general(a, b, (((1,), (0,)), ((), ())), preferred_element_type=F32)


def dot_t(a, b):
    return lax.dot_general(a, b, (((1,), (1,)), ((), ())), preferred_element_type=F32)


def fold(v):
    total = v[0:8]
    for q in range(1, v.shape[0] // 8):
        total = total + v[q * 8 : (q + 1) * 8]
    return total


def row_mean(blocks):
    total = blocks[0]
    for b in blocks[1:]:
        total = total + b
    return jnp.sum(total, axis=1, keepdims=True) * (1.0 / WIDTH)


def lanes(b):
    return pl.ds(b * LANES if isinstance(b, int) else pl.multiple_of(b * LANES, LANES), LANES)


def find_rows(lengths, offsets, r):
    slot_len = SLOT
    rows = lax.broadcasted_iota(jnp.int32, (ROWS, LANES), 0)
    pick = jnp.zeros((ROWS, LANES), jnp.int32)
    behind = jnp.zeros((ROWS, LANES), jnp.int32)
    ahead = jnp.zeros((ROWS, LANES), jnp.int32)
    for s in range(N_DP):
        begin = offsets[s]
        end = begin + lengths[s]
        inside = (rows >= begin) & (rows < end)
        pick = jnp.where(inside, rows - begin + s * slot_len, pick)
        behind = jnp.where(inside, rows - begin, behind)
        ahead = jnp.where(inside, end - 1 - rows, ahead)
    r["behind"][...] = behind
    r["ahead"][...] = ahead
    lane = lax.broadcasted_iota(jnp.int32, (ROWS, LANES), 1)
    for t in range(N_DP * SLOT // LANES):
        r["chosen"][:, lanes(t)] = (pick == lane + t * LANES).astype(F32).astype(BF)


def load_inputs(pool, gain1, r):
    def gather(t, carry):
        cols = pl.ds(pl.multiple_of(t * TILE, TILE), TILE)
        r["unit_in"][:, cols] = dot(r["chosen"][...], pool[:, cols])
        return carry

    lax.fori_loop(0, WIDTH // TILE, gather, 0)

    def norm(i, carry):
        rows = pl.ds(pl.multiple_of(i * STEP, STEP), STEP)
        x = [r["unit_in"][rows, lanes(b)] for b in range(BLOCKS)]
        mean = row_mean(x)
        x = [v - mean for v in x]
        inverse = lax.rsqrt(row_mean([v * v for v in x]) + EPSILON)
        r["inv_in"][rows, :] = jnp.broadcast_to(inverse, (STEP, LANES))
        for b in range(BLOCKS):
            unit = x[b] * inverse
            r["unit_in"][rows, lanes(b)] = unit
            r["normed"][rows, lanes(b)] = (unit * gain1[lanes(b)].reshape(1, LANES)).astype(BF)
        return carry

    lax.fori_loop(0, ROWS // STEP, norm, 0)


def transpose_normed(r):
    for b in range(BLOCKS):
        r["normed_t"][lanes(b), :] = r["normed"][:, lanes(b)].T


def project_tile(t, w, r):
    cols = pl.ds(pl.multiple_of(t * TILE, TILE), TILE)
    gates = pl.ds(pl.multiple_of(t * TILE + WIDTH, TILE), TILE)
    linear = dot(r["normed"][...], w[:, cols])
    sig = sigmoid(dot(r["normed"][...], w[:, gates]))
    r["linear"][:, cols] = linear
    r["sig"][:, cols] = sig
    gated = (linear * sig).astype(BF).astype(F32)
    for j in range(TILE // LANES):
        r["gated"][t * (TILE // LANES) + j, PAD : PAD + ROWS, :] = gated[:, j * LANES : (j + 1) * LANES]


def tap_mask(behind, ahead, shift):
    return ahead >= shift if shift > 0 else behind >= -shift


def convolve_pair(c, w_depth, r):
    for g in range(ROWS // GROUP):
        begin = g * GROUP
        behind = r["behind"][begin : begin + GROUP, :]
        ahead = r["ahead"][begin : begin + GROUP, :]
        total = [jnp.zeros((GROUP, LANES), F32)] * 2
        for k in range(TAPS):
            shift = k - REACH
            same = tap_mask(behind, ahead, shift)
            for j in range(2):
                b = c * 2 + j
                x = r["gated"][b, PAD + begin + shift : PAD + begin + shift + GROUP, :]
                if shift != 0:
                    x = jnp.where(same, x, 0.0)
                total[j] = total[j] + x * w_depth[k : k + 1, lanes(b)]
        for j in range(2):
            r["conv"][c * 2 + j, PAD + begin : PAD + begin + GROUP, :] = total[j]


def project_and_convolve(w, w_depth, r):
    project_tile(0, w, r)

    def step(t, carry):
        convolve_pair(t - 1, w_depth, r)
        project_tile(t, w, r)
        return carry

    lax.fori_loop(1, BLOCKS // 2, step, 0)
    convolve_pair(BLOCKS // 2 - 1, w_depth, r)


def finish_forward(gain2, cotangent, output, r):
    r["gain2_sum"][...] = jnp.zeros_like(r["gain2_sum"])

    def row_step(i, carry):
        rows = pl.ds(pl.multiple_of(i * STEP, STEP), STEP)
        held = pl.ds(pl.multiple_of(i * STEP + PAD, 16), STEP)
        x = [r["conv"][b, held, :] for b in range(BLOCKS)]
        mean = row_mean(x)
        x = [v - mean for v in x]
        inverse = lax.rsqrt(row_mean([v * v for v in x]) + EPSILON)
        units, grads = [], []
        for b in range(BLOCKS):
            unit = x[b] * inverse
            gain = gain2[lanes(b)].reshape(1, LANES)
            scaled = unit * gain
            sig = sigmoid(scaled)
            output[rows, lanes(b)] = (scaled * sig).astype(BF)
            grad = cotangent[rows, lanes(b)].astype(F32) * sig * (1.0 + scaled * (1.0 - sig))
            both = grad * unit
            r["gain2_sum"][b] = r["gain2_sum"][b] + fold(both)
            units.append(unit)
            grads.append(grad * gain)
        first = row_mean(grads)
        second = row_mean([q * u for q, u in zip(grads, units)])
        for b in range(BLOCKS):
            r["conv"][b, held, :] = inverse * (grads[b] - first - units[b] * second)
        return carry

    lax.fori_loop(0, ROWS // STEP, row_step, 0)


def back_convolve_pair(c, w_depth, small, r):
    first = c * 2
    r["tap_sum"][...] = jnp.zeros_like(r["tap_sum"])
    for g in range(ROWS // GROUP):
        begin = g * GROUP
        rows = slice(begin, begin + GROUP)
        behind = r["behind"][rows, :]
        ahead = r["ahead"][rows, :]
        total = [jnp.zeros((GROUP, LANES), F32)] * 2
        gated = [r["gated"][first + j, PAD + begin : PAD + begin + GROUP, :] for j in range(2)]
        for k in range(TAPS):
            shift = REACH - k
            same = tap_mask(behind, ahead, shift)
            for j in range(2):
                x = r["conv"][first + j, PAD + begin + shift : PAD + begin + shift + GROUP, :]
                if shift != 0:
                    x = jnp.where(same, x, 0.0)
                total[j] = total[j] + x * w_depth[k : k + 1, lanes(first + j)]
                product = x * gated[j]
                r["tap_sum"][j, k] = r["tap_sum"][j, k] + fold(product)
        for j in range(2):
            at = pl.multiple_of((first + j) * LANES, LANES)
            linear = r["linear"][rows, pl.ds(at, LANES)]
            sig = r["sig"][rows, pl.ds(at, LANES)]
            grad = total[j] * sig
            r["grad_pre"][rows, pl.ds(at, LANES)] = grad.astype(BF)
            r["grad_pre"][rows, pl.ds(at + WIDTH, LANES)] = (grad * linear * (1.0 - sig)).astype(BF)
    for j in range(2):
        at = pl.multiple_of((first + j) * LANES, LANES)
        small[0:TAPS, pl.ds(at, LANES)] = jnp.sum(r["tap_sum"][j], axis=1)


def back_convolve(chunk, w_depth, small, r, beside):
    count = HALF // LANES // 2

    def pair(c, carry):
        back_convolve_pair(chunk * count + c, w_depth, small, r)
        beside(c)
        return carry

    lax.fori_loop(0, count, pair, 0)


def weight_term(chunk, part, r):
    def tile(i, carry):
        rows = pl.ds(pl.multiple_of(i * 384, 384), 384)
        for h in range(2):
            cols = pl.ds(pl.multiple_of(h * WIDTH + chunk * HALF, HALF), HALF)
            value = dot(r["normed_t"][rows, :], r["grad_pre"][:, cols]).astype(BF)
            for q in range(4):
                part[i // 2, (i % 2) * 2 + q // 2, q % 2, :, h * HALF : (h + 1) * HALF] = value[q * 96 : (q + 1) * 96]
        return carry

    lax.fori_loop(0, 4, tile, 0)


def back_project(w, r, beside):
    def tile(t, carry):
        cols = pl.ds(pl.multiple_of(t * TILE, TILE), TILE)
        r["linear"][:, cols] = dot_t(r["grad_pre"][...], w[cols, :])
        beside(t)
        return carry

    lax.fori_loop(0, WIDTH // TILE, tile, 0)


def finish_back(gain1, grad_input, small, r):
    r["gain1_sum"][...] = jnp.zeros_like(r["gain1_sum"])

    def row_step(i, carry):
        rows = pl.ds(pl.multiple_of(i * STEP, STEP), STEP)
        inverse = r["inv_in"][rows, :]
        units = [r["unit_in"][rows, lanes(b)] for b in range(BLOCKS)]
        grads = [r["linear"][rows, lanes(b)] for b in range(BLOCKS)]
        for b in range(BLOCKS):
            both = grads[b] * units[b]
            r["gain1_sum"][b] = r["gain1_sum"][b] + fold(both)
        grads = [grads[b] * gain1[lanes(b)].reshape(1, LANES) for b in range(BLOCKS)]
        first = row_mean(grads)
        second = row_mean([q * u for q, u in zip(grads, units)])
        for b in range(BLOCKS):
            grad_input[rows, lanes(b)] = (inverse * (grads[b] - first - units[b] * second)).astype(BF)
        return carry

    lax.fori_loop(0, ROWS // STEP, row_step, 0)
    for b in range(BLOCKS):
        small[TAPS : TAPS + 1, lanes(b)] = jnp.sum(r["gain1_sum"][b], axis=0, keepdims=True)
        small[TAPS + 1 : TAPS + 2, lanes(b)] = jnp.sum(r["gain2_sum"][b], axis=0, keepdims=True)
    small[TAPS + 2 : SMALL_ROWS, :] = jnp.zeros((SMALL_ROWS - TAPS - 2, WIDTH), F32)


WORK = (
    ("behind", (ROWS, LANES), jnp.int32),
    ("ahead", (ROWS, LANES), jnp.int32),
    ("chosen", (ROWS, N_DP * SLOT), BF),
    ("unit_in", (ROWS, WIDTH), F32),
    ("inv_in", (ROWS, LANES), F32),
    ("normed", (ROWS, WIDTH), BF),
    ("normed_t", (WIDTH, ROWS), BF),
    ("linear", (ROWS, WIDTH), F32),
    ("sig", (ROWS, WIDTH), F32),
    ("gated", (BLOCKS, PAD + ROWS + PAD, LANES), F32),
    ("conv", (BLOCKS, PAD + ROWS + PAD, LANES), F32),
    ("gain1_sum", (BLOCKS, 8, LANES), F32),
    ("gain2_sum", (BLOCKS, 8, LANES), F32),
    ("tap_sum", (2, TAPS, 8, LANES), F32),
    ("grad_pre", (ROWS, 2 * WIDTH), BF),
)


def add_blocks(dst, src, count, cols):
    def step(i, carry):
        block, row = i // 2, pl.multiple_of((i % 2) * 48, 48)
        d, s = dst(block), src(block)
        value = d[pl.ds(row, 48), cols].astype(F32) + s[pl.ds(row, 48), :].astype(F32)
        d[pl.ds(row, 48), cols] = value.astype(BF)
        return carry

    lax.fori_loop(0, count * 2, step, 0)


X_FIRST = (False, True, False)


def module_kernel(
    frames_hbm, slot_dest, lengths, offsets, gain1, w_own, w_depth, gain2, cotangent_hbm,
    output_hbm, grad_input_hbm, out, depth_out, gain1_out, gain2_out,
    frames, cotangent, output, grad_input, io_sems, arriving, pool, w, outgoing, own_sem, a2a_send, a2a_recv, w_send, w_recv, small, part, rx0, rx1, rx2, rx3, rx3_all, rx4, red, fin, rxs, rxd, small_fin,
    s0, r0, s1, r1, s2, r2, s3, r3, s4, r4, s5, r5, st1, rt1, st2, rt2, st3, rt3,
    *work
):
    r = {name: ref for (name, _, _), ref in zip(WORK, work)}
    p, g = lax.axis_index("dp"), lax.axis_index("shard")
    x_lo, y, core = g // 8, (g // 2) % 4, g % 2
    mates = (y + 1 - 2 * (y % 2), 3 - y)
    scale = 1.0 / (N_DP * N_SHARD)

    barrier = pltpu.get_barrier_semaphore()

    def greet(i, carry):
        signal(barrier, ((p + i) % N_DP, g))
        signal(barrier, (p, (g + i) % N_SHARD))
        return carry

    lax.fori_loop(1, 16, greet, 0)

    def core_copy(k):
        return remote(
            part.at[k, :, :, 1 - core], rx0.at[k], s0.at[k], r0.at[k], (p, shard_index(x_lo, y, 1 - core))
        )

    def finish_core(k):
        core_copy(k).wait_recv()
        add_blocks(
            lambda i: part.at[k, i // 4, i % 4, core], lambda i: rx0.at[k, i // 4, i % 4], 8, slice(None)
        )

    def cols(h):
        return pl.ds(HALF * h, HALF)

    def wide(k):
        return 1 if X_FIRST[k] else 2

    def first_x(k, i):
        return x_lo if X_FIRST[k] else i

    def y_block(k, block, h):
        if X_FIRST[k]:
            return part.at[k, pl.ds(x_lo, 1), block, core, :, cols(h)]
        return part.at[k, :, block, core, :, cols(h)]

    def y1_copy(k, h, j):
        q = mates[h]
        after = 3 - q if h == 0 else q + 1 - 2 * (q % 2)
        return remote(
            y_block(k, q if j == 0 else after, h), rx1.at[k, h, j, pl.ds(0, wide(k))],
            s1.at[k, h, j], r1.at[k, h, j], (p, shard_index(x_lo, q, core)),
        )

    def start_y1(k):
        for j in (1, 0):
            for h in range(2):
                y1_copy(k, h, j).start()

    def y2_copy(k, h):
        q = mates[1 - h]
        return remote(
            y_block(k, q, h), rx2.at[k, h, pl.ds(0, wide(k))], s2.at[k, h], r2.at[k, h],
            (p, shard_index(x_lo, q, core)),
        )

    def turn_y(k):
        for h in range(2):
            y1_copy(k, h, 1).wait_recv()
            add_blocks(
                lambda i: part.at[k, first_x(k, i), mates[1 - h], core],
                lambda i: rx1.at[k, h, 1, i], wide(k), cols(h),
            )
            y2_copy(k, h).start()
        for h in range(2):
            y1_copy(k, h, 0).wait_recv()
            add_blocks(
                lambda i: part.at[k, first_x(k, i), y, core], lambda i: rx1.at[k, h, 0, i], wide(k), cols(h)
            )

    def finish_y(k):
        for h in range(2):
            y2_copy(k, h).wait_recv()
            add_blocks(
                lambda i: part.at[k, first_x(k, i), y, core], lambda i: rx2.at[k, h, i], wide(k), cols(h)
            )

    def x_copy(k):
        peer = (p, shard_index(1 - x_lo, y, core))
        if X_FIRST[k]:
            return remote(part.at[k, 1 - x_lo, :, core], rx3_all, s3.at[k], r3.at[k], peer)
        return remote(part.at[k, 1 - x_lo, y, core], rx3.at[k], s3.at[k], r3.at[k], peer)

    def finish_x(k):
        x_copy(k).wait_recv()
        if X_FIRST[k]:
            add_blocks(lambda i: part.at[k, x_lo, i, core], lambda i: rx3_all.at[i], 4, slice(None))
        else:
            add_blocks(lambda i: part.at[k, x_lo, y, core], lambda i: rx3.at[k], 1, slice(None))

    def at_piece(ref, d, base):
        return ref.at[
            pl.ds(pl.multiple_of((d % 2) * 48, 48), 48), pl.ds(pl.multiple_of(base + (d // 2) * 128, 128), 128)
        ]

    def piece_copy(k, i):
        d = (p + i) % N_DP
        return remote(
            at_piece(part.at[k, x_lo, y, core], d, 0), rx4.at[k, i - 1], s4.at[k, i - 1], r4.at[k, i - 1], (d, g)
        )

    def sum_copy(k, i, sender):
        d = (p + i) % N_DP
        return remote(red.at[k], at_piece(fin, sender, CHUNK * k), s5.at[k, i - 1], r5.at[k, i - 1], (d, g))

    def each(count, do):
        def step(i, carry):
            do(i)
            return carry

        lax.fori_loop(1, count, step, 0)

    def start_pieces(k):
        each(N_DP, lambda i: piece_copy(k, i).start())

    def turn_pieces(k):
        each(N_DP, lambda i: piece_copy(k, i).wait_recv())
        total = at_piece(part.at[k, x_lo, y, core], p, 0)[...].astype(F32)
        for i in range(N_DP - 1):
            total = total + rx4[k, i].astype(F32)
        total = total.astype(BF)
        red[k] = total
        at_piece(fin, p, CHUNK * k)[...] = total
        each(N_DP, lambda i: sum_copy(k, i, p).start())

    def finish_pieces(k):
        each(N_DP, lambda i: sum_copy(k, i, (p + N_DP - i) % N_DP).wait_recv())

        def widen(i, carry):
            rows = pl.ds(pl.multiple_of(i * 48, 48), 48)
            for h in range(2):
                out[rows, pl.ds(h * WIDTH + HALF * k, HALF)] = (
                    fin[rows, pl.ds(CHUNK * k + HALF * h, HALF)].astype(F32) * scale
                )
            return carry

        lax.fori_loop(0, 2, widen, 0)

    def column(j):
        return pl.ds(pl.multiple_of(j * LANES, LANES), LANES)

    def small_copy(j):
        return remote(small.at[:, column(j)], rxs.at[g], st1.at[j], rt1.at[g], (p, j))

    def each_owner(do):
        def step(j, carry):
            @pl.when(j != g)
            def _():
                do(j)

            return carry

        lax.fori_loop(0, SMALL_OWNERS, step, 0)

    def small_sum_copy(i):
        return remote(rxd.at[p], rxd.at[p], st2.at[i - 1], rt2.at[p], ((p + i) % N_DP, g))

    def small_final_copy(i):
        return remote(
            small_fin.at[:, column(g)], small_fin.at[:, column(g)], st3.at[i - 1], rt3.at[g],
            (p, (g + i) % N_SHARD),
        )

    def add_small_shard():
        @pl.when(g < SMALL_OWNERS)
        def _():
            def take(i):
                s = (g + i) % N_SHARD
                remote(small.at[:, column(0)], rxs.at[s], st1.at[0], rt1.at[s], (p, s)).wait_recv()

            each(N_SHARD, take)
            rxs[g] = small[:, column(g)]
            total = rxs[0]
            for s in range(1, N_SHARD):
                total = total + rxs[s]
            rxd[p] = total
            each(N_DP, lambda i: small_sum_copy(i).start())

    def add_small_dp():
        @pl.when(g < SMALL_OWNERS)
        def _():
            def take(i):
                s = (p + i) % N_DP
                remote(rxd.at[s], rxd.at[s], st2.at[0], rt2.at[s], (s, g)).wait_recv()

            each(N_DP, take)
            total = rxd[0]
            for s in range(1, N_DP):
                total = total + rxd[s]
            small_fin[:, column(g)] = total
            each(N_SHARD, lambda i: small_final_copy(i).start())

    load_frames = pltpu.make_async_copy(frames_hbm, frames, io_sems.at[0])
    load_frames.start()
    load_cotangent = pltpu.make_async_copy(cotangent_hbm, cotangent, io_sems.at[1])
    load_cotangent.start()
    store_output = pltpu.make_async_copy(output, output_hbm, io_sems.at[2])
    store_grad = pltpu.make_async_copy(grad_input, grad_input_hbm, io_sems.at[3])
    load_frames.wait()

    def ready():
        pl.semaphore_wait(barrier, 30)

    def between():
        for name in ("gated", "conv"):
            r[name][:, 0:PAD, :] = jnp.zeros((BLOCKS, PAD, LANES), F32)
            r[name][:, PAD + ROWS :, :] = jnp.zeros((BLOCKS, PAD, LANES), F32)
        find_rows(lengths, offsets, r)

    finish_weight, finish_sends = exchange(
        frames, slot_dest, w_own, arriving, w, outgoing, own_sem, a2a_send, a2a_recv, w_send, w_recv, ready, between
    )
    for s in range(N_DP):
        pool[s * SLOT : (s + 1) * SLOT, :] = arriving[s]
    load_inputs(pool, gain1, r)
    finish_weight()
    project_and_convolve(w, w_depth, r)
    load_cotangent.wait()
    finish_forward(gain2, cotangent, output, r)
    store_output.start()
    transpose_normed(r)
    def beside_first(c):
        pass

    def beside_second(c):
        @pl.when(c == 0)
        def _():
            finish_core(0)
            start_y1(0)

    def beside_third(c):
        @pl.when(c == 0)
        def _():
            finish_core(1)
            x_copy(1).start()
            turn_y(0)

    for k, beside in enumerate((beside_first, beside_second, beside_third)):
        back_convolve(k, w_depth, small, r, beside)
        weight_term(k, part.at[k], r)
        core_copy(k).start()
    finish_y(0)
    x_copy(0).start()

    def beside(t):
        @pl.when(t == 2)
        def _():
            finish_core(2)
            start_y1(2)

        @pl.when(t == 5)
        def _():
            finish_x(0)
            start_pieces(0)

    back_project(w, r, beside)
    finish_back(gain1, grad_input, small, r)
    store_grad.start()
    each_owner(lambda j: small_copy(j).start())
    turn_y(2)
    finish_x(1)
    start_y1(1)
    turn_pieces(0)
    finish_y(2)
    x_copy(2).start()
    add_small_shard()
    turn_y(1)
    finish_x(2)
    start_pieces(2)
    finish_y(1)
    start_pieces(1)
    add_small_dp()
    turn_pieces(2)
    turn_pieces(1)
    finish_pieces(0)

    def take_final(j):
        remote(
            small_fin.at[:, column(j)], small_fin.at[:, column(j)], st3.at[0], rt3.at[j], (p, j)
        ).wait_recv()

    each_owner(take_final)
    depth_out[...] = small_fin[0:TAPS, :] * scale
    for b in range(BLOCKS):
        gain1_out[lanes(b)] = small_fin[TAPS, lanes(b)] * scale
        gain2_out[lanes(b)] = small_fin[TAPS + 1, lanes(b)] * scale
    finish_sends()
    store_output.wait()
    store_grad.wait()
    finish_pieces(2)
    finish_pieces(1)

    for k in range(CHUNKS):
        core_copy(k).wait_send()
        x_copy(k).wait_send()
        for h in range(2):
            y1_copy(k, h, 0).wait_send()
            y1_copy(k, h, 1).wait_send()
            y2_copy(k, h).wait_send()

        def sent(i):
            piece_copy(k, i).wait_send()
            sum_copy(k, i, p).wait_send()

        each(N_DP, sent)
    each_owner(lambda j: small_copy(j).wait_send())

    @pl.when(g < SMALL_OWNERS)
    def _():
        def sent(i):
            small_sum_copy(i).wait_send()
            small_final_copy(i).wait_send()

        each(16, sent)


def module(frames, slot_dest, lengths, offsets, gain1, w_in, w_depth, gain2, cotangent):
    vmem = pl.BlockSpec(memory_space=pltpu.VMEM)
    smem = pl.BlockSpec(memory_space=pltpu.SMEM)
    hbm = pl.BlockSpec(memory_space=pl.ANY)
    block = WIDTH // N_SHARD
    dma = pltpu.SemaphoreType.DMA
    return pl.pallas_call(
        module_kernel,
        out_shape=(
            jax.ShapeDtypeStruct((ROWS, WIDTH), BF),
            jax.ShapeDtypeStruct((ROWS, WIDTH), BF),
            jax.ShapeDtypeStruct((block, 2 * WIDTH), F32),
            jax.ShapeDtypeStruct((TAPS, WIDTH), F32),
            jax.ShapeDtypeStruct((WIDTH,), F32),
            jax.ShapeDtypeStruct((WIDTH,), F32),
        ),
        in_specs=[hbm, smem, smem, smem, vmem, hbm, vmem, vmem, hbm],
        out_specs=(hbm, hbm, vmem, vmem, vmem, vmem),
        scratch_shapes=[
            pltpu.VMEM((N_DP, SLOT, WIDTH), BF),
            pltpu.VMEM((ROWS, WIDTH), BF),
            pltpu.VMEM((ROWS, WIDTH), BF),
            pltpu.VMEM((ROWS, WIDTH), BF),
            dma((4,)),
            pltpu.VMEM((N_DP, SLOT, WIDTH), BF),
            pltpu.VMEM((N_DP * SLOT, WIDTH), BF),
            pltpu.VMEM((WIDTH, 2 * WIDTH), BF),
            pltpu.VMEM((N_DP, SLOT, WIDTH), BF),
            dma,
            dma((N_DP,)), dma((N_DP,)),
            dma((15,)), dma((15,)),
            pltpu.VMEM((SMALL_ROWS, WIDTH), F32),
            pltpu.VMEM((CHUNKS, 2, 4, 2, block, CHUNK), BF),
            pltpu.VMEM((CHUNKS, 2, 4, block, CHUNK), BF),
            pltpu.VMEM((CHUNKS, 2, 2, 2, block, HALF), BF),
            pltpu.VMEM((CHUNKS, 2, 2, block, HALF), BF),
            pltpu.VMEM((CHUNKS, block, CHUNK), BF),
            pltpu.VMEM((4, block, CHUNK), BF),
            pltpu.VMEM((CHUNKS, N_DP - 1, block // 2, 128), BF),
            pltpu.VMEM((CHUNKS, block // 2, 128), BF),
            pltpu.VMEM((block, 2 * WIDTH), BF),
            pltpu.VMEM((N_SHARD, SMALL_ROWS, 128), F32),
            pltpu.VMEM((N_DP, SMALL_ROWS, 128), F32),
            pltpu.VMEM((SMALL_ROWS, WIDTH), F32),
            dma((CHUNKS,)), dma((CHUNKS,)),
            dma((CHUNKS, 2, 2)), dma((CHUNKS, 2, 2)),
            dma((CHUNKS, 2)), dma((CHUNKS, 2)),
            dma((CHUNKS,)), dma((CHUNKS,)),
            dma((CHUNKS, N_DP - 1)), dma((CHUNKS, N_DP - 1)),
            dma((CHUNKS, N_DP - 1)), dma((CHUNKS, N_DP - 1)),
            dma((SMALL_OWNERS,)), dma((N_SHARD,)),
            dma((N_DP - 1,)), dma((N_DP,)),
            dma((N_SHARD - 1,)), dma((SMALL_OWNERS,)),
            *[pltpu.VMEM(shape, dtype) for _, shape, dtype in WORK],
        ],
        compiler_params=pltpu.CompilerParams(
            collective_id=0, has_side_effects=True, vmem_limit_bytes=64 * 1024 * 1024 - 65536
        ),
        name="module",
    )(frames, slot_dest, lengths, offsets, gain1, w_in, w_depth, gain2, cotangent)


def body(frames, slot_dest, recv_length, recv_offset, gain1, w_in, w_depth, gain2, cotangent):
    return module(frames, slot_dest, recv_length, recv_offset, gain1, w_in, w_depth, gain2, cotangent)


def solution(mesh):
    in_specs = (
        P(("dp", "shard"), None, None),
        P(("dp", "shard")),
        P(("dp", "shard")),
        P(("dp", "shard")),
        P(),
        P("shard", None),
        P(),
        P(),
        P(("dp", "shard"), None),
    )
    out_specs = (
        P(("dp", "shard"), None),
        P(("dp", "shard"), None),
        P("shard", None),
        P(),
        P(),
        P(),
    )
    return jax.shard_map(body, mesh=mesh, in_specs=in_specs, out_specs=out_specs, check_vma=False)
```

```python
import jax
import jax.numpy as jnp
from jax import lax
from jax.experimental import pallas as pl
from jax.experimental.pallas import tpu as pltpu
from jax.sharding import PartitionSpec as P

EPSILON = 1e-05
MESH = pl.DeviceIdType.MESH
BF = jnp.bfloat16
F32 = jnp.float32

N_DP = 16
N_SHARD = 16
SMALL_ROWS = 40
SMALL_OWNERS = 12
CHUNKS = 3
CHUNK = 1024
HALF = CHUNK // 2


def shard_index(x_lo, y, core):
    return x_lo * 8 + y * 2 + core


def signal(sem, device):
    pl.semaphore_signal(sem, inc=1, device_id=device, device_id_type=MESH)


def remote(src, dst, send, recv, device):
    return pltpu.make_async_remote_copy(
        src_ref=src, dst_ref=dst, send_sem=send, recv_sem=recv, device_id=device, device_id_type=MESH
    )


def source_of(slot_dest, d):
    index = jnp.int32(0)
    for j in range(N_DP):
        index = index + jnp.where(slot_dest[j] == d, j, 0)
    return jnp.minimum(index, N_DP - 1)


def exchange(frames, slot_dest, w_own, pool, w, outgoing, own_sem, a2a_send, a2a_recv, w_send, w_recv, ready, between):
    p, g = lax.axis_index("dp"), lax.axis_index("shard")
    x_lo, y, core = g // 8, (g // 2) % 4, g % 2
    up, down, across = (y + 1) % 4, (y + 3) % 4, (y + 2) % 4
    g_x = shard_index(1 - x_lo, y, core)
    g_up = shard_index(x_lo, up, core)
    g_down = shard_index(x_lo, down, core)
    g_core = shard_index(x_lo, y, 1 - core)
    depth = w_own.shape[0]

    def order(j, carry):
        outgoing[j] = frames[source_of(slot_dest, (p + j) % N_DP)]
        return carry

    lax.fori_loop(1, N_DP, order, 0)
    pool[p] = frames[source_of(slot_dest, p)]
    ready()

    def rows(block):
        return w.at[pl.ds(pl.multiple_of(block * depth, depth), depth), :]

    def send(block, peer, slot, src=None):
        return remote(
            rows(block) if src is None else src, rows(block), w_send.at[slot], w_recv.at[slot], (p, peer)
        )

    sent = []

    def go(copy):
        copy.start()
        sent.append(copy)

    go(send(g, g_up, 1, w_own))
    go(send(g, g_down, 2, w_own))
    go(send(g, g_x, 0, w_own))

    def post(j):
        d = (p + j) % N_DP
        remote(outgoing.at[j], pool.at[p], a2a_send.at[j], a2a_recv.at[j], (d, g)).start()

    def post_even(i, carry):
        post(2 * i)
        return carry

    def post_odd(i, carry):
        post(2 * i + 1)
        return carry

    lax.fori_loop(1, N_DP // 2, post_even, 0)
    lax.fori_loop(0, N_DP // 2, post_odd, 0)
    go(send(g, g_core, 7, w_own))
    own_w = pltpu.make_async_copy(w_own, rows(g), own_sem)
    own_w.start()
    between()

    def arrived(block, slot):
        remote(rows(block), rows(block), w_send.at[slot], w_recv.at[slot], (p, g_x)).wait_recv()

    arrived(g_x, 0)
    go(send(g_x, g_down, 4))
    go(send(g_x, g_up, 3))
    go(send(g_x, g_core, 8))
    b = shard_index(x_lo, down, core)
    arrived(b, 1)
    go(send(b, g_up, 5))
    go(send(b, g_core, 9))
    b = shard_index(x_lo, up, core)
    arrived(b, 2)
    go(send(b, g_core, 10))
    b = shard_index(1 - x_lo, up, core)
    arrived(b, 4)
    go(send(b, g_down, 6))
    go(send(b, g_core, 11))
    b = shard_index(1 - x_lo, down, core)
    arrived(b, 3)
    go(send(b, g_core, 12))
    b = shard_index(x_lo, across, core)
    arrived(b, 5)
    go(send(b, g_core, 13))
    b = shard_index(1 - x_lo, across, core)
    arrived(b, 6)
    go(send(b, g_core, 14))

    def collect(i, carry):
        s = (p + N_DP - i) % N_DP
        copy = remote(outgoing.at[i], pool.at[s], a2a_send.at[i], a2a_recv.at[i], (s, g))
        copy.wait_recv()
        return carry

    lax.fori_loop(1, N_DP, collect, 0)

    def finish_weight():
        other = 1 - core
        theirs = [
            (x_lo, y, 7), (1 - x_lo, y, 8), (x_lo, down, 9), (x_lo, up, 10),
            (1 - x_lo, up, 11), (1 - x_lo, down, 12), (x_lo, across, 13), (1 - x_lo, across, 14),
        ]
        for bx, by, slot in theirs:
            arrived(shard_index(bx, by, other), slot)
        own_w.wait()

    def finish_sends():
        def collect_sent(i, carry):
            remote(outgoing.at[i], pool.at[p], a2a_send.at[i], a2a_recv.at[i], (p, g_x)).wait_send()
            return carry

        lax.fori_loop(1, N_DP, collect_sent, 0)
        for copy in sent:
            copy.wait_send()

    return finish_weight, finish_sends


ROWS = 384
WIDTH = 1536
TAPS = 31
REACH = 15
PAD = 16
LANES = 128
BLOCKS = WIDTH // LANES
TILE = 256
GROUP = 48
STEP = 32
SLOT = 40


def sigmoid(v):
    return 1.0 / (1.0 + jnp.exp(-v))


def dot(a, b):
    return lax.dot_general(a, b, (((1,), (0,)), ((), ())), preferred_element_type=F32)


def dot_t(a, b):
    return lax.dot_general(a, b, (((1,), (1,)), ((), ())), preferred_element_type=F32)


def fold(v):
    total = v[0:8]
    for q in range(1, v.shape[0] // 8):
        total = total + v[q * 8 : (q + 1) * 8]
    return total


def row_mean(blocks):
    total = blocks[0]
    for b in blocks[1:]:
        total = total + b
    return jnp.sum(total, axis=1, keepdims=True) * (1.0 / WIDTH)


def lanes(b):
    return pl.ds(b * LANES if isinstance(b, int) else pl.multiple_of(b * LANES, LANES), LANES)


def find_rows(lengths, offsets, r):
    slot_len = SLOT
    rows = lax.broadcasted_iota(jnp.int32, (ROWS, LANES), 0)
    pick = jnp.zeros((ROWS, LANES), jnp.int32)
    behind = jnp.zeros((ROWS, LANES), jnp.int32)
    ahead = jnp.zeros((ROWS, LANES), jnp.int32)
    for s in range(N_DP):
        begin = offsets[s]
        end = begin + lengths[s]
        inside = (rows >= begin) & (rows < end)
        pick = jnp.where(inside, rows - begin + s * slot_len, pick)
        behind = jnp.where(inside, rows - begin, behind)
        ahead = jnp.where(inside, end - 1 - rows, ahead)
    r["behind"][...] = behind
    r["ahead"][...] = ahead
    lane = lax.broadcasted_iota(jnp.int32, (ROWS, LANES), 1)
    for t in range(N_DP * SLOT // LANES):
        r["chosen"][:, lanes(t)] = (pick == lane + t * LANES).astype(F32).astype(BF)


def load_inputs(pool, gain1, r):
    def gather(t, carry):
        cols = pl.ds(pl.multiple_of(t * TILE, TILE), TILE)
        r["unit_in"][:, cols] = dot(r["chosen"][...], pool[:, cols])
        return carry

    lax.fori_loop(0, WIDTH // TILE, gather, 0)

    def norm(i, carry):
        rows = pl.ds(pl.multiple_of(i * STEP, STEP), STEP)
        x = [r["unit_in"][rows, lanes(b)] for b in range(BLOCKS)]
        mean = row_mean(x)
        x = [v - mean for v in x]
        inverse = lax.rsqrt(row_mean([v * v for v in x]) + EPSILON)
        r["inv_in"][rows, :] = jnp.broadcast_to(inverse, (STEP, LANES))
        for b in range(BLOCKS):
            unit = x[b] * inverse
            r["unit_in"][rows, lanes(b)] = unit
            r["normed"][rows, lanes(b)] = (unit * gain1[lanes(b)].reshape(1, LANES)).astype(BF)
        return carry

    lax.fori_loop(0, ROWS // STEP, norm, 0)


def transpose_normed(r):
    for b in range(BLOCKS):
        r["normed_t"][lanes(b), :] = r["normed"][:, lanes(b)].T


def project_tile(t, w, r):
    cols = pl.ds(pl.multiple_of(t * TILE, TILE), TILE)
    gates = pl.ds(pl.multiple_of(t * TILE + WIDTH, TILE), TILE)
    linear = dot(r["normed"][...], w[:, cols])
    sig = sigmoid(dot(r["normed"][...], w[:, gates]))
    r["linear"][:, cols] = linear
    r["sig"][:, cols] = sig
    gated = (linear * sig).astype(BF).astype(F32)
    for j in range(TILE // LANES):
        r["gated"][t * (TILE // LANES) + j, PAD : PAD + ROWS, :] = gated[:, j * LANES : (j + 1) * LANES]


def tap_mask(behind, ahead, shift):
    return ahead >= shift if shift > 0 else behind >= -shift


def convolve_pair(c, w_depth, r):
    for g in range(ROWS // GROUP):
        begin = g * GROUP
        behind = r["behind"][begin : begin + GROUP, :]
        ahead = r["ahead"][begin : begin + GROUP, :]
        total = [jnp.zeros((GROUP, LANES), F32)] * 2
        for k in range(TAPS):
            shift = k - REACH
            same = tap_mask(behind, ahead, shift)
            for j in range(2):
                b = c * 2 + j
                x = r["gated"][b, PAD + begin + shift : PAD + begin + shift + GROUP, :]
                if shift != 0:
                    x = jnp.where(same, x, 0.0)
                total[j] = total[j] + x * w_depth[k : k + 1, lanes(b)]
        for j in range(2):
            r["conv"][c * 2 + j, PAD + begin : PAD + begin + GROUP, :] = total[j]


def project_and_convolve(w, w_depth, r):
    project_tile(0, w, r)

    def step(t, carry):
        convolve_pair(t - 1, w_depth, r)
        project_tile(t, w, r)
        return carry

    lax.fori_loop(1, BLOCKS // 2, step, 0)
    convolve_pair(BLOCKS // 2 - 1, w_depth, r)


def finish_forward(gain2, cotangent, output, r):
    r["gain2_sum"][...] = jnp.zeros_like(r["gain2_sum"])

    def row_step(i, carry):
        rows = pl.ds(pl.multiple_of(i * STEP, STEP), STEP)
        held = pl.ds(pl.multiple_of(i * STEP + PAD, 16), STEP)
        x = [r["conv"][b, held, :] for b in range(BLOCKS)]
        mean = row_mean(x)
        x = [v - mean for v in x]
        inverse = lax.rsqrt(row_mean([v * v for v in x]) + EPSILON)
        units, grads = [], []
        for b in range(BLOCKS):
            unit = x[b] * inverse
            gain = gain2[lanes(b)].reshape(1, LANES)
            scaled = unit * gain
            sig = sigmoid(scaled)
            output[rows, lanes(b)] = (scaled * sig).astype(BF)
            grad = cotangent[rows, lanes(b)].astype(F32) * sig * (1.0 + scaled * (1.0 - sig))
            both = grad * unit
            r["gain2_sum"][b] = r["gain2_sum"][b] + fold(both)
            units.append(unit)
            grads.append(grad * gain)
        first = row_mean(grads)
        second = row_mean([q * u for q, u in zip(grads, units)])
        for b in range(BLOCKS):
            r["conv"][b, held, :] = inverse * (grads[b] - first - units[b] * second)
        return carry

    lax.fori_loop(0, ROWS // STEP, row_step, 0)


def back_convolve_pair(c, w_depth, small, r):
    first = c * 2
    r["tap_sum"][...] = jnp.zeros_like(r["tap_sum"])
    for g in range(ROWS // GROUP):
        begin = g * GROUP
        rows = slice(begin, begin + GROUP)
        behind = r["behind"][rows, :]
        ahead = r["ahead"][rows, :]
        total = [jnp.zeros((GROUP, LANES), F32)] * 2
        gated = [r["gated"][first + j, PAD + begin : PAD + begin + GROUP, :] for j in range(2)]
        for k in range(TAPS):
            shift = REACH - k
            same = tap_mask(behind, ahead, shift)
            for j in range(2):
                x = r["conv"][first + j, PAD + begin + shift : PAD + begin + shift + GROUP, :]
                if shift != 0:
                    x = jnp.where(same, x, 0.0)
                total[j] = total[j] + x * w_depth[k : k + 1, lanes(first + j)]
                product = x * gated[j]
                r["tap_sum"][j, k] = r["tap_sum"][j, k] + fold(product)
        for j in range(2):
            at = pl.multiple_of((first + j) * LANES, LANES)
            linear = r["linear"][rows, pl.ds(at, LANES)]
            sig = r["sig"][rows, pl.ds(at, LANES)]
            grad = total[j] * sig
            r["grad_pre"][rows, pl.ds(at, LANES)] = grad.astype(BF)
            r["grad_pre"][rows, pl.ds(at + WIDTH, LANES)] = (grad * linear * (1.0 - sig)).astype(BF)
    for j in range(2):
        at = pl.multiple_of((first + j) * LANES, LANES)
        small[0:TAPS, pl.ds(at, LANES)] = jnp.sum(r["tap_sum"][j], axis=1)


def back_convolve(chunk, w_depth, small, r, beside):
    count = HALF // LANES // 2

    def pair(c, carry):
        back_convolve_pair(chunk * count + c, w_depth, small, r)
        beside(c)
        return carry

    lax.fori_loop(0, count, pair, 0)


def weight_term(chunk, part, r):
    def tile(i, carry):
        rows = pl.ds(pl.multiple_of(i * 384, 384), 384)
        for h in range(2):
            cols = pl.ds(pl.multiple_of(h * WIDTH + chunk * HALF, HALF), HALF)
            value = dot(r["normed_t"][rows, :], r["grad_pre"][:, cols]).astype(BF)
            for q in range(4):
                part[i // 2, (i % 2) * 2 + q // 2, q % 2, :, h * HALF : (h + 1) * HALF] = value[q * 96 : (q + 1) * 96]
        return carry

    lax.fori_loop(0, 4, tile, 0)


def back_project(w, r, beside):
    def tile(t, carry):
        cols = pl.ds(pl.multiple_of(t * TILE, TILE), TILE)
        r["linear"][:, cols] = dot_t(r["grad_pre"][...], w[cols, :])
        beside(t)
        return carry

    lax.fori_loop(0, WIDTH // TILE, tile, 0)


def finish_back(gain1, grad_input, small, r):
    r["gain1_sum"][...] = jnp.zeros_like(r["gain1_sum"])

    def row_step(i, carry):
        rows = pl.ds(pl.multiple_of(i * STEP, STEP), STEP)
        inverse = r["inv_in"][rows, :]
        units = [r["unit_in"][rows, lanes(b)] for b in range(BLOCKS)]
        grads = [r["linear"][rows, lanes(b)] for b in range(BLOCKS)]
        for b in range(BLOCKS):
            both = grads[b] * units[b]
            r["gain1_sum"][b] = r["gain1_sum"][b] + fold(both)
        grads = [grads[b] * gain1[lanes(b)].reshape(1, LANES) for b in range(BLOCKS)]
        first = row_mean(grads)
        second = row_mean([q * u for q, u in zip(grads, units)])
        for b in range(BLOCKS):
            grad_input[rows, lanes(b)] = (inverse * (grads[b] - first - units[b] * second)).astype(BF)
        return carry

    lax.fori_loop(0, ROWS // STEP, row_step, 0)
    for b in range(BLOCKS):
        small[TAPS : TAPS + 1, lanes(b)] = jnp.sum(r["gain1_sum"][b], axis=0, keepdims=True)
        small[TAPS + 1 : TAPS + 2, lanes(b)] = jnp.sum(r["gain2_sum"][b], axis=0, keepdims=True)
    small[TAPS + 2 : SMALL_ROWS, :] = jnp.zeros((SMALL_ROWS - TAPS - 2, WIDTH), F32)


WORK = (
    ("behind", (ROWS, LANES), jnp.int32),
    ("ahead", (ROWS, LANES), jnp.int32),
    ("chosen", (ROWS, N_DP * SLOT), BF),
    ("unit_in", (ROWS, WIDTH), F32),
    ("inv_in", (ROWS, LANES), F32),
    ("normed", (ROWS, WIDTH), BF),
    ("normed_t", (WIDTH, ROWS), BF),
    ("linear", (ROWS, WIDTH), F32),
    ("sig", (ROWS, WIDTH), F32),
    ("gated", (BLOCKS, PAD + ROWS + PAD, LANES), F32),
    ("conv", (BLOCKS, PAD + ROWS + PAD, LANES), F32),
    ("gain1_sum", (BLOCKS, 8, LANES), F32),
    ("gain2_sum", (BLOCKS, 8, LANES), F32),
    ("tap_sum", (2, TAPS, 8, LANES), F32),
    ("grad_pre", (ROWS, 2 * WIDTH), BF),
)


def add_blocks(dst, src, count, cols):
    def step(i, carry):
        block, row = i // 2, pl.multiple_of((i % 2) * 48, 48)
        d, s = dst(block), src(block)
        d[pl.ds(row, 48), cols] = d[pl.ds(row, 48), cols] + s[pl.ds(row, 48), :]
        return carry

    lax.fori_loop(0, count * 2, step, 0)


X_FIRST = (False, True, False)


def module_kernel(
    frames_hbm, slot_dest, lengths, offsets, gain1, w_own, w_depth, gain2, cotangent_hbm,
    output_hbm, grad_input_hbm, out, depth_out, gain1_out, gain2_out,
    frames, cotangent, output, grad_input, io_sems, arriving, pool, w, outgoing, own_sem, a2a_send, a2a_recv, w_send, w_recv, small, part, rx0, rx1, rx2, rx3, rx3_all, rx4, red, fin, rxs, rxd, small_fin,
    s0, r0, s1, r1, s2, r2, s3, r3, s4, r4, s5, r5, st1, rt1, st2, rt2, st3, rt3,
    *work
):
    r = {name: ref for (name, _, _), ref in zip(WORK, work)}
    p, g = lax.axis_index("dp"), lax.axis_index("shard")
    x_lo, y, core = g // 8, (g // 2) % 4, g % 2
    mates = (y + 1 - 2 * (y % 2), 3 - y)
    scale = 1.0 / (N_DP * N_SHARD)

    barrier = pltpu.get_barrier_semaphore()

    def greet(i, carry):
        signal(barrier, ((p + i) % N_DP, g))
        signal(barrier, (p, (g + i) % N_SHARD))
        return carry

    lax.fori_loop(1, 16, greet, 0)

    def core_copy(k):
        return remote(
            part.at[k, :, :, 1 - core], rx0.at[k], s0.at[k], r0.at[k], (p, shard_index(x_lo, y, 1 - core))
        )

    def finish_core(k):
        core_copy(k).wait_recv()
        add_blocks(
            lambda i: part.at[k, i // 4, i % 4, core], lambda i: rx0.at[k, i // 4, i % 4], 8, slice(None)
        )

    def cols(h):
        return pl.ds(HALF * h, HALF)

    def wide(k):
        return 1 if X_FIRST[k] else 2

    def first_x(k, i):
        return x_lo if X_FIRST[k] else i

    def y_block(k, block, h):
        if X_FIRST[k]:
            return part.at[k, pl.ds(x_lo, 1), block, core, :, cols(h)]
        return part.at[k, :, block, core, :, cols(h)]

    def y1_copy(k, h, j):
        q = mates[h]
        after = 3 - q if h == 0 else q + 1 - 2 * (q % 2)
        return remote(
            y_block(k, q if j == 0 else after, h), rx1.at[k, h, j, pl.ds(0, wide(k))],
            s1.at[k, h, j], r1.at[k, h, j], (p, shard_index(x_lo, q, core)),
        )

    def start_y1(k):
        for j in (1, 0):
            for h in range(2):
                y1_copy(k, h, j).start()

    def y2_copy(k, h):
        q = mates[1 - h]
        return remote(
            y_block(k, q, h), rx2.at[k, h, pl.ds(0, wide(k))], s2.at[k, h], r2.at[k, h],
            (p, shard_index(x_lo, q, core)),
        )

    def turn_y(k):
        for h in range(2):
            y1_copy(k, h, 1).wait_recv()
            add_blocks(
                lambda i: part.at[k, first_x(k, i), mates[1 - h], core],
                lambda i: rx1.at[k, h, 1, i], wide(k), cols(h),
            )
            y2_copy(k, h).start()
        for h in range(2):
            y1_copy(k, h, 0).wait_recv()
            add_blocks(
                lambda i: part.at[k, first_x(k, i), y, core], lambda i: rx1.at[k, h, 0, i], wide(k), cols(h)
            )

    def finish_y(k):
        for h in range(2):
            y2_copy(k, h).wait_recv()
            add_blocks(
                lambda i: part.at[k, first_x(k, i), y, core], lambda i: rx2.at[k, h, i], wide(k), cols(h)
            )

    def x_copy(k):
        peer = (p, shard_index(1 - x_lo, y, core))
        if X_FIRST[k]:
            return remote(part.at[k, 1 - x_lo, :, core], rx3_all, s3.at[k], r3.at[k], peer)
        return remote(part.at[k, 1 - x_lo, y, core], rx3.at[k], s3.at[k], r3.at[k], peer)

    def finish_x(k):
        x_copy(k).wait_recv()
        if X_FIRST[k]:
            add_blocks(lambda i: part.at[k, x_lo, i, core], lambda i: rx3_all.at[i], 4, slice(None))
        else:
            add_blocks(lambda i: part.at[k, x_lo, y, core], lambda i: rx3.at[k], 1, slice(None))

    def at_piece(ref, d, base):
        return ref.at[
            pl.ds(pl.multiple_of((d % 2) * 48, 48), 48), pl.ds(pl.multiple_of(base + (d // 2) * 128, 128), 128)
        ]

    def piece_copy(k, i):
        d = (p + i) % N_DP
        return remote(
            at_piece(part.at[k, x_lo, y, core], d, 0), rx4.at[k, i - 1], s4.at[k, i - 1], r4.at[k, i - 1], (d, g)
        )

    def sum_copy(k, i, sender):
        d = (p + i) % N_DP
        return remote(red.at[k], at_piece(fin, sender, CHUNK * k), s5.at[k, i - 1], r5.at[k, i - 1], (d, g))

    def each(count, do):
        def step(i, carry):
            do(i)
            return carry

        lax.fori_loop(1, count, step, 0)

    def start_pieces(k):
        each(N_DP, lambda i: piece_copy(k, i).start())

    def turn_pieces(k):
        each(N_DP, lambda i: piece_copy(k, i).wait_recv())
        total = at_piece(part.at[k, x_lo, y, core], p, 0)[...].astype(F32)
        for i in range(N_DP - 1):
            total = total + rx4[k, i].astype(F32)
        total = total.astype(BF)
        red[k] = total
        at_piece(fin, p, CHUNK * k)[...] = total
        each(N_DP, lambda i: sum_copy(k, i, p).start())

    def finish_pieces(k):
        each(N_DP, lambda i: sum_copy(k, i, (p + N_DP - i) % N_DP).wait_recv())

        def widen(i, carry):
            rows = pl.ds(pl.multiple_of(i * 48, 48), 48)
            for h in range(2):
                out[rows, pl.ds(h * WIDTH + HALF * k, HALF)] = (
                    fin[rows, pl.ds(CHUNK * k + HALF * h, HALF)].astype(F32) * scale
                )
            return carry

        lax.fori_loop(0, 2, widen, 0)

    def column(j):
        return pl.ds(pl.multiple_of(j * LANES, LANES), LANES)

    def small_copy(j):
        return remote(small.at[:, column(j)], rxs.at[g], st1.at[j], rt1.at[g], (p, j))

    def each_owner(do):
        def step(j, carry):
            @pl.when(j != g)
            def _():
                do(j)

            return carry

        lax.fori_loop(0, SMALL_OWNERS, step, 0)

    def small_sum_copy(i):
        return remote(rxd.at[p], rxd.at[p], st2.at[i - 1], rt2.at[p], ((p + i) % N_DP, g))

    def small_final_copy(i):
        return remote(
            small_fin.at[:, column(g)], small_fin.at[:, column(g)], st3.at[i - 1], rt3.at[g],
            (p, (g + i) % N_SHARD),
        )

    def add_small_shard():
        @pl.when(g < SMALL_OWNERS)
        def _():
            def take(i):
                s = (g + i) % N_SHARD
                remote(small.at[:, column(0)], rxs.at[s], st1.at[0], rt1.at[s], (p, s)).wait_recv()

            each(N_SHARD, take)
            rxs[g] = small[:, column(g)]
            total = rxs[0]
            for s in range(1, N_SHARD):
                total = total + rxs[s]
            rxd[p] = total
            each(N_DP, lambda i: small_sum_copy(i).start())

    def add_small_dp():
        @pl.when(g < SMALL_OWNERS)
        def _():
            def take(i):
                s = (p + i) % N_DP
                remote(rxd.at[s], rxd.at[s], st2.at[0], rt2.at[s], (s, g)).wait_recv()

            each(N_DP, take)
            total = rxd[0]
            for s in range(1, N_DP):
                total = total + rxd[s]
            small_fin[:, column(g)] = total
            each(N_SHARD, lambda i: small_final_copy(i).start())

    load_frames = pltpu.make_async_copy(frames_hbm, frames, io_sems.at[0])
    load_frames.start()
    load_cotangent = pltpu.make_async_copy(cotangent_hbm, cotangent, io_sems.at[1])
    load_cotangent.start()
    store_output = pltpu.make_async_copy(output, output_hbm, io_sems.at[2])
    store_grad = pltpu.make_async_copy(grad_input, grad_input_hbm, io_sems.at[3])
    load_frames.wait()

    def ready():
        pl.semaphore_wait(barrier, 30)

    def between():
        for name in ("gated", "conv"):
            r[name][:, 0:PAD, :] = jnp.zeros((BLOCKS, PAD, LANES), F32)
            r[name][:, PAD + ROWS :, :] = jnp.zeros((BLOCKS, PAD, LANES), F32)
        find_rows(lengths, offsets, r)

    finish_weight, finish_sends = exchange(
        frames, slot_dest, w_own, arriving, w, outgoing, own_sem, a2a_send, a2a_recv, w_send, w_recv, ready, between
    )
    for s in range(N_DP):
        pool[s * SLOT : (s + 1) * SLOT, :] = arriving[s]
    load_inputs(pool, gain1, r)
    finish_weight()
    project_and_convolve(w, w_depth, r)
    load_cotangent.wait()
    finish_forward(gain2, cotangent, output, r)
    store_output.start()
    transpose_normed(r)
    def beside_first(c):
        pass

    def beside_second(c):
        @pl.when(c == 0)
        def _():
            finish_core(0)
            start_y1(0)

    def beside_third(c):
        @pl.when(c == 0)
        def _():
            finish_core(1)
            x_copy(1).start()
            turn_y(0)

    for k, beside in enumerate((beside_first, beside_second, beside_third)):
        back_convolve(k, w_depth, small, r, beside)
        weight_term(k, part.at[k], r)
        core_copy(k).start()
    finish_y(0)
    x_copy(0).start()

    def beside(t):
        @pl.when(t == 2)
        def _():
            finish_core(2)
            start_y1(2)

        @pl.when(t == 5)
        def _():
            finish_x(0)
            start_pieces(0)

    back_project(w, r, beside)
    finish_back(gain1, grad_input, small, r)
    store_grad.start()
    each_owner(lambda j: small_copy(j).start())
    turn_y(2)
    finish_x(1)
    start_y1(1)
    turn_pieces(0)
    finish_y(2)
    x_copy(2).start()
    add_small_shard()
    turn_y(1)
    finish_x(2)
    start_pieces(2)
    finish_y(1)
    start_pieces(1)
    add_small_dp()
    turn_pieces(2)
    turn_pieces(1)
    finish_pieces(0)

    def take_final(j):
        remote(
            small_fin.at[:, column(j)], small_fin.at[:, column(j)], st3.at[0], rt3.at[j], (p, j)
        ).wait_recv()

    each_owner(take_final)
    depth_out[...] = small_fin[0:TAPS, :] * scale
    for b in range(BLOCKS):
        gain1_out[lanes(b)] = small_fin[TAPS, lanes(b)] * scale
        gain2_out[lanes(b)] = small_fin[TAPS + 1, lanes(b)] * scale
    finish_sends()
    store_output.wait()
    store_grad.wait()
    finish_pieces(2)
    finish_pieces(1)

    for k in range(CHUNKS):
        core_copy(k).wait_send()
        x_copy(k).wait_send()
        for h in range(2):
            y1_copy(k, h, 0).wait_send()
            y1_copy(k, h, 1).wait_send()
            y2_copy(k, h).wait_send()

        def sent(i):
            piece_copy(k, i).wait_send()
            sum_copy(k, i, p).wait_send()

        each(N_DP, sent)
    each_owner(lambda j: small_copy(j).wait_send())

    @pl.when(g < SMALL_OWNERS)
    def _():
        def sent(i):
            small_sum_copy(i).wait_send()
            small_final_copy(i).wait_send()

        each(16, sent)


def module(frames, slot_dest, lengths, offsets, gain1, w_in, w_depth, gain2, cotangent):
    vmem = pl.BlockSpec(memory_space=pltpu.VMEM)
    smem = pl.BlockSpec(memory_space=pltpu.SMEM)
    hbm = pl.BlockSpec(memory_space=pl.ANY)
    block = WIDTH // N_SHARD
    dma = pltpu.SemaphoreType.DMA
    return pl.pallas_call(
        module_kernel,
        out_shape=(
            jax.ShapeDtypeStruct((ROWS, WIDTH), BF),
            jax.ShapeDtypeStruct((ROWS, WIDTH), BF),
            jax.ShapeDtypeStruct((block, 2 * WIDTH), F32),
            jax.ShapeDtypeStruct((TAPS, WIDTH), F32),
            jax.ShapeDtypeStruct((WIDTH,), F32),
            jax.ShapeDtypeStruct((WIDTH,), F32),
        ),
        in_specs=[hbm, smem, smem, smem, vmem, hbm, vmem, vmem, hbm],
        out_specs=(hbm, hbm, vmem, vmem, vmem, vmem),
        scratch_shapes=[
            pltpu.VMEM((N_DP, SLOT, WIDTH), BF),
            pltpu.VMEM((ROWS, WIDTH), BF),
            pltpu.VMEM((ROWS, WIDTH), BF),
            pltpu.VMEM((ROWS, WIDTH), BF),
            dma((4,)),
            pltpu.VMEM((N_DP, SLOT, WIDTH), BF),
            pltpu.VMEM((N_DP * SLOT, WIDTH), BF),
            pltpu.VMEM((WIDTH, 2 * WIDTH), BF),
            pltpu.VMEM((N_DP, SLOT, WIDTH), BF),
            dma,
            dma((N_DP,)), dma((N_DP,)),
            dma((15,)), dma((15,)),
            pltpu.VMEM((SMALL_ROWS, WIDTH), F32),
            pltpu.VMEM((CHUNKS, 2, 4, 2, block, CHUNK), BF),
            pltpu.VMEM((CHUNKS, 2, 4, block, CHUNK), BF),
            pltpu.VMEM((CHUNKS, 2, 2, 2, block, HALF), BF),
            pltpu.VMEM((CHUNKS, 2, 2, block, HALF), BF),
            pltpu.VMEM((CHUNKS, block, CHUNK), BF),
            pltpu.VMEM((4, block, CHUNK), BF),
            pltpu.VMEM((CHUNKS, N_DP - 1, block // 2, 128), BF),
            pltpu.VMEM((CHUNKS, block // 2, 128), BF),
            pltpu.VMEM((block, 2 * WIDTH), BF),
            pltpu.VMEM((N_SHARD, SMALL_ROWS, 128), F32),
            pltpu.VMEM((N_DP, SMALL_ROWS, 128), F32),
            pltpu.VMEM((SMALL_ROWS, WIDTH), F32),
            dma((CHUNKS,)), dma((CHUNKS,)),
            dma((CHUNKS, 2, 2)), dma((CHUNKS, 2, 2)),
            dma((CHUNKS, 2)), dma((CHUNKS, 2)),
            dma((CHUNKS,)), dma((CHUNKS,)),
            dma((CHUNKS, N_DP - 1)), dma((CHUNKS, N_DP - 1)),
            dma((CHUNKS, N_DP - 1)), dma((CHUNKS, N_DP - 1)),
            dma((SMALL_OWNERS,)), dma((N_SHARD,)),
            dma((N_DP - 1,)), dma((N_DP,)),
            dma((N_SHARD - 1,)), dma((SMALL_OWNERS,)),
            *[pltpu.VMEM(shape, dtype) for _, shape, dtype in WORK],
        ],
        compiler_params=pltpu.CompilerParams(
            collective_id=0, has_side_effects=True, vmem_limit_bytes=64 * 1024 * 1024 - 65536
        ),
        name="module",
    )(frames, slot_dest, lengths, offsets, gain1, w_in, w_depth, gain2, cotangent)


def body(frames, slot_dest, recv_length, recv_offset, gain1, w_in, w_depth, gain2, cotangent):
    return module(frames, slot_dest, recv_length, recv_offset, gain1, w_in, w_depth, gain2, cotangent)


def solution(mesh):
    in_specs = (
        P(("dp", "shard"), None, None),
        P(("dp", "shard")),
        P(("dp", "shard")),
        P(("dp", "shard")),
        P(),
        P("shard", None),
        P(),
        P(),
        P(("dp", "shard"), None),
    )
    out_specs = (
        P(("dp", "shard"), None),
        P(("dp", "shard"), None),
        P("shard", None),
        P(),
        P(),
        P(),
    )
    return jax.shard_map(body, mesh=mesh, in_specs=in_specs, out_specs=out_specs, check_vma=False)
```
